32 devices in a mesh: parts: 2 (over y), req: 8 (over z, x), tp: 2 (over core).
Axes of the slice: x: 2, y: 2, z: 4, core: 2. Of those that a mesh axis runs over, the one named last changes fastest.
Arguments:
- counts: int32 [16], P('parts'), parts along dimension 0, may hold values from 1 to 2, as said below
- move_plan: int32 [32], P('parts'), parts along dimension 0, may hold values from 0 to 15, as said below
- ssm_state: float32 [32, 128, 4096], P(('parts', 'req'), 'tp'), parts along dimension 0, may hold values from -6 to 6
- conv_x_state: bfloat16 [32, 3, 8192], P(('parts', 'req'), None, 'tp'), parts along dimension 0, may hold values from -6 to 6
- conv_bc_state: bfloat16 [32, 3, 4, 128], P(('parts', 'req'), None, 'tp'), parts along dimension 0, may hold values from -6 to 6
- x_in: bfloat16 [32, 4, 8192], P(('parts', 'req'), None, 'tp'), parts along dimension 0, may hold values from -6 to 6
- bc_in: bfloat16 [32, 4, 4, 128], P(('parts', 'req'), None, 'tp'), parts along dimension 0, may hold values from -6 to 6
- z_in: bfloat16 [32, 4, 8192], P(('parts', 'req'), None, 'tp'), parts along dimension 0, may hold values from -6 to 6
- dt_in: float32 [32, 4, 128], P(('parts', 'req'), None, 'tp'), parts along dimension 0, may hold values from -1.5 to 1.5
- conv_w_x: float32 [4, 8192], P(None, 'tp'), may hold values from -3 to 3
- conv_b_x: float32 [8192], P('tp'), may hold values from -3 to 3
- conv_w_bc: float32 [4, 4, 128], P(None, 'tp'), may hold values from -3 to 3
- conv_b_bc: float32 [4, 128], P('tp'), may hold values from -3 to 3
- dt_bias: float32 [128], P('tp'), may hold values from -4 to -1
- a_log: float32 [128], P('tp'), may hold values from -2.5 to -0.5
- d_skip: float32 [128], P('tp'), may hold values from 0.3 to 1.5
- norm_w: float32 [8192], P('tp'), may hold values from 0.1 to 1.9
Outputs:
- y_out: bfloat16 [32, 4, 8192], P(('parts', 'req'), None, 'tp'), parts along dimension 0
- new_ssm: float32 [32, 128, 4096], P(('parts', 'req'), 'tp'), parts along dimension 0
- new_conv_x: bfloat16 [32, 3, 8192], P(('parts', 'req'), None, 'tp'), parts along dimension 0
- new_conv_bc: bfloat16 [32, 3, 4, 128], P(('parts', 'req'), None, 'tp'), parts along dimension 0
The draws below stay inside these ranges and needn't reach their ends.
There are 2 independent parts, one for each index of `parts`. The reference program is written for one: setup_inputs(seed, part) draws one part's arguments, and reference() takes and returns one part's arrays. A program takes and returns all parts, laid end to end along the dimension named above; an argument that names none is the same for every part. Nothing has to cross between parts.
Inputs may be any that keep to these rules, and one draw needn't show every extreme that they name: `counts`: at least 1; every draw has owners with 2 live requests. `move_plan`: A destination slot is owner times 2 plus a local slot. Entries of slots that are not live are meaningless. Live requests have distinct destinations. An owner sends at most 1 live requests to other owners and receives at most 1 from other owners, and keeps at most 1 of its own; both bounds are reached in every draw, and some owner has all 2 destination slots taken.
All inputs are finite; a program needn't handle non-finite values.
Results may differ from the reference program's by a relative error of at most 0.001.
Values may be sent and summed in bfloat16 or wider, within the bound.
No kernel may reach another device: no remote copies, remote signals or barrier semaphores. Data moves between devices by JAX's collectives and lax.ppermute only.
A program may use at most 128 MiB of HBM per device.

```python
import jax
import jax.numpy as jnp
from jax import lax

H = 128
P_SIZE = 64
N = 64
G = 4
CAP = 2
STEPS = 4
REQS = 16
CAPS = 16
N_REQ = 8


def plan_draw(key):
    base = jax.random.fold_in(key, 11)
    keys = jax.random.split(base, 6)
    order = jax.random.permutation(keys[0], N_REQ).astype(jnp.int32)
    following = jnp.zeros((N_REQ,), jnp.int32).at[order].set(jnp.roll(order, -1))
    counts = 1 + jax.random.randint(keys[1], (N_REQ,), 0, 2)
    counts = counts.at[order[0]].set(2).at[order[1]].set(2)
    leaves = jnp.where(counts == 2, 1, jax.random.randint(keys[2], (N_REQ,), 0, 2))
    leaving_slot = jnp.where(counts == 2, jax.random.randint(keys[3], (N_REQ,), 0, 2), 0)
    side = jax.random.randint(keys[4], (N_REQ,), 0, 2)
    owners = jnp.arange(N_REQ, dtype=jnp.int32)
    junk = jax.random.randint(keys[5], (N_REQ, 2), 0, N_REQ * CAP)
    moved_dest = following * CAP + jnp.take(side, following)
    stay_dest = owners * CAP + 1 - side
    columns = []
    for slot in range(2):
        live = slot < counts
        moving = live & (leaves == 1) & (leaving_slot == slot)
        columns.append(jnp.where(moving, moved_dest, jnp.where(live, stay_dest, junk[:, slot])))
    plan = jnp.stack(columns, 1).reshape(-1)
    return (counts.astype(jnp.int32), plan.astype(jnp.int32))


def draw_counts(key, part):
    return plan_draw(key)[0]


def draw_move_plan(key, part):
    return plan_draw(key)[1]


def shard_levels(own_key, extent, cuts, least, high):
    factor_of, own = 1.0, jax.random.fold_in(own_key, 6)
    for axis_at, blocks in cuts:
        draws = jnp.exp(jax.random.uniform(jax.random.fold_in(own, axis_at), (blocks,), jnp.float32, least / len(cuts), high / len(cuts)))
        factor_of = factor_of * jnp.repeat(draws, extent[axis_at] // blocks).reshape([-1 if axis == axis_at else 1 for axis in range(len(extent))])
    return factor_of


def normal_values(stream_key, shape, scale, reach, pieces=(), kind=jnp.bfloat16):
    loudness = shard_levels(stream_key, shape, pieces, -0.22, 0.18) if pieces else 1.0
    result = jax.random.normal(stream_key, shape, jnp.float32) * scale * loudness
    return jnp.minimum(jnp.maximum(result, -reach), reach).astype(kind)


def setup_inputs(seed: int = 0, part: int = 0) -> dict:
    arg_keys = jax.random.split(jax.random.key(seed), 18)
    own_keys = jax.random.split(jax.random.fold_in(arg_keys[17], part), 18)
    return {
        "counts": draw_counts(jax.random.fold_in(jax.random.fold_in(arg_keys[17], part), 71), part),
        "move_plan": draw_move_plan(jax.random.fold_in(jax.random.fold_in(arg_keys[17], part), 71), part),
        "ssm_state": normal_values(own_keys[2], (REQS, H, P_SIZE * N), 1.0, 6.0, ((0, 8), (1, 2)), jnp.float32),
        "conv_x_state": normal_values(own_keys[3], (REQS, 3, H * P_SIZE), 1.0, 6.0, ((0, 8), (2, 2))),
        "conv_bc_state": normal_values(own_keys[4], (REQS, 3, G, 2 * N), 1.0, 6.0, ((0, 8), (2, 2))),
        "x_in": normal_values(own_keys[5], (CAPS, STEPS, H * P_SIZE), 1.0, 6.0, ((0, 8), (2, 2))),
        "bc_in": normal_values(own_keys[6], (CAPS, STEPS, G, 2 * N), 1.0, 6.0, ((0, 8), (2, 2))),
        "z_in": normal_values(own_keys[7], (CAPS, STEPS, H * P_SIZE), 1.0, 6.0, ((0, 8), (2, 2))),
        "dt_in": normal_values(own_keys[8], (CAPS, STEPS, H), 0.5, 1.5, ((0, 8), (2, 2)), jnp.float32),
        "conv_w_x": normal_values(arg_keys[9], (4, H * P_SIZE), 4 ** -0.5, 3.0, ((1, 2),), jnp.float32),
        "conv_b_x": normal_values(arg_keys[10], (H * P_SIZE,), 0.5, 3.0, ((0, 2),), jnp.float32),
        "conv_w_bc": normal_values(arg_keys[11], (4, G, 2 * N), 4 ** -0.5, 3.0, ((1, 2),), jnp.float32),
        "conv_b_bc": normal_values(arg_keys[12], (G, 2 * N), 0.5, 3.0, ((0, 2),), jnp.float32),
        "dt_bias": jnp.clip(-4.0 + 3.0 * jax.random.uniform(arg_keys[13], (H,), jnp.float32) ** shard_levels(arg_keys[13], (H,), ((0, 2),), -0.2, 0.2), -4.0, -1.0),
        "a_log": jnp.clip(-2.5 + 2.0 * jax.random.uniform(arg_keys[14], (H,), jnp.float32) ** shard_levels(arg_keys[14], (H,), ((0, 2),), -0.2, 0.2), -2.5, -0.5),
        "d_skip": jnp.clip(0.3 + 1.2 * jax.random.uniform(arg_keys[15], (H,), jnp.float32) ** shard_levels(arg_keys[15], (H,), ((0, 2),), -0.2, 0.2), 0.3, 1.5),
        "norm_w": jnp.clip(1.0 + 0.18 * jax.random.normal(arg_keys[16], (H * P_SIZE,), jnp.float32), 0.1, 1.9),
    }


def plan_slots(counts, move_plan, caps):
    reqs = move_plan.shape[0]
    slots = reqs // counts.shape[0]
    ids = jnp.arange(reqs, dtype=jnp.int32)
    live = ids % slots < jnp.take(counts, ids // slots)
    targets = jnp.arange(caps, dtype=jnp.int32)
    match = live[None, :] & (move_plan[None, :] == targets[:, None])
    source = lax.optimization_barrier(jnp.sum(jnp.where(match, ids[None, :], 0), axis=1)).astype(jnp.int32)
    filled = jnp.any(match, axis=1)
    return (source, filled)

def reference(counts, move_plan, ssm_state, conv_x_state, conv_bc_state, x_in, bc_in, z_in, dt_in, conv_w_x, conv_b_x, conv_w_bc, conv_b_bc, dt_bias, a_log, d_skip, norm_w):
    caps = x_in.shape[0]
    source, filled = plan_slots(counts, move_plan, caps)
    per_group = H // G
    rate = jnp.exp(a_log)

    def one_slot(item):
        src, full, x_seq, bc_seq, z_seq, dt_seq = item
        state = jnp.take(ssm_state, src, axis=0).reshape(H, P_SIZE, N)
        state = jnp.where(full, state, jnp.zeros_like(state))
        conv_x = jnp.take(conv_x_state, src, axis=0)
        conv_x = jnp.where(full, conv_x, jnp.zeros_like(conv_x))
        conv_bc = jnp.take(conv_bc_state, src, axis=0)
        conv_bc = jnp.where(full, conv_bc, jnp.zeros_like(conv_bc))
        outputs = []
        for step in range(STEPS):
            x_new = x_seq[step]
            window = jnp.concatenate([conv_x, x_new[None]], 0).astype(jnp.float32)
            xconv = jax.nn.silu(lax.optimization_barrier(jnp.sum(window * conv_w_x, axis=0)) + conv_b_x)
            conv_x = jnp.concatenate([conv_x[1:], x_new[None]], 0)
            bc_new = bc_seq[step]
            bwindow = jnp.concatenate([conv_bc, bc_new[None]], 0).astype(jnp.float32)
            bconv = jax.nn.silu(lax.optimization_barrier(jnp.sum(bwindow * conv_w_bc, axis=0)) + conv_b_bc)
            conv_bc = jnp.concatenate([conv_bc[1:], bc_new[None]], 0)
            b_head = jnp.repeat(bconv[:, :N], per_group, axis=0)
            c_head = jnp.repeat(bconv[:, N:], per_group, axis=0)
            delta = jax.nn.softplus(dt_seq[step] + dt_bias)
            decay = jnp.exp(-delta * rate)
            heads_x = xconv.reshape(H, P_SIZE)
            state = decay[:, None, None] * state + (delta[:, None] * heads_x)[:, :, None] * b_head[:, None, :]
            mixed = lax.optimization_barrier(jnp.sum(state * c_head[:, None, :], axis=-1)) + d_skip[:, None] * heads_x
            gated = mixed.reshape(H * P_SIZE) * jax.nn.silu(z_seq[step].astype(jnp.float32))
            total = jnp.sum(gated * gated)
            normed = gated * lax.rsqrt(total / (H * P_SIZE) + 1e-05) * norm_w
            outputs.append(jnp.where(full, normed, jnp.zeros_like(normed)).astype(jnp.bfloat16))
        final = jnp.where(full, state.reshape(H, P_SIZE * N), jnp.zeros((H, P_SIZE * N), jnp.float32))
        conv_x = jnp.where(full, conv_x, jnp.zeros_like(conv_x))
        conv_bc = jnp.where(full, conv_bc, jnp.zeros_like(conv_bc))
        return (jnp.stack(outputs, 0), final, conv_x, conv_bc)
    y_out, new_ssm, new_conv_x, new_conv_bc = lax.map(one_slot, (source, filled, x_in, bc_in, z_in, dt_in))
    return (y_out, new_ssm, new_conv_x, new_conv_bc)
```

```python
import jax
import jax.numpy as jnp
from jax import lax
from jax.experimental import pallas as pl
from jax.experimental.pallas import tpu as pltpu
from jax.sharding import PartitionSpec as P

H = 128
P_SIZE = 64
LANES = 128
AUX = 16
REACH = 6.0
LEVELS = 32767.0
VMEM_LIMIT = 48 * 1024 * 1024


def level_code(top):
    code = jnp.floor(-8.0 / jnp.log(2.0) * jnp.log(jnp.maximum(top, 1e-30) / REACH) - 0.01)
    return jnp.clip(code, 0.0, 800.0)


def level_scale(code):
    return REACH * jnp.exp(code * (-0.125 * jnp.log(2.0)))


def moving_slot(counts_ref, plan_ref, me_ref, slots):
    me = me_ref[0]
    slot = jnp.int32(0)
    for local in range(1, slots):
        live = local < counts_ref[me]
        away = plan_ref[me * slots + local] // slots != me
        slot = jnp.where(live & away, local, slot)
    return slot


def pack_kernel(counts_ref, plan_ref, me_ref, state_ref, cx_ref, cb_ref, out_ref, rows_ref):
    heads, columns = state_ref.shape[1:]
    owners, piece, _ = out_ref.shape
    share = piece - AUX
    top = jnp.abs(state_ref[0, :, :LANES])
    for j in range(1, columns // LANES):
        top = jnp.maximum(top, jnp.abs(state_ref[0, :, j * LANES : (j + 1) * LANES]))
    code = level_code(jnp.max(top, axis=1, keepdims=True))
    factor = LEVELS / level_scale(code)
    run = min(share, heads)
    for j in range(columns // LANES):
        tile = state_ref[0, :, j * LANES : (j + 1) * LANES] * factor
        tile = jnp.round(tile).astype(jnp.int32).astype(jnp.int16)
        for at in range(0, heads, run):
            flat = j * heads + at
            out_ref[flat // share, flat % share : flat % share + run, :] = tile[at : at + run]
    taps, channels = cx_ref.shape[1:]
    groups = cb_ref.shape[2]
    blocks = channels // LANES
    cx = cx_ref[0].astype(jnp.float32)
    cb = cb_ref[0].astype(jnp.float32)
    code_x = level_code(jnp.max(jnp.abs(cx)).reshape(1, 1))
    code_b = level_code(jnp.max(jnp.abs(cb)).reshape(1, 1))
    for b in range(blocks):
        rows_ref[pl.ds(b, taps, stride=blocks), :] = cx[:, b * LANES : (b + 1) * LANES]
    last = taps * blocks
    rows_ref[last:, :] = jnp.zeros((rows_ref.shape[0] - last, LANES), jnp.float32)
    for k in range(taps):
        rows_ref[last + k * groups : last + (k + 1) * groups, :] = cb[k]
    row = lax.broadcasted_iota(jnp.int32, (heads, LANES), 0)
    lane = lax.broadcasted_iota(jnp.int32, (heads, LANES), 1)
    codes = jnp.sum(jnp.where(row == lane, code, 0.0), axis=0, keepdims=True)
    codes = jnp.where(lane[:1] == heads, code_x, codes)
    codes = jnp.where(lane[:1] == heads + 1, code_b, codes)
    factor_x = LEVELS / level_scale(code_x)
    factor_b = LEVELS / level_scale(code_b)
    used = rows_ref.shape[0] // AUX
    line = lax.broadcasted_iota(jnp.int32, (AUX, LANES), 0)
    for m in range(owners):
        if m < used:
            values = rows_ref[m * AUX : (m + 1) * AUX, :]
            if m * AUX < last:
                values = values * factor_x
            else:
                values = jnp.where(line == taps * groups, codes, values * factor_b)
        else:
            values = jnp.zeros((AUX, LANES), jnp.float32)
        out_ref[m, share:, :] = jnp.round(values).astype(jnp.int32).astype(jnp.int16)


def silu(v):
    return v / (1.0 + jnp.exp(-v))


def split(v):
    high = v.astype(jnp.bfloat16)
    low = (v - high.astype(jnp.float32)).astype(jnp.bfloat16)
    return high, low


def small_steps(seq_x, seq_b, wx_ref, bx_ref, wb_ref, bb_ref, steps):
    taps = len(seq_x) - steps + 1
    xs, bs, cs = [], [], []
    for t in range(steps):
        total = bx_ref[...]
        pairs = bb_ref[...]
        for k in range(taps):
            total = total + wx_ref[k] * seq_x[t + k]
            pairs = pairs + wb_ref[k] * seq_b[t + k]
        xs.append(silu(total))
        pairs = silu(pairs)
        turned = jnp.concatenate([pairs[:, LANES // 2 :], pairs[:, : LANES // 2]], 1)
        lower = lax.broadcasted_iota(jnp.int32, pairs.shape, 1) < LANES // 2
        bs.append(jnp.where(lower, pairs, turned))
        cs.append(jnp.where(lower, turned, pairs))
    return xs, bs, cs


def by_group(rows, count):
    groups = rows.shape[0]
    run = count // groups
    return jnp.concatenate(
        [jnp.broadcast_to(rows[g : g + 1], (run, rows.shape[1])) for g in range(groups)], 0
    )


def slot_steps(
    tile, column, scale, xs, bs, cs, dec, dts, skip, gate, write, spread_ref, mixed_ref
):
    steps = len(xs)
    heads = column.shape[0]
    blocks = xs[0].shape[0]
    lane = lax.broadcasted_iota(jnp.int32, (blocks, LANES), 1)
    lower = lane < LANES // 2
    later = None
    for t in reversed(range(steps)):
        weighted = xs[t] * dts[t]
        if later is not None:
            weighted = weighted * later
        later = dec[t] if later is None else later * dec[t]
        spread_ref[pl.ds(t * heads, blocks, stride=2), :] = jnp.where(lower, weighted, 0.0)
        spread_ref[pl.ds(t * heads + 1, blocks, stride=2), :] = jnp.where(lower, 0.0, weighted)
    high, low = split(spread_ref[...])
    spread = jnp.concatenate([high, low], 1)
    b_rows = [by_group(b, heads) for b in bs]
    c_rows = [by_group(c, heads) for c in cs]
    at = lax.broadcasted_iota(jnp.int32, (2 * LANES, LANES), 0) // P_SIZE
    to = lax.broadcasted_iota(jnp.int32, (2 * LANES, LANES), 1) % P_SIZE
    place = to - at
    wide = jnp.broadcast_to(column, (heads, LANES))
    mixed = jnp.zeros((steps * heads, LANES), jnp.float32)
    count = P_SIZE * P_SIZE // (2 * LANES)
    for k in range(count):
        chosen = jnp.where(place == k * (2 * LANES // P_SIZE), 1.0, 0.0).astype(jnp.bfloat16)
        states = [tile(2 * k), tile(2 * k + 1)]
        highs, lows = [], []
        for t in range(steps):
            parts = [split(s * c_rows[t]) for s in states]
            highs.append(jnp.concatenate([p[0] for p in parts], 1))
            lows.append(jnp.concatenate([p[1] for p in parts], 1))
        mixed = mixed + jnp.dot(
            jnp.concatenate(highs, 0), chosen, preferred_element_type=jnp.float32
        )
        mixed = mixed + jnp.dot(
            jnp.concatenate(lows, 0), chosen, preferred_element_type=jnp.float32
        )
        both = jnp.concatenate([chosen, chosen], 1)
        grown = lax.dot_general(
            spread, both, (((1,), (1,)), ((), ())), preferred_element_type=jnp.float32
        )
        for half in range(2):
            new = wide * states[half]
            for t in range(steps):
                piece = grown[t * heads : (t + 1) * heads, half * LANES : (half + 1) * LANES]
                new = new + piece * b_rows[t]
            write(2 * k + half, new)
    for t in range(steps):
        part = mixed[t * heads : (t + 1) * heads]
        if scale is not None:
            part = part * scale
        mixed_ref[t * heads : (t + 1) * heads, :] = part
    gated, sums = [], []
    ahead = None
    weights = []
    for t in range(steps):
        weights = [w * dec[t] for w in weights] + [dts[t]]
        ahead = dec[t] if ahead is None else ahead * dec[t]
        even = mixed_ref[pl.ds(t * heads, blocks, stride=2), :]
        odd = mixed_ref[pl.ds(t * heads + 1, blocks, stride=2), :]
        out = ahead * jnp.where(lower, even, odd) + skip * xs[t]
        for s in range(t + 1):
            inner = 0.5 * jnp.sum(bs[s] * cs[t], axis=1, keepdims=True)
            inner = by_group(jnp.broadcast_to(inner, (inner.shape[0], LANES)), blocks)
            out = out + weights[s] * inner * xs[s]
        out = out * gate[t]
        gated.append(out)
        squares = jnp.sum(jnp.sum(out * out, axis=0, keepdims=True), axis=1, keepdims=True)
        sums.append(jnp.broadcast_to(squares, (1, LANES)))
    return gated, sums


def kept_kernel(
    info_ref, state_ref, cx_ref, cb_ref, x_ref, bc_ref, gate_ref, dec_ref, dt_ref, skip_ref,
    column_ref, wx_ref, bx_ref, wb_ref, bb_ref,
    new_ref, gated_ref, sums_ref, spread_ref, mixed_ref,
):
    steps = x_ref.shape[1]
    taps = cx_ref.shape[1]
    seq_x = [cx_ref[0, k] for k in range(taps)] + [x_ref[0, t] for t in range(steps)]
    seq_b = [cb_ref[0, k] for k in range(taps)] + [bc_ref[0, t] for t in range(steps)]
    xs, bs, cs = small_steps(seq_x, seq_b, wx_ref, bx_ref, wb_ref, bb_ref, steps)
    full = info_ref[2] > 0

    def write(j, new):
        new_ref[0, :, j * LANES : (j + 1) * LANES] = jnp.where(full, new, 0.0)

    gated, sums = slot_steps(
        lambda j: state_ref[0, :, j * LANES : (j + 1) * LANES],
        column_ref[0], None, xs, bs, cs,
        [dec_ref[0, t] for t in range(steps)], [dt_ref[0, t] for t in range(steps)],
        skip_ref[...], [gate_ref[0, t] for t in range(steps)], write, spread_ref, mixed_ref,
    )
    for t in range(steps):
        gated_ref[t] = gated[t]
    sums_ref[...] = jnp.concatenate(sums, 0)


def moved_kernel(
    info_ref, got_ref, held_ref, kept_sums_ref, x_ref, bc_ref, gate_ref, dec_ref, dt_ref, skip_ref,
    column_ref, wx_ref, bx_ref, wb_ref, bb_ref,
    new_ref, gated_ref, sums_ref, spread_ref, mixed_ref,
):
    del held_ref
    steps, blocks = x_ref.shape[1:3]
    groups = bc_ref.shape[2]
    taps = wx_ref.shape[0] - 1
    heads = column_ref.shape[1]
    share = got_ref.shape[1] - AUX

    def aux(m):
        return got_ref[m, share:, :].astype(jnp.int32).astype(jnp.float32)

    per = blocks // AUX
    last = aux(taps * per)
    codes = last[taps * groups : taps * groups + 1]
    row = lax.broadcasted_iota(jnp.int32, (heads, LANES), 0)
    lane = lax.broadcasted_iota(jnp.int32, (heads, LANES), 1)
    code = jnp.sum(jnp.where(row == lane, codes, 0.0), axis=1, keepdims=True)
    scale = level_scale(code) * (1.0 / LEVELS)
    scale_x = level_scale(codes[:, heads : heads + 1]) * (1.0 / LEVELS)
    scale_b = level_scale(codes[:, heads + 1 : heads + 2]) * (1.0 / LEVELS)
    seq_x = [
        jnp.concatenate([aux(k * per + m) for m in range(per)], 0) * scale_x for k in range(taps)
    ] + [x_ref[0, t] for t in range(steps)]
    seq_b = [last[k * groups : (k + 1) * groups] * scale_b for k in range(taps)] + [
        bc_ref[0, t] for t in range(steps)
    ]
    xs, bs, cs = small_steps(seq_x, seq_b, wx_ref, bx_ref, wb_ref, bb_ref, steps)
    full = info_ref[4] > 0
    run = min(share, heads)

    def tile(j):
        parts = []
        for at in range(0, heads, run):
            flat = j * heads + at
            part = got_ref[flat // share, flat % share : flat % share + run, :]
            parts.append(part.astype(jnp.int32).astype(jnp.float32))
        return jnp.concatenate(parts, 0)

    def write(j, new):
        new_ref[0, :, j * LANES : (j + 1) * LANES] = jnp.where(full, new, 0.0)

    gated, sums = slot_steps(
        tile, column_ref[0] * scale, scale, xs, bs, cs,
        [dec_ref[0, t] for t in range(steps)], [dt_ref[0, t] for t in range(steps)],
        skip_ref[...], [gate_ref[0, t] for t in range(steps)], write, spread_ref, mixed_ref,
    )
    for t in range(steps):
        gated_ref[t] = gated[t]
    sums_ref[...] = jnp.concatenate([kept_sums_ref[...]] + sums, 0)


def norm_kernel(info_ref, kept_ref, moved_ref, mine_ref, theirs_ref, norm_ref, out_ref, rows_ref):
    steps, blocks = kept_ref.shape[:2]
    factor = lax.rsqrt((mine_ref[...] + theirs_ref[...]) * (1.0 / (H * P_SIZE)) + 1e-05)
    for which, ref in enumerate((kept_ref, moved_ref)):
        slot = info_ref[3 * which]
        full = info_ref[2 + 2 * which] > 0
        for t in range(steps):
            at = which * steps + t
            rows_ref[t * blocks : (t + 1) * blocks, :] = jnp.where(
                full, ref[t] * factor[at : at + 1] * norm_ref[...], 0.0
            )
        for b in range(blocks):
            out_ref[slot, :, b * LANES : (b + 1) * LANES] = rows_ref[
                pl.ds(b, steps, stride=blocks), :
            ].astype(jnp.bfloat16)


def on_device(
    counts,
    move_plan,
    ssm_state,
    conv_x_state,
    conv_bc_state,
    x_in,
    bc_in,
    z_in,
    dt_in,
    conv_w_x,
    conv_b_x,
    conv_w_bc,
    conv_b_bc,
    dt_bias,
    a_log,
    d_skip,
    norm_w,
):
    owners = lax.axis_size("req")
    owner = lax.axis_index("req").astype(jnp.int32)
    slots, heads, columns = ssm_state.shape
    places, steps, channels = x_in.shape
    taps = conv_x_state.shape[1]
    groups, pair = conv_bc_state.shape[2:]
    blocks = channels // LANES
    rows = heads * columns // LANES
    share = rows // owners
    params = pltpu.CompilerParams(vmem_limit_bytes=VMEM_LIMIT)
    f32 = jnp.float32

    def moving(i, counts_ref, plan_ref, me_ref):
        return moving_slot(counts_ref, plan_ref, me_ref, slots)

    payload = pl.pallas_call(
        pack_kernel,
        grid_spec=pltpu.PrefetchScalarGridSpec(
            num_scalar_prefetch=3,
            grid=(1,),
            in_specs=[
                pl.BlockSpec((1, heads, columns), lambda *a: (moving(*a), 0, 0)),
                pl.BlockSpec((1, taps, channels), lambda *a: (moving(*a), 0, 0)),
                pl.BlockSpec((1, taps, groups, pair), lambda *a: (moving(*a), 0, 0, 0)),
            ],
            out_specs=pl.BlockSpec((owners, share + AUX, LANES), lambda *a: (0, 0, 0)),
            scratch_shapes=[pltpu.VMEM((taps * blocks + AUX, LANES), f32)],
        ),
        out_shape=jax.ShapeDtypeStruct((owners, share + AUX, LANES), jnp.int16),
        compiler_params=params,
        name="pack",
    )(counts, move_plan, owner.reshape(1), ssm_state, conv_x_state, conv_bc_state)
    spread = lax.all_to_all(payload, "req", split_axis=0, concat_axis=0, tiled=True)

    ids = jnp.arange(move_plan.shape[0], dtype=jnp.int32)
    home = ids // slots
    live = ids % slots < jnp.repeat(counts, slots)
    target = move_plan // places
    away = live & (target != home)
    own = live & (target == home) & (home == owner)
    every = jnp.arange(owners, dtype=jnp.int32)
    source = jnp.sum(jnp.where(away[None] & (target[None] == every[:, None]), home[None], 0), axis=1)
    into = away & (target == owner)
    has_moved = jnp.any(into).astype(jnp.int32)
    has_kept = jnp.any(own).astype(jnp.int32)
    moved_to = jnp.sum(jnp.where(into, move_plan % places, 0))
    kept_to = jnp.sum(jnp.where(own, move_plan % places, 0))
    kept_from = jnp.sum(jnp.where(own, ids % slots, 0))
    moved_to = jnp.where(has_moved > 0, moved_to, jnp.where(has_kept > 0, 1 - kept_to, 0))
    kept_to = 1 - moved_to
    info = jnp.stack([kept_to, kept_from, has_kept, moved_to, has_moved]).astype(jnp.int32)

    picked = jnp.take(spread, source, axis=0, mode="clip")
    got = lax.all_to_all(picked, "req", split_axis=0, concat_axis=0, tiled=True)

    def dense(v):
        return v.astype(f32).reshape(*v.shape[:-1], blocks, LANES)

    def per_channel(v):
        return dense(jnp.repeat(v, P_SIZE, axis=-1))

    x_dense = dense(x_in)
    gate = jax.nn.silu(dense(z_in))
    delta = jax.nn.softplus(dt_in + dt_bias)
    decay = jnp.exp(-delta * jnp.exp(a_log))
    dt_dense = per_channel(delta)
    dec_dense = per_channel(decay)
    column = jnp.prod(decay, axis=1)[..., None]
    bc = bc_in.astype(f32)
    common = [x_dense, bc, gate, dec_dense, dt_dense, per_channel(d_skip), column]
    common += [dense(conv_w_x), dense(conv_b_x), conv_w_bc, conv_b_bc]

    def common_specs(at):
        def slot(*shape):
            return pl.BlockSpec((1, *shape), lambda i, info: (info[at], *[0] * len(shape)))

        def whole(*shape):
            return pl.BlockSpec(shape, lambda i, info: tuple([0] * len(shape)))

        return [
            slot(steps, blocks, LANES), slot(steps, groups, pair), slot(steps, blocks, LANES),
            slot(steps, blocks, LANES), slot(steps, blocks, LANES), whole(blocks, LANES),
            slot(heads, 1), whole(taps + 1, blocks, LANES), whole(blocks, LANES),
            whole(taps + 1, groups, pair), whole(groups, pair),
        ]

    state_shape = jax.ShapeDtypeStruct((places, heads, columns), f32)
    gated_shape = jax.ShapeDtypeStruct((steps, blocks, LANES), f32)
    scratch = [pltpu.VMEM((steps * heads, LANES), f32)] * 2

    def out_specs(at, count):
        return [
            pl.BlockSpec((1, heads, columns), lambda i, info: (info[at], 0, 0)),
            pl.BlockSpec((steps, blocks, LANES), lambda i, info: (0, 0, 0)),
            pl.BlockSpec((count, LANES), lambda i, info: (0, 0)),
        ]

    held, kept_gated, kept_sums = pl.pallas_call(
        kept_kernel,
        grid_spec=pltpu.PrefetchScalarGridSpec(
            num_scalar_prefetch=1,
            grid=(1,),
            in_specs=[
                pl.BlockSpec((1, heads, columns), lambda i, info: (info[1], 0, 0)),
                pl.BlockSpec((1, taps, blocks, LANES), lambda i, info: (info[1], 0, 0, 0)),
                pl.BlockSpec((1, taps, groups, pair), lambda i, info: (info[1], 0, 0, 0)),
            ]
            + common_specs(0),
            out_specs=out_specs(0, steps),
            scratch_shapes=scratch,
        ),
        out_shape=[state_shape, gated_shape, jax.ShapeDtypeStruct((steps, LANES), f32)],
        compiler_params=params,
        name="kept",
    )(info, ssm_state, dense(conv_x_state), conv_bc_state.astype(f32), *common)

    new_ssm, moved_gated, sums = pl.pallas_call(
        moved_kernel,
        grid_spec=pltpu.PrefetchScalarGridSpec(
            num_scalar_prefetch=1,
            grid=(1,),
            in_specs=[
                pl.BlockSpec((owners, share + AUX, LANES), lambda i, info: (0, 0, 0)),
                pl.BlockSpec(memory_space=pl.ANY),
                pl.BlockSpec((steps, LANES), lambda i, info: (0, 0)),
            ]
            + common_specs(3),
            out_specs=out_specs(3, 2 * steps),
            scratch_shapes=scratch,
        ),
        out_shape=[state_shape, gated_shape, jax.ShapeDtypeStruct((2 * steps, LANES), f32)],
        input_output_aliases={2: 0},
        compiler_params=params,
        name="moved",
    )(info, got, held, kept_sums, *common)

    theirs = lax.ppermute(sums, "tp", [(0, 1), (1, 0)])
    y_out = pl.pallas_call(
        norm_kernel,
        grid_spec=pltpu.PrefetchScalarGridSpec(
            num_scalar_prefetch=1,
            grid=(1,),
            in_specs=[
                pl.BlockSpec((steps, blocks, LANES), lambda i, info: (0, 0, 0)),
                pl.BlockSpec((steps, blocks, LANES), lambda i, info: (0, 0, 0)),
                pl.BlockSpec((2 * steps, LANES), lambda i, info: (0, 0)),
                pl.BlockSpec((2 * steps, LANES), lambda i, info: (0, 0)),
                pl.BlockSpec((blocks, LANES), lambda i, info: (0, 0)),
            ],
            out_specs=pl.BlockSpec((places, steps, channels), lambda i, info: (0, 0, 0)),
            scratch_shapes=[pltpu.VMEM((steps * blocks, LANES), f32)],
        ),
        out_shape=jax.ShapeDtypeStruct((places, steps, channels), jnp.bfloat16),
        compiler_params=params,
        name="norm",
    )(info, kept_gated, moved_gated, sums, theirs, dense(norm_w))

    filled = jnp.where(jnp.arange(places) == kept_to, has_kept, has_moved) > 0
    last_x = x_in[:, steps - taps :]
    last_bc = bc_in[:, steps - taps :]
    new_conv_x = jnp.where(filled[:, None, None], last_x, jnp.zeros_like(last_x))
    new_conv_bc = jnp.where(filled[:, None, None, None], last_bc, jnp.zeros_like(last_bc))
    return (y_out, new_ssm, new_conv_x, new_conv_bc)


def solution(mesh):
    in_specs = (
        P("parts"),
        P("parts"),
        P(("parts", "req"), "tp", None),
        P(("parts", "req"), None, "tp"),
        P(("parts", "req"), None, "tp", None),
        P(("parts", "req"), None, "tp"),
        P(("parts", "req"), None, "tp", None),
        P(("parts", "req"), None, "tp"),
        P(("parts", "req"), None, "tp"),
        P(None, "tp"),
        P("tp"),
        P(None, "tp", None),
        P("tp", None),
        P("tp"),
        P("tp"),
        P("tp"),
        P("tp"),
    )
    out_specs = (
        P(("parts", "req"), None, "tp"),
        P(("parts", "req"), "tp", None),
        P(("parts", "req"), None, "tp"),
        P(("parts", "req"), None, "tp", None),
    )
    return jax.shard_map(
        on_device, mesh=mesh, in_specs=in_specs, out_specs=out_specs, check_vma=False
    )
```

```python
import functools

import jax
import jax.numpy as jnp
from jax import lax
from jax.experimental import pallas as pl
from jax.experimental.pallas import tpu as pltpu
from jax.sharding import PartitionSpec as P

H = 128
P_SIZE = 64
LANES = 128
AUX = 16
BLOCK = 16
INFO = 8
REACH = 6.0
LEVELS = 32767.0
VMEM_LIMIT = 48 * 1024 * 1024


def level_code(top):
    code = jnp.floor(-8.0 / jnp.log(2.0) * jnp.log(jnp.maximum(top, 1e-30) / REACH) - 0.01)
    return jnp.clip(code, 0.0, 800.0)


def level_scale(code):
    return REACH * jnp.exp(code * (-0.125 * jnp.log(2.0)))


def moving_slot(counts_ref, plan_ref, me, slots):
    slot = jnp.int32(0)
    for local in range(1, slots):
        live = local < counts_ref[me]
        away = plan_ref[me * slots + local] // slots != me
        slot = jnp.where(live & away, local, slot)
    return slot


def dense_rows(rows_ref, at, values):
    count, channels = values.shape
    blocks = channels // LANES
    for b in range(blocks):
        part = values[:, b * LANES : (b + 1) * LANES]
        if count == 1:
            rows_ref[at + b : at + b + 1, :] = part
        else:
            rows_ref[pl.ds(at + b, count, stride=blocks), :] = part


def of_slot(values, slot):
    return jnp.where(slot == 0, values[0], values[1])


def pack_kernel(me_ref, counts_hbm, plan_hbm, state_hbm, cx_hbm, cb_hbm, *refs):
    *out_refs, counts_ref, plan_ref, state_ref, cx_ref, cb_ref, rows_ref, sems = refs
    direct = len(out_refs) > 1
    slots, heads, columns = state_ref.shape
    owners = len(out_refs) if direct else out_refs[0].shape[0]
    share = out_refs[0].shape[-2] - AUX
    run = min(share, BLOCK)
    each = share // heads
    me = me_ref[0]
    small = [
        pltpu.make_async_copy(src, dst, sems.at[i])
        for i, (src, dst) in enumerate(
            ((counts_hbm, counts_ref), (plan_hbm, plan_ref), (cx_hbm, cx_ref), (cb_hbm, cb_ref))
        )
    ]
    for copy in small:
        copy.start()
    large = []
    for at in range(0, heads, BLOCK):
        for slot in range(slots):
            part = (slot, pl.ds(at, BLOCK))
            copy = pltpu.make_async_copy(
                state_hbm.at[part], state_ref.at[part], sems.at[len(small) + len(large)]
            )
            copy.start()
            large.append(copy)
    small[0].wait()
    small[1].wait()
    slot = moving_slot(counts_ref, plan_ref, me, slots)
    small[2].wait()
    small[3].wait()
    taps, _, channels = cx_ref.shape
    groups = cb_ref.shape[2]
    blocks = channels // LANES
    cx = cx_ref[...].astype(jnp.float32)
    cx = jnp.where(slot == 0, cx[:, 0], cx[:, 1])
    cb = of_slot(cb_ref[...].astype(jnp.float32), slot)
    code_x = level_code(jnp.max(jnp.abs(cx)).reshape(1, 1))
    code_b = level_code(jnp.max(jnp.abs(cb)).reshape(1, 1))
    dense_rows(rows_ref, 0, cx)
    last = taps * blocks
    rows_ref[last:, :] = jnp.zeros((rows_ref.shape[0] - last, LANES), jnp.float32)
    for k in range(taps):
        rows_ref[last + k * groups : last + (k + 1) * groups, :] = cb[k]
    lane = lax.broadcasted_iota(jnp.int32, (BLOCK, LANES), 1)
    row = lax.broadcasted_iota(jnp.int32, (BLOCK, LANES), 0)
    codes = jnp.where(lane[:1] == heads, code_x, 0.0)
    codes = jnp.where(lane[:1] == heads + 1, code_b, codes)
    for q in range(heads // BLOCK):
        for copy in large[q * slots : (q + 1) * slots]:
            copy.wait()
        at = q * BLOCK
        top = jnp.abs(state_ref[slot, at : at + BLOCK, :LANES])
        for j in range(1, columns // LANES):
            tile = state_ref[slot, at : at + BLOCK, j * LANES : (j + 1) * LANES]
            top = jnp.maximum(top, jnp.abs(tile))
        code = level_code(jnp.max(top, axis=1, keepdims=True))
        codes = codes + jnp.sum(jnp.where(row + at == lane, code, 0.0), axis=0, keepdims=True)
        factor = jnp.broadcast_to(LEVELS / level_scale(code), (BLOCK, LANES))
        for j in range(columns // LANES):
            place = (me ^ (j // each)) * each + j % each if direct else j
            lanes = pl.ds(pl.multiple_of(place * LANES, LANES), LANES)
            tile = state_ref[slot, at : at + BLOCK, lanes] * factor
            tile = jnp.round(tile).astype(jnp.int32).astype(jnp.int16)
            for part in range(0, BLOCK, run):
                flat = j * heads + at + part
                rows = pl.ds(flat % share, run)
                if direct:
                    out_refs[flat // share][rows, :] = tile[part : part + run]
                else:
                    out_refs[0][flat // share, rows, :] = tile[part : part + run]
    factor_x = LEVELS / level_scale(code_x)
    factor_b = LEVELS / level_scale(code_b)
    line = lax.broadcasted_iota(jnp.int32, (AUX, LANES), 0)
    rows_ref[:last, :] = rows_ref[:last, :] * factor_x
    values = rows_ref[last : last + AUX, :] * factor_b
    rows_ref[last : last + AUX, :] = jnp.where(line == taps * groups, codes, values)
    for m in range(owners):
        if direct:
            values = rows_ref[pl.ds(pl.multiple_of((me ^ m) * AUX, AUX), AUX), :]
        elif m * AUX < last + AUX:
            values = rows_ref[m * AUX : (m + 1) * AUX, :]
        else:
            values = jnp.zeros((AUX, LANES), jnp.float32)
        values = jnp.round(values).astype(jnp.int32).astype(jnp.int16)
        if direct:
            out_refs[m][share:, :] = values
        else:
            out_refs[0][m, share:, :] = values


def pick_kernel(info_ref, *refs):
    if len(refs) == 2:
        in_ref, out_ref = refs
        for m in range(out_ref.shape[0]):
            out_ref[m] = in_ref[info_ref[INFO + m]]
        return
    owners = len(refs) // 2
    *in_refs, all_ref = refs[:owners] + refs[-1:]
    out_refs = refs[owners:-1]
    me = info_ref[5]
    for k in range(owners):
        all_ref[k] = in_refs[k][...]
    for k in range(owners):
        out_refs[k][...] = all_ref[info_ref[INFO + (me ^ k)] ^ me]


def silu(v):
    return v / (1.0 + jnp.exp(-v))


def split(v):
    high = v.astype(jnp.bfloat16)
    low = (v - high.astype(jnp.float32)).astype(jnp.bfloat16)
    return high, low


def small_steps(seq_x, seq_b, wx_ref, bx_ref, wb_ref, bb_ref, steps):
    taps = len(seq_x) - steps + 1
    blocks = bx_ref.shape[0]
    xs, bs, cs = [], [], []
    for t in range(steps):
        total = bx_ref[...]
        pairs = bb_ref[...]
        for k in range(taps):
            total = total + wx_ref[k * blocks : (k + 1) * blocks, :] * seq_x[t + k]
            pairs = pairs + wb_ref[k] * seq_b[t + k]
        xs.append(silu(total))
        pairs = silu(pairs)
        turned = jnp.concatenate([pairs[:, LANES // 2 :], pairs[:, : LANES // 2]], 1)
        lower = lax.broadcasted_iota(jnp.int32, pairs.shape, 1) < LANES // 2
        bs.append(jnp.where(lower, pairs, turned))
        cs.append(jnp.where(lower, turned, pairs))
    return xs, bs, cs


def by_group(rows, count):
    groups = rows.shape[0]
    run = count // groups
    return jnp.concatenate(
        [jnp.broadcast_to(rows[g : g + 1], (run, rows.shape[1])) for g in range(groups)], 0
    )


def slot_steps(
    tile, first, wide, scale, xs, bs, cs, dec, dts, skip, gate, write, spread_ref, mixed_ref
):
    steps = len(xs)
    heads = wide.shape[0]
    blocks = xs[0].shape[0]
    lane = lax.broadcasted_iota(jnp.int32, (blocks, LANES), 1)
    lower = lane < LANES // 2
    later = None
    for t in reversed(range(steps)):
        weighted = xs[t] * dts[t]
        if later is not None:
            weighted = weighted * later
        later = dec[t] if later is None else later * dec[t]
        spread_ref[pl.ds(t * heads, blocks, stride=2), :] = jnp.where(lower, weighted, 0.0)
        spread_ref[pl.ds(t * heads + 1, blocks, stride=2), :] = jnp.where(lower, 0.0, weighted)
    high, low = split(spread_ref[...])
    spread = jnp.concatenate([high, low], 1)
    b_rows = [by_group(b, heads) for b in bs]
    c_rows = [by_group(c, heads) for c in cs]
    at = lax.broadcasted_iota(jnp.int32, (2 * LANES, LANES), 0) // P_SIZE
    to = lax.broadcasted_iota(jnp.int32, (2 * LANES, LANES), 1) % P_SIZE
    place = to - at
    mixed = jnp.zeros((steps * heads, LANES), jnp.float32)
    count = P_SIZE * P_SIZE // (2 * LANES)
    for k in range(count):
        chosen = jnp.where(place == first(2 * k) * (LANES // P_SIZE), 1.0, 0.0)
        chosen = chosen.astype(jnp.bfloat16)
        states = [tile(2 * k), tile(2 * k + 1)]
        highs, lows = [], []
        for t in range(steps):
            parts = [split(s * c_rows[t]) for s in states]
            highs.append(jnp.concatenate([p[0] for p in parts], 1))
            lows.append(jnp.concatenate([p[1] for p in parts], 1))
        mixed = mixed + jnp.dot(
            jnp.concatenate(highs, 0), chosen, preferred_element_type=jnp.float32
        )
        mixed = mixed + jnp.dot(
            jnp.concatenate(lows, 0), chosen, preferred_element_type=jnp.float32
        )
        both = jnp.concatenate([chosen, chosen], 1)
        grown = lax.dot_general(
            spread, both, (((1,), (1,)), ((), ())), preferred_element_type=jnp.float32
        )
        for half in range(2):
            new = wide * states[half]
            for t in range(steps):
                piece = grown[t * heads : (t + 1) * heads, half * LANES : (half + 1) * LANES]
                new = new + piece * b_rows[t]
            write(2 * k + half, new)
    for t in range(steps):
        part = mixed[t * heads : (t + 1) * heads]
        if scale is not None:
            part = part * scale
        mixed_ref[t * heads : (t + 1) * heads, :] = part
    gated, sums = [], []
    ahead = None
    weights = []
    for t in range(steps):
        weights = [w * dec[t] for w in weights] + [dts[t]]
        ahead = dec[t] if ahead is None else ahead * dec[t]
        even = mixed_ref[pl.ds(t * heads, blocks, stride=2), :]
        odd = mixed_ref[pl.ds(t * heads + 1, blocks, stride=2), :]
        out = ahead * jnp.where(lower, even, odd) + skip * xs[t]
        for s in range(t + 1):
            inner = 0.5 * jnp.sum(bs[s] * cs[t], axis=1, keepdims=True)
            inner = by_group(jnp.broadcast_to(inner, (inner.shape[0], LANES)), blocks)
            out = out + weights[s] * inner * xs[s]
        out = out * gate[t]
        gated.append(out)
        squares = jnp.sum(jnp.sum(out * out, axis=0, keepdims=True), axis=1, keepdims=True)
        sums.append(jnp.broadcast_to(squares, (1, LANES)))
    return gated, sums


def prep_kernel(
    me_ref, counts_hbm, plan_hbm, x_ref, z_ref, bc_ref, dt_ref, bias_ref, rate_ref, skip_ref,
    wx_ref,
    info_ref, xd_ref, gate_ref, dec_ref, dtd_ref, wide_ref, skipd_ref, wxd_ref, cx_ref, cb_ref,
    counts_ref, plan_ref, sems,
):
    slots, steps, channels = x_ref.shape
    heads = dt_ref.shape[2]
    blocks = channels // LANES
    taps = cx_ref.shape[0]
    me = me_ref[0]
    copies = [
        pltpu.make_async_copy(counts_hbm, counts_ref, sems.at[0]),
        pltpu.make_async_copy(plan_hbm, plan_ref, sems.at[1]),
    ]
    for copy in copies:
        copy.start()
    x = [x_ref[s].astype(jnp.float32) for s in range(slots)]
    for s in range(slots):
        dense_rows(xd_ref.at[s], 0, x[s])
        dense_rows(gate_ref.at[s], 0, z_ref[s].astype(jnp.float32))
    dense_rows(wxd_ref, 0, wx_ref[...])
    gate_ref[...] = silu(gate_ref[...])
    rate = jnp.exp(rate_ref[...])
    raw = [dt_ref[s] + bias_ref[...] for s in range(slots)]
    delta = [jnp.maximum(v, 0.0) + jnp.log1p(jnp.exp(-jnp.abs(v))) for v in raw]
    decay = [jnp.exp(-v * rate) for v in delta]
    at = lax.broadcasted_iota(jnp.int32, (blocks, heads), 0)
    of = lax.broadcasted_iota(jnp.int32, (blocks, heads), 1)
    lines = [v[t : t + 1] for v in delta + decay for t in range(steps)] + [skip_ref[...]]
    spread = jnp.concatenate([jnp.where(of // 2 == at, line, 0.0) for line in lines], 0)
    high = spread.astype(jnp.bfloat16)
    rest = spread - high.astype(jnp.float32)
    middle = rest.astype(jnp.bfloat16)
    low = (rest - middle.astype(jnp.float32)).astype(jnp.bfloat16)
    head = lax.broadcasted_iota(jnp.int32, (heads, LANES), 0)
    lane = lax.broadcasted_iota(jnp.int32, (heads, LANES), 1)
    chosen = jnp.where(head % 2 == lane // (LANES // 2), 1.0, 0.0).astype(jnp.bfloat16)
    out = jnp.dot(high, chosen, preferred_element_type=jnp.float32)
    out = out + jnp.dot(middle, chosen, preferred_element_type=jnp.float32)
    out = out + jnp.dot(low, chosen, preferred_element_type=jnp.float32)
    run = steps * blocks
    for s in range(slots):
        dtd_ref[s] = out[s * run : (s + 1) * run]
        dec_ref[s] = out[(slots + s) * run : (slots + s + 1) * run]
        total = decay[s][:1]
        for t in range(1, steps):
            total = total * decay[s][t : t + 1]
        total = jnp.concatenate([total, total], 1)
        wide = jnp.sum(jnp.where(head == lane, total, 0.0), axis=1, keepdims=True)
        wide_ref[s] = jnp.broadcast_to(wide, (heads, LANES))
    skipd_ref[...] = out[2 * slots * run :]
    for copy in copies:
        copy.wait()
    reqs = plan_ref.shape[0]
    owners = counts_ref.shape[0]
    for d in range(owners):
        info_ref[INFO + d] = 0

    def look(r, carry):
        kept_to, kept_from, has_kept, moved_to, has_moved = carry
        home, local = r // slots, r % slots
        goal = plan_ref[r]
        live = local < counts_ref[home]
        owner, place = goal // slots, goal % slots
        mine = live & (owner == me)
        own = mine & (home == me)
        into = mine & (home != me)

        @pl.when(live & (owner != home))
        def _():
            info_ref[INFO + owner] = home

        return (
            jnp.where(own, place, kept_to), jnp.where(own, local, kept_from),
            jnp.where(own, 1, has_kept), jnp.where(into, place, moved_to),
            jnp.where(into, 1, has_moved),
        )

    carry = (jnp.int32(0),) * 5
    if reqs <= 32:
        for r in range(reqs):
            carry = look(r, carry)
    else:
        carry = lax.fori_loop(0, reqs, look, carry)
    kept_to, kept_from, has_kept, moved_to, has_moved = carry
    moved_to = jnp.where(has_moved > 0, moved_to, jnp.where(has_kept > 0, 1 - kept_to, 0))
    kept_to = 1 - moved_to
    for i, v in enumerate((kept_to, kept_from, has_kept, moved_to, has_moved, me)):
        info_ref[i] = v
    full = [jnp.where(kept_to == s, has_kept, has_moved) > 0 for s in range(slots)]
    for k in range(taps):
        t = steps - taps + k
        rows = [jnp.where(full[s], x[s][t : t + 1], 0.0) for s in range(slots)]
        cx_ref[k] = jnp.concatenate(rows, 0).astype(jnp.bfloat16)
        for s in range(slots):
            pairs = bc_ref[s, t].astype(jnp.float32)
            cb_ref[s, k] = jnp.where(full[s], pairs, 0.0).astype(jnp.bfloat16)


def slot_inputs(slot, steps, x_ref, bc_ref, gate_ref, dec_ref, dt_ref):
    blocks = x_ref.shape[1] // steps
    rows = [pl.ds(t * blocks, blocks) for t in range(steps)]
    return [[ref[slot, r, :] for r in rows] for ref in (x_ref, gate_ref, dec_ref, dt_ref)] + [
        [bc_ref[slot, t].astype(jnp.float32) for t in range(steps)]
    ]


def kept_kernel(
    info_ref, state_ref, cx_ref, cb_ref, x_ref, bc_ref, gate_ref, dec_ref, dt_ref, skip_ref,
    wide_ref, wx_ref, bx_ref, wb_ref, bb_ref,
    out_hbm, gated_ref, sums_ref, spread_ref, mixed_ref, rows_ref, new_ref, sem,
):
    steps = bc_ref.shape[1]
    blocks = bx_ref.shape[0]
    taps = cx_ref.shape[0]
    slot, origin, full = info_ref[0], info_ref[1], info_ref[2] > 0
    cx = cx_ref[...].astype(jnp.float32)
    dense_rows(rows_ref, 0, jnp.where(origin == 0, cx[:, 0], cx[:, 1]))
    cb = of_slot(cb_ref[...].astype(jnp.float32), origin)
    new_x, gate, dec, dts, new_b = slot_inputs(
        slot, steps, x_ref, bc_ref, gate_ref, dec_ref, dt_ref
    )
    seq_x = [rows_ref[k * blocks : (k + 1) * blocks, :] for k in range(taps)] + new_x
    seq_b = [cb[k] for k in range(taps)] + new_b
    xs, bs, cs = small_steps(seq_x, seq_b, wx_ref, bx_ref, wb_ref, bb_ref, steps)

    def write(j, new):
        new_ref[:, j * LANES : (j + 1) * LANES] = jnp.where(full, new, 0.0)

    gated, sums = slot_steps(
        lambda j: state_ref[origin, :, j * LANES : (j + 1) * LANES],
        lambda j: j, wide_ref[slot], None, xs, bs, cs, dec, dts,
        skip_ref[...], gate, write, spread_ref, mixed_ref,
    )
    copy = pltpu.make_async_copy(new_ref, out_hbm.at[slot], sem)
    copy.start()
    for t in range(steps):
        gated_ref[t] = gated[t]
    sums_ref[...] = jnp.concatenate(sums, 0)
    copy.wait()


def moved_kernel(pieces, info_ref, *refs):
    got_refs = refs[:pieces]
    (
        held_hbm, kept_sums_ref, x_ref, bc_ref, gate_ref, dec_ref, dt_ref, skip_ref,
        wide_ref, wx_ref, bx_ref, wb_ref, bb_ref,
        out_hbm, gated_ref, sums_ref, spread_ref, mixed_ref, aux_ref, new_ref, sems,
    ) = refs[pieces:]
    del held_hbm
    direct = pieces > 1
    steps, groups = bc_ref.shape[1:3]
    blocks = bx_ref.shape[0]
    taps = wx_ref.shape[0] // blocks - 1
    heads = wide_ref.shape[1]
    share = got_refs[0].shape[-2] - AUX
    slot, full, me = info_ref[3], info_ref[4] > 0, info_ref[5]
    new_x, gate, dec, dts, new_b = slot_inputs(
        slot, steps, x_ref, bc_ref, gate_ref, dec_ref, dt_ref
    )

    def load(m, rows):
        part = got_refs[m][rows, :] if direct else got_refs[0][m, rows, :]
        return part.astype(jnp.int32).astype(jnp.float32)

    for m in range(pieces if direct else got_refs[0].shape[0]):
        if direct:
            at = pl.ds(pl.multiple_of((me ^ m) * AUX, AUX), AUX)
            aux_ref[at, :] = load(m, pl.ds(share, AUX))
        elif m * AUX < aux_ref.shape[0]:
            aux_ref[m * AUX : (m + 1) * AUX, :] = load(m, pl.ds(share, AUX))

    last = aux_ref[taps * blocks : taps * blocks + AUX, :]
    codes = last[taps * groups : taps * groups + 1]
    row = lax.broadcasted_iota(jnp.int32, (heads, LANES), 0)
    lane = lax.broadcasted_iota(jnp.int32, (heads, LANES), 1)
    code = jnp.sum(jnp.where(row == lane, codes, 0.0), axis=1, keepdims=True)
    scale = level_scale(code) * (1.0 / LEVELS)
    scale_x = level_scale(codes[:, heads : heads + 1]) * (1.0 / LEVELS)
    scale_b = level_scale(codes[:, heads + 1 : heads + 2]) * (1.0 / LEVELS)
    seq_x = [aux_ref[k * blocks : (k + 1) * blocks, :] * scale_x for k in range(taps)] + new_x
    seq_b = [last[k * groups : (k + 1) * groups] * scale_b for k in range(taps)] + new_b
    xs, bs, cs = small_steps(seq_x, seq_b, wx_ref, bx_ref, wb_ref, bb_ref, steps)
    run = min(share, heads)
    each = share // heads
    copies = []

    def tile(j):
        if direct:
            return load(j // each, pl.ds(j % each * heads, heads))
        flats = range(j * heads, (j + 1) * heads, run)
        return jnp.concatenate([load(f // share, pl.ds(f % share, run)) for f in flats], 0)

    def first(j):
        return (me ^ (j // each)) * each + j % each if direct else j

    def write(j, new):
        at = pl.ds(pl.multiple_of(first(j) * LANES, LANES), LANES)
        new_ref[:, at] = jnp.where(full, new, 0.0)
        if direct and j % each == each - 1:
            span = pl.ds(pl.multiple_of(first(j - each + 1) * LANES, LANES), each * LANES)
            copy = pltpu.make_async_copy(
                new_ref.at[:, span], out_hbm.at[slot, :, span], sems.at[j // each]
            )
            copy.start()
            copies.append(copy)

    gated, sums = slot_steps(
        tile, first, wide_ref[slot] * scale, scale, xs, bs, cs, dec, dts,
        skip_ref[...], gate, write, spread_ref, mixed_ref,
    )
    for t in range(steps):
        gated_ref[t] = gated[t]
    sums_ref[...] = jnp.concatenate([kept_sums_ref[...]] + sums, 0)
    if not direct:
        copies.append(pltpu.make_async_copy(new_ref, out_hbm.at[slot], sems.at[0]))
        copies[0].start()
    for copy in copies:
        copy.wait()


def norm_kernel(info_ref, kept_ref, moved_ref, mine_ref, theirs_ref, norm_ref, out_ref, rows_ref):
    steps, blocks = kept_ref.shape[:2]
    factor = lax.rsqrt((mine_ref[...] + theirs_ref[...]) * (1.0 / (H * P_SIZE)) + 1e-05)
    for which, ref in enumerate((kept_ref, moved_ref)):
        slot = info_ref[3 * which]
        full = info_ref[2 + 2 * which] > 0
        for t in range(steps):
            at = which * steps + t
            rows_ref[t * blocks : (t + 1) * blocks, :] = jnp.where(
                full, ref[t] * factor[at : at + 1] * norm_ref[...], 0.0
            )
        for b in range(blocks):
            out_ref[slot, :, b * LANES : (b + 1) * LANES] = rows_ref[
                pl.ds(b, steps, stride=blocks), :
            ].astype(jnp.bfloat16)


def on_device(
    counts,
    move_plan,
    ssm_state,
    conv_x_state,
    conv_bc_state,
    x_in,
    bc_in,
    z_in,
    dt_in,
    conv_w_x,
    conv_b_x,
    conv_w_bc,
    conv_b_bc,
    dt_bias,
    a_log,
    d_skip,
    norm_w,
):
    owners = lax.axis_size("req")
    owner = lax.axis_index("req").astype(jnp.int32)
    slots, heads, columns = ssm_state.shape
    places, steps, channels = x_in.shape
    taps = conv_x_state.shape[1]
    groups, pair = conv_bc_state.shape[2:]
    blocks = channels // LANES
    share = heads * columns // LANES // owners
    aux_rows = taps * blocks + AUX
    f32 = jnp.float32
    direct = owners <= 16 and owners & (owners - 1) == 0 and share % heads == 0
    pieces = owners if direct else 1
    smem = pl.BlockSpec(memory_space=pltpu.SMEM)
    vmem = pl.BlockSpec(memory_space=pltpu.VMEM)
    anywhere = pl.BlockSpec(memory_space=pl.ANY)

    def shaped(*shape, dtype=f32):
        return jax.ShapeDtypeStruct(shape, dtype)

    def call(kernel, name, in_specs, out_specs, out_shape, scratch=(), **more):
        return pl.pallas_call(
            kernel,
            in_specs=in_specs,
            out_specs=out_specs,
            out_shape=out_shape,
            scratch_shapes=scratch,
            compiler_params=pltpu.CompilerParams(vmem_limit_bytes=VMEM_LIMIT),
            name=name,
            **more,
        )

    def in_hbm(*values):
        return [pltpu.with_memory_space_constraint(v, pltpu.MemorySpace.HBM) for v in values]

    me = owner.reshape(1)
    conv_x_taps = jnp.transpose(conv_x_state, (1, 0, 2))
    piece = (share + AUX, LANES) if direct else (owners, share + AUX, LANES)
    sent = [shaped(*piece, dtype=jnp.int16)] * pieces
    payload = call(
        pack_kernel, "pack", [smem] + [anywhere] * 5, [vmem] * pieces, sent,
        [
            pltpu.SMEM(counts.shape, jnp.int32),
            pltpu.SMEM(move_plan.shape, jnp.int32),
            pltpu.VMEM(ssm_state.shape, f32),
            pltpu.VMEM(conv_x_taps.shape, jnp.bfloat16),
            pltpu.VMEM(conv_bc_state.shape, jnp.bfloat16),
            pltpu.VMEM((max(aux_rows, pieces * AUX), LANES), f32),
            pltpu.SemaphoreType.DMA((4 + slots * heads // BLOCK,)),
        ],
    )(me, *in_hbm(counts, move_plan, ssm_state, conv_x_taps, conv_bc_state))

    def exchange(values):
        if not direct:
            return [lax.all_to_all(values[0], "req", split_axis=0, concat_axis=0, tiled=True)]
        out = list(values)
        for k in reversed(range(1, pieces)):
            out[k] = lax.ppermute(values[k], "req", [(i, i ^ k) for i in range(owners)])
        return out

    spread = exchange(payload)

    _, x_late = lax.optimization_barrier((payload[0], x_in))
    rows = (places, steps * blocks, LANES)
    info, x_dense, gate, dec, dt_dense, wide, skip, wx, new_conv_x, new_conv_bc = call(
        prep_kernel, "prep", [smem] + [anywhere] * 2 + [vmem] * 8, [smem] + [vmem] * 9,
        [
            shaped(INFO + owners, dtype=jnp.int32), shaped(*rows), shaped(*rows), shaped(*rows),
            shaped(*rows), shaped(places, heads, LANES), shaped(blocks, LANES),
            shaped((taps + 1) * blocks, LANES),
            shaped(taps, places, channels, dtype=jnp.bfloat16),
            shaped(*conv_bc_state.shape, dtype=jnp.bfloat16),
        ],
        [
            pltpu.SMEM(counts.shape, jnp.int32),
            pltpu.SMEM(move_plan.shape, jnp.int32),
            pltpu.SemaphoreType.DMA((2,)),
        ],
    )(
        me, *in_hbm(counts, move_plan), x_late, z_in, bc_in, dt_in, dt_bias.reshape(1, -1),
        a_log.reshape(1, -1), d_skip.reshape(1, -1), conv_w_x,
    )

    picked = call(
        pick_kernel, "pick", [smem] + [vmem] * pieces, [vmem] * pieces, sent,
        [pltpu.VMEM((owners, *piece), jnp.int16)] if direct else [],
    )(info, *spread)
    got = exchange(picked)

    _, info = lax.optimization_barrier((picked[0], info))
    common = [x_dense, bc_in, gate, dec, dt_dense, skip, wide, wx]
    common += [conv_b_x.reshape(blocks, LANES), conv_w_bc, conv_b_bc]
    scratch = [pltpu.VMEM((steps * heads, LANES), f32)] * 2
    held, kept_gated, kept_sums = call(
        kept_kernel, "kept", [smem] + [vmem] * (3 + len(common)), [anywhere, vmem, vmem],
        [shaped(places, heads, columns), shaped(steps, blocks, LANES), shaped(steps, LANES)],
        scratch
        + [
            pltpu.VMEM((taps * blocks, LANES), f32),
            pltpu.VMEM((heads, columns), f32),
            pltpu.SemaphoreType.DMA,
        ],
    )(info, ssm_state, conv_x_taps, conv_bc_state, *common)
    new_ssm, moved_gated, sums = call(
        functools.partial(moved_kernel, pieces), "moved",
        [smem] + [vmem] * pieces + [anywhere] + [vmem] * (1 + len(common)),
        [anywhere, vmem, vmem],
        [shaped(places, heads, columns), shaped(steps, blocks, LANES), shaped(2 * steps, LANES)],
        scratch
        + [
            pltpu.VMEM((max(aux_rows, pieces * AUX), LANES), f32),
            pltpu.VMEM((heads, columns), f32),
            pltpu.SemaphoreType.DMA((pieces,)),
        ],
        input_output_aliases={1 + pieces: 0},
    )(info, *got, held, kept_sums, *common)

    theirs = lax.ppermute(sums, "tp", [(0, 1), (1, 0)])
    y_out = call(
        norm_kernel, "norm", [smem] + [vmem] * 5, vmem,
        shaped(places, steps, channels, dtype=jnp.bfloat16),
        [pltpu.VMEM((steps * blocks, LANES), f32)],
    )(info, kept_gated, moved_gated, sums, theirs, norm_w.reshape(blocks, LANES))
    return (y_out, new_ssm, jnp.transpose(new_conv_x, (1, 0, 2)), new_conv_bc)


def solution(mesh):
    in_specs = (
        P("parts"),
        P("parts"),
        P(("parts", "req"), "tp", None),
        P(("parts", "req"), None, "tp"),
        P(("parts", "req"), None, "tp", None),
        P(("parts", "req"), None, "tp"),
        P(("parts", "req"), None, "tp", None),
        P(("parts", "req"), None, "tp"),
        P(("parts", "req"), None, "tp"),
        P(None, "tp"),
        P("tp"),
        P(None, "tp", None),
        P("tp", None),
        P("tp"),
        P("tp"),
        P("tp"),
        P("tp"),
    )
    out_specs = (
        P(("parts", "req"), None, "tp"),
        P(("parts", "req"), "tp", None),
        P(("parts", "req"), None, "tp"),
        P(("parts", "req"), None, "tp", None),
    )
    return jax.shard_map(
        on_device, mesh=mesh, in_specs=in_specs, out_specs=out_specs, check_vma=False
    )
```

```python
import functools

import jax
import jax.numpy as jnp
from jax import lax
from jax.experimental import pallas as pl
from jax.experimental.pallas import tpu as pltpu
from jax.sharding import PartitionSpec as P

H = 128
P_SIZE = 64
LANES = 128
AUX = 16
BLOCK = 16
QUAD = 4
INFO = 8
REACH = 6.0
LEVELS = 32767.0
VMEM_LIMIT = 48 * 1024 * 1024


def level_code(top):
    code = jnp.floor(-8.0 / jnp.log(2.0) * jnp.log(jnp.maximum(top, 1e-30) / REACH) - 0.01)
    return jnp.clip(code, 0.0, 800.0)


def level_scale(code):
    return REACH * jnp.exp(code * (-0.125 * jnp.log(2.0)))


def moving_slot(counts_ref, plan_ref, me, slots):
    slot = jnp.int32(0)
    for local in range(1, slots):
        live = local < counts_ref[me]
        away = plan_ref[me * slots + local] // slots != me
        slot = jnp.where(live & away, local, slot)
    return slot


def dense_rows(rows_ref, at, values):
    count, channels = values.shape
    blocks = channels // LANES
    for b in range(blocks):
        part = values[:, b * LANES : (b + 1) * LANES]
        if count == 1:
            rows_ref[at + b : at + b + 1, :] = part
        else:
            rows_ref[pl.ds(at + b, count, stride=blocks), :] = part


def of_slot(values, slot):
    return jnp.where(slot == 0, values[0], values[1])


def pack_kernel(masks, me_ref, counts_hbm, plan_hbm, state_hbm, cx_hbm, cb_hbm, *refs):
    *out_refs, counts_ref, plan_ref, state_ref, cx_ref, cb_ref, rows_ref, sems = refs
    direct = len(out_refs) > 1
    slots, heads, columns = state_ref.shape
    owners = len(out_refs) if direct else out_refs[0].shape[0]
    share = out_refs[0].shape[-2] - AUX
    run = min(share, BLOCK)
    each = share // heads
    me = me_ref[0]
    small = [
        pltpu.make_async_copy(src, dst, sems.at[i])
        for i, (src, dst) in enumerate(
            ((counts_hbm, counts_ref), (plan_hbm, plan_ref), (cx_hbm, cx_ref), (cb_hbm, cb_ref))
        )
    ]
    for copy in small:
        copy.start()
    large = []
    for at in range(0, heads, BLOCK):
        for slot in range(slots):
            part = (slot, pl.ds(at, BLOCK))
            copy = pltpu.make_async_copy(
                state_hbm.at[part], state_ref.at[part], sems.at[len(small) + len(large)]
            )
            copy.start()
            large.append(copy)
    small[0].wait()
    small[1].wait()
    slot = moving_slot(counts_ref, plan_ref, me, slots)
    small[2].wait()
    small[3].wait()
    taps, _, channels = cx_ref.shape
    groups = cb_ref.shape[2]
    blocks = channels // LANES
    cx = cx_ref[...].astype(jnp.float32)
    cx = jnp.where(slot == 0, cx[:, 0], cx[:, 1])
    cb = of_slot(cb_ref[...].astype(jnp.float32), slot)
    code_x = level_code(jnp.max(jnp.abs(cx)).reshape(1, 1))
    code_b = level_code(jnp.max(jnp.abs(cb)).reshape(1, 1))
    dense_rows(rows_ref, 0, cx)
    last = taps * blocks
    rows_ref[last:, :] = jnp.zeros((rows_ref.shape[0] - last, LANES), jnp.float32)
    for k in range(taps):
        rows_ref[last + k * groups : last + (k + 1) * groups, :] = cb[k]
    lane = lax.broadcasted_iota(jnp.int32, (BLOCK, LANES), 1)
    row = lax.broadcasted_iota(jnp.int32, (BLOCK, LANES), 0)
    codes = jnp.where(lane[:1] == heads, code_x, 0.0)
    codes = jnp.where(lane[:1] == heads + 1, code_b, codes)
    for q in range(heads // BLOCK):
        for copy in large[q * slots : (q + 1) * slots]:
            copy.wait()
        at = q * BLOCK
        top = jnp.abs(state_ref[slot, at : at + BLOCK, :LANES])
        for j in range(1, columns // LANES):
            tile = state_ref[slot, at : at + BLOCK, j * LANES : (j + 1) * LANES]
            top = jnp.maximum(top, jnp.abs(tile))
        code = level_code(jnp.max(top, axis=1, keepdims=True))
        codes = codes + jnp.sum(jnp.where(row + at == lane, code, 0.0), axis=0, keepdims=True)
        factor = jnp.broadcast_to(LEVELS / level_scale(code), (BLOCK, LANES))
        for j in range(columns // LANES):
            place = (me ^ masks[j // each]) * each + j % each if direct else j
            lanes = pl.ds(pl.multiple_of(place * LANES, LANES), LANES)
            tile = state_ref[slot, at : at + BLOCK, lanes] * factor
            tile = jnp.round(tile).astype(jnp.int32).astype(jnp.int16)
            for part in range(0, BLOCK, run):
                flat = j * heads + at + part
                rows = pl.ds(flat % share, run)
                if direct:
                    out_refs[flat // share][rows, :] = tile[part : part + run]
                else:
                    out_refs[0][flat // share, rows, :] = tile[part : part + run]
    factor_x = LEVELS / level_scale(code_x)
    factor_b = LEVELS / level_scale(code_b)
    line = lax.broadcasted_iota(jnp.int32, (AUX, LANES), 0)
    rows_ref[:last, :] = rows_ref[:last, :] * factor_x
    values = rows_ref[last : last + AUX, :] * factor_b
    rows_ref[last : last + AUX, :] = jnp.where(line == taps * groups, codes, values)
    for m in range(owners):
        if direct:
            values = rows_ref[pl.ds(pl.multiple_of((me ^ masks[m]) * AUX, AUX), AUX), :]
        elif m * AUX < last + AUX:
            values = rows_ref[m * AUX : (m + 1) * AUX, :]
        else:
            values = jnp.zeros((AUX, LANES), jnp.float32)
        values = jnp.round(values).astype(jnp.int32).astype(jnp.int16)
        if direct:
            out_refs[m][share:, :] = values
        else:
            out_refs[0][m, share:, :] = values


def pick_kernel(masks, info_ref, *refs):
    if len(refs) == 2:
        in_ref, out_ref = refs
        for m in range(out_ref.shape[0]):
            out_ref[m] = in_ref[info_ref[INFO + m]]
        return
    owners = len(refs) // 2
    *in_refs, all_ref = refs[:owners] + refs[-1:]
    out_refs = refs[owners:-1]
    me = info_ref[5]
    for i, k in enumerate(masks):
        all_ref[k] = in_refs[i][...]
    for i, k in enumerate(masks):
        out_refs[i][...] = all_ref[info_ref[INFO + (me ^ k)] ^ me]


def silu(v):
    return v / (1.0 + jnp.exp(-v))


def split(v):
    high = v.astype(jnp.bfloat16)
    low = (v - high.astype(jnp.float32)).astype(jnp.bfloat16)
    return high, low


def small_steps(seq_x, seq_b, wx_ref, bx_ref, wb_ref, bb_ref, steps):
    taps = len(seq_x) - steps + 1
    blocks = bx_ref.shape[0]
    xs, bs, cs = [], [], []
    for t in range(steps):
        total = bx_ref[...]
        pairs = bb_ref[...]
        for k in range(taps):
            total = total + wx_ref[k * blocks : (k + 1) * blocks, :] * seq_x[t + k]
            pairs = pairs + wb_ref[k] * seq_b[t + k]
        xs.append(silu(total))
        pairs = silu(pairs)
        turned = jnp.concatenate([pairs[:, LANES // 2 :], pairs[:, : LANES // 2]], 1)
        lower = lax.broadcasted_iota(jnp.int32, pairs.shape, 1) < LANES // 2
        bs.append(jnp.where(lower, pairs, turned))
        cs.append(jnp.where(lower, turned, pairs))
    return xs, bs, cs


def by_group(rows, count):
    groups = rows.shape[0]
    run = count // groups
    return jnp.concatenate(
        [jnp.broadcast_to(rows[g : g + 1], (run, rows.shape[1])) for g in range(groups)], 0
    )


def spread_x(xs, dec, dts, spread_ref):
    blocks = xs[0].shape[0]
    heads = 2 * blocks
    lower = lax.broadcasted_iota(jnp.int32, (blocks, LANES), 1) < LANES // 2
    later = None
    for t in reversed(range(len(xs))):
        weighted = xs[t] * dts[t]
        if later is not None:
            weighted = weighted * later
        later = dec[t] if later is None else later * dec[t]
        spread_ref[pl.ds(t * heads, blocks, stride=2), :] = jnp.where(lower, weighted, 0.0)
        spread_ref[pl.ds(t * heads + 1, blocks, stride=2), :] = jnp.where(lower, 0.0, weighted)
    return jnp.concatenate(split(spread_ref[...]), 1)


def new_state(tile, first, wide, spread, bs, write):
    steps = len(bs)
    heads = wide.shape[0]
    b_rows = [by_group(b, heads) for b in bs]
    at = lax.broadcasted_iota(jnp.int32, (2 * LANES, LANES), 0) // P_SIZE
    to = lax.broadcasted_iota(jnp.int32, (2 * LANES, LANES), 1) % P_SIZE
    place = to - at
    for k in range(P_SIZE * P_SIZE // (2 * LANES)):
        chosen = jnp.where(place == first(2 * k) * (LANES // P_SIZE), 1.0, 0.0)
        chosen = chosen.astype(jnp.bfloat16)
        both = jnp.concatenate([chosen, chosen], 1)
        grown = lax.dot_general(
            spread, both, (((1,), (1,)), ((), ())), preferred_element_type=jnp.float32
        )
        for half in range(2):
            new = wide * tile(2 * k + half)
            for t in range(steps):
                piece = grown[t * heads : (t + 1) * heads, half * LANES : (half + 1) * LANES]
                new = new + piece * b_rows[t]
            write(2 * k + half, new)


def against_c(tile, first, cs, perm_ref, rows_ref):
    steps = len(cs)
    groups = cs[0].shape[0]
    lower = lax.broadcasted_iota(jnp.int32, (steps, LANES), 1) < LANES // 2
    lefts = []
    for g in range(groups):
        rows = jnp.concatenate([c[g : g + 1] for c in cs], 0)
        rows = jnp.concatenate([jnp.where(lower, rows, 0.0), jnp.where(lower, 0.0, rows)], 0)
        lefts.append(jnp.concatenate([jnp.concatenate([v, v], 1) for v in split(rows)], 0))
    count = P_SIZE * P_SIZE // LANES
    line = 2 * steps
    run = LANES // QUAD
    for u in range(0, count, 2 * QUAD):
        parts = [jnp.concatenate(split(tile(j)), 1) for j in range(u, u + 2 * QUAD)]
        for g in range(groups):
            right = jnp.concatenate([p[g * run : (g + 1) * run] for p in parts], 0)
            out = lax.dot_general(
                lefts[g], right, (((1,), (1,)), ((), ())), preferred_element_type=jnp.float32
            )
            out = out[:line] + out[line:]
            for w in range(2):
                quad = first(u + w * QUAD) // QUAD
                at = pl.ds(pl.multiple_of(g * (count // QUAD) * line + quad * line, 8), line)
                rows_ref[at, :] = out[:, w * LANES : (w + 1) * LANES]
    turned = jnp.transpose(rows_ref[...])
    lower = lax.broadcasted_iota(jnp.int32, (run, LANES), 1) < LANES // 2
    straight = [turned[i * run : (i + 1) * run] for i in range(QUAD)]
    rolled = [
        jnp.concatenate([v[:, LANES // 2 :], v[:, : LANES // 2]], 1) for v in straight
    ]
    low_group = [jnp.where(lower, straight[i], rolled[i + 1]) for i in range(0, QUAD, 2)]
    high_group = [jnp.where(lower, rolled[i], straight[i + 1]) for i in range(0, QUAD, 2)]
    values = jnp.concatenate(
        [jnp.concatenate(low_group, 1), jnp.concatenate(high_group, 1)], 0
    )
    high = values.astype(jnp.bfloat16)
    rest = values - high.astype(jnp.float32)
    middle = rest.astype(jnp.bfloat16)
    low = (rest - middle.astype(jnp.float32)).astype(jnp.bfloat16)
    heads = values.shape[0]
    out = jnp.dot(
        jnp.concatenate([high, middle, low], 0), perm_ref[...], preferred_element_type=jnp.float32
    )
    return out[:heads] + out[heads : 2 * heads] + out[2 * heads :]


def gated_steps(mixed, scale, xs, bs, cs, dec, dts, skip, gate, mixed_ref):
    steps = len(xs)
    heads = mixed.shape[0]
    blocks = heads // 2
    lower = lax.broadcasted_iota(jnp.int32, (blocks, LANES), 1) < LANES // 2
    for t in range(steps):
        part = mixed[:, t * LANES : (t + 1) * LANES]
        mixed_ref[t * heads : (t + 1) * heads, :] = part if scale is None else part * scale
    gated, sums = [], []
    ahead = None
    weights = []
    for t in range(steps):
        weights = [w * dec[t] for w in weights] + [dts[t]]
        ahead = dec[t] if ahead is None else ahead * dec[t]
        even = mixed_ref[pl.ds(t * heads, blocks, stride=2), :]
        odd = mixed_ref[pl.ds(t * heads + 1, blocks, stride=2), :]
        out = ahead * jnp.where(lower, even, odd) + skip * xs[t]
        for s in range(t + 1):
            inner = 0.5 * jnp.sum(bs[s] * cs[t], axis=1, keepdims=True)
            inner = by_group(jnp.broadcast_to(inner, (inner.shape[0], LANES)), blocks)
            out = out + weights[s] * inner * xs[s]
        out = out * gate[t]
        gated.append(out)
        squares = jnp.sum(jnp.sum(out * out, axis=0, keepdims=True), axis=1, keepdims=True)
        sums.append(jnp.broadcast_to(squares, (1, LANES)))
    return gated, sums


def prep_kernel(
    me_ref, counts_hbm, plan_hbm, x_ref, z_ref, bc_ref, dt_ref, bias_ref, rate_ref, skip_ref,
    wx_ref,
    info_ref, xd_ref, gate_ref, dec_ref, dtd_ref, wide_ref, skipd_ref, wxd_ref, perm_ref, cx_ref,
    cb_ref,
    counts_ref, plan_ref, sems,
):
    slots, steps, channels = x_ref.shape
    heads = dt_ref.shape[2]
    blocks = channels // LANES
    taps = cx_ref.shape[0]
    me = me_ref[0]
    copies = [
        pltpu.make_async_copy(counts_hbm, counts_ref, sems.at[0]),
        pltpu.make_async_copy(plan_hbm, plan_ref, sems.at[1]),
    ]
    for copy in copies:
        copy.start()
    x = [x_ref[s].astype(jnp.float32) for s in range(slots)]
    for s in range(slots):
        dense_rows(xd_ref.at[s], 0, x[s])
        dense_rows(gate_ref.at[s], 0, z_ref[s].astype(jnp.float32))
    dense_rows(wxd_ref, 0, wx_ref[...])
    gate_ref[...] = silu(gate_ref[...])
    rate = jnp.exp(rate_ref[...])
    raw = [dt_ref[s] + bias_ref[...] for s in range(slots)]
    delta = [jnp.maximum(v, 0.0) + jnp.log1p(jnp.exp(-jnp.abs(v))) for v in raw]
    decay = [jnp.exp(-v * rate) for v in delta]
    at = lax.broadcasted_iota(jnp.int32, (blocks, heads), 0)
    of = lax.broadcasted_iota(jnp.int32, (blocks, heads), 1)
    lines = [v[t : t + 1] for v in delta + decay for t in range(steps)] + [skip_ref[...]]
    spread = jnp.concatenate([jnp.where(of // 2 == at, line, 0.0) for line in lines], 0)
    high = spread.astype(jnp.bfloat16)
    rest = spread - high.astype(jnp.float32)
    middle = rest.astype(jnp.bfloat16)
    low = (rest - middle.astype(jnp.float32)).astype(jnp.bfloat16)
    head = lax.broadcasted_iota(jnp.int32, (heads, LANES), 0)
    lane = lax.broadcasted_iota(jnp.int32, (heads, LANES), 1)
    chosen = jnp.where(head % 2 == lane // (LANES // 2), 1.0, 0.0).astype(jnp.bfloat16)
    out = jnp.dot(high, chosen, preferred_element_type=jnp.float32)
    out = out + jnp.dot(middle, chosen, preferred_element_type=jnp.float32)
    out = out + jnp.dot(low, chosen, preferred_element_type=jnp.float32)
    run = steps * blocks
    for s in range(slots):
        dtd_ref[s] = out[s * run : (s + 1) * run]
        dec_ref[s] = out[(slots + s) * run : (slots + s + 1) * run]
        total = decay[s][:1]
        for t in range(1, steps):
            total = total * decay[s][t : t + 1]
        total = jnp.concatenate([total, total], 1)
        wide = jnp.sum(jnp.where(head == lane, total, 0.0), axis=1, keepdims=True)
        wide_ref[s] = jnp.broadcast_to(wide, (heads, LANES))
    skipd_ref[...] = out[2 * slots * run :]
    shape = perm_ref.shape
    line = lax.broadcasted_iota(jnp.int32, shape, 0)
    lane = lax.broadcasted_iota(jnp.int32, shape, 1)
    span = shape[0] // QUAD
    p = (line % span // (2 * steps) * QUAD + line // span) * 2 + line % (2 * steps) // steps
    hit = (lane // LANES == line % steps) & (lane % P_SIZE == p)
    perm_ref[...] = jnp.where(hit, 1.0, 0.0).astype(jnp.bfloat16)
    for copy in copies:
        copy.wait()
    reqs = plan_ref.shape[0]
    owners = counts_ref.shape[0]
    for d in range(owners):
        info_ref[INFO + d] = 0

    def look(r, carry):
        kept_to, kept_from, has_kept, moved_to, has_moved = carry
        home, local = r // slots, r % slots
        goal = plan_ref[r]
        live = local < counts_ref[home]
        owner, place = goal // slots, goal % slots
        mine = live & (owner == me)
        own = mine & (home == me)
        into = mine & (home != me)

        @pl.when(live & (owner != home))
        def _():
            info_ref[INFO + owner] = home

        return (
            jnp.where(own, place, kept_to), jnp.where(own, local, kept_from),
            jnp.where(own, 1, has_kept), jnp.where(into, place, moved_to),
            jnp.where(into, 1, has_moved),
        )

    carry = (jnp.int32(0),) * 5
    if reqs <= 32:
        for r in range(reqs):
            carry = look(r, carry)
    else:
        carry = lax.fori_loop(0, reqs, look, carry)
    kept_to, kept_from, has_kept, moved_to, has_moved = carry
    moved_to = jnp.where(has_moved > 0, moved_to, jnp.where(has_kept > 0, 1 - kept_to, 0))
    kept_to = 1 - moved_to
    for i, v in enumerate((kept_to, kept_from, has_kept, moved_to, has_moved, me)):
        info_ref[i] = v
    full = [jnp.where(kept_to == s, has_kept, has_moved) > 0 for s in range(slots)]
    for k in range(taps):
        t = steps - taps + k
        rows = [jnp.where(full[s], x[s][t : t + 1], 0.0) for s in range(slots)]
        cx_ref[k] = jnp.concatenate(rows, 0).astype(jnp.bfloat16)
        for s in range(slots):
            pairs = bc_ref[s, t].astype(jnp.float32)
            cb_ref[s, k] = jnp.where(full[s], pairs, 0.0).astype(jnp.bfloat16)


def slot_inputs(slot, steps, x_ref, bc_ref, gate_ref, dec_ref, dt_ref):
    blocks = x_ref.shape[1] // steps
    rows = [pl.ds(t * blocks, blocks) for t in range(steps)]
    return [[ref[slot, r, :] for r in rows] for ref in (x_ref, gate_ref, dec_ref, dt_ref)] + [
        [bc_ref[slot, t].astype(jnp.float32) for t in range(steps)]
    ]


def kept_kernel(
    info_ref, state_ref, cx_ref, cb_ref, x_ref, bc_ref, gate_ref, dec_ref, dt_ref, skip_ref,
    wx_ref, bx_ref, wb_ref, bb_ref, perm_ref, wide_ref,
    out_hbm, gated_ref, sums_ref, spread_ref, mixed_ref, turn_ref, rows_ref, new_ref, sem,
):
    steps = bc_ref.shape[1]
    blocks = bx_ref.shape[0]
    taps = cx_ref.shape[0]
    slot, origin, full = info_ref[0], info_ref[1], info_ref[2] > 0
    cx = cx_ref[...].astype(jnp.float32)
    dense_rows(rows_ref, 0, jnp.where(origin == 0, cx[:, 0], cx[:, 1]))
    cb = of_slot(cb_ref[...].astype(jnp.float32), origin)
    new_x, gate, dec, dts, new_b = slot_inputs(
        slot, steps, x_ref, bc_ref, gate_ref, dec_ref, dt_ref
    )
    seq_x = [rows_ref[k * blocks : (k + 1) * blocks, :] for k in range(taps)] + new_x
    seq_b = [cb[k] for k in range(taps)] + new_b
    xs, bs, cs = small_steps(seq_x, seq_b, wx_ref, bx_ref, wb_ref, bb_ref, steps)

    def write(j, new):
        new_ref[:, j * LANES : (j + 1) * LANES] = jnp.where(full, new, 0.0)

    def tile(j):
        return state_ref[origin, :, j * LANES : (j + 1) * LANES]

    mixed = against_c(tile, lambda j: j, cs, perm_ref, turn_ref)
    gated, sums = gated_steps(
        mixed, None, xs, bs, cs, dec, dts, skip_ref[...], gate, mixed_ref
    )
    spread = spread_x(xs, dec, dts, spread_ref)
    new_state(tile, lambda j: j, wide_ref[slot], spread, bs, write)
    copy = pltpu.make_async_copy(new_ref, out_hbm.at[slot], sem)
    copy.start()
    for t in range(steps):
        gated_ref[t] = gated[t]
    sums_ref[...] = jnp.concatenate(sums, 0)
    copy.wait()


def piece_tiles(masks, me, got_refs, heads):
    direct = len(masks) > 1
    share = got_refs[0].shape[-2] - AUX
    run = min(share, heads)
    each = share // heads

    def load(m, rows):
        part = got_refs[m][rows, :] if direct else got_refs[0][m, rows, :]
        return part.astype(jnp.int32).astype(jnp.float32)

    def tile(j):
        if direct:
            return load(j // each, pl.ds(j % each * heads, heads))
        flats = range(j * heads, (j + 1) * heads, run)
        return jnp.concatenate([load(f // share, pl.ds(f % share, run)) for f in flats], 0)

    def first(j):
        return (me ^ masks[j // each]) * each + j % each if direct else j

    return load, tile, first


def moved_kernel(masks, info_ref, *refs):
    pieces = len(masks)
    got_refs = refs[:pieces]
    (
        kept_sums_ref, x_ref, bc_ref, gate_ref, dec_ref, dt_ref, skip_ref,
        wx_ref, bx_ref, wb_ref, bb_ref, perm_ref, wide_ref,
        gated_ref, sums_ref, spread_ref, b_ref, wide_out_ref, rows_ref, mixed_ref, turn_ref, aux_ref,
    ) = refs[pieces:]
    direct = pieces > 1
    steps, groups = bc_ref.shape[1:3]
    blocks = bx_ref.shape[0]
    taps = wx_ref.shape[0] // blocks - 1
    heads = wide_ref.shape[1]
    share = got_refs[0].shape[-2] - AUX
    slot, me = info_ref[3], info_ref[5]
    new_x, gate, dec, dts, new_b = slot_inputs(
        slot, steps, x_ref, bc_ref, gate_ref, dec_ref, dt_ref
    )
    load, tile, first = piece_tiles(masks, me, got_refs, heads)
    for m in range(pieces if direct else got_refs[0].shape[0]):
        if direct:
            at = pl.ds(pl.multiple_of((me ^ masks[m]) * AUX, AUX), AUX)
            aux_ref[at, :] = load(m, pl.ds(share, AUX))
        elif m * AUX < aux_ref.shape[0]:
            aux_ref[m * AUX : (m + 1) * AUX, :] = load(m, pl.ds(share, AUX))

    last = aux_ref[taps * blocks : taps * blocks + AUX, :]
    codes = last[taps * groups : taps * groups + 1]
    row = lax.broadcasted_iota(jnp.int32, (heads, LANES), 0)
    lane = lax.broadcasted_iota(jnp.int32, (heads, LANES), 1)
    code = jnp.sum(jnp.where(row == lane, codes, 0.0), axis=1, keepdims=True)
    scale = level_scale(code) * (1.0 / LEVELS)
    scale_x = level_scale(codes[:, heads : heads + 1]) * (1.0 / LEVELS)
    scale_b = level_scale(codes[:, heads + 1 : heads + 2]) * (1.0 / LEVELS)
    seq_x = [aux_ref[k * blocks : (k + 1) * blocks, :] * scale_x for k in range(taps)] + new_x
    seq_b = [last[k * groups : (k + 1) * groups] * scale_b for k in range(taps)] + new_b
    xs, bs, cs = small_steps(seq_x, seq_b, wx_ref, bx_ref, wb_ref, bb_ref, steps)
    mixed = against_c(tile, first, cs, perm_ref, turn_ref)
    gated, sums = gated_steps(
        mixed, scale, xs, bs, cs, dec, dts, skip_ref[...], gate, mixed_ref
    )
    for t in range(steps):
        gated_ref[t] = gated[t]
        b_ref[t] = bs[t]
    sums_ref[...] = jnp.concatenate([kept_sums_ref[...]] + sums, 0)
    spread_ref[...] = spread_x(xs, dec, dts, rows_ref)
    wide_out_ref[...] = wide_ref[slot] * scale


def state_kernel(masks, info_ref, *refs):
    pieces = len(masks)
    got_refs = refs[:pieces]
    (
        held_hbm, kept_ref, moved_ref, norm_ref, spread_ref, b_ref, wide_ref,
        out_hbm, ready_ref, rows_ref, new_ref, sems,
    ) = refs[pieces:]
    del held_hbm
    direct = pieces > 1
    steps, blocks = kept_ref.shape[:2]
    heads = wide_ref.shape[0]
    each = (got_refs[0].shape[-2] - AUX) // heads
    slot, full, me = info_ref[3], info_ref[4] > 0, info_ref[5]
    _, tile, first = piece_tiles(masks, me, got_refs, heads)
    copies = []

    def write(j, new):
        at = pl.ds(pl.multiple_of(first(j) * LANES, LANES), LANES)
        new_ref[:, at] = jnp.where(full, new, 0.0)
        if direct and j % each == each - 1:
            span = pl.ds(pl.multiple_of(first(j - each + 1) * LANES, LANES), each * LANES)
            copy = pltpu.make_async_copy(
                new_ref.at[:, span], out_hbm.at[slot, :, span], sems.at[j // each]
            )
            copy.start()
            copies.append(copy)

    bs = [b_ref[t] for t in range(steps)]
    new_state(tile, first, wide_ref[...], spread_ref[...], bs, write)
    if not direct:
        copies.append(pltpu.make_async_copy(new_ref, out_hbm.at[slot], sems.at[0]))
        copies[0].start()
    for which, ref in enumerate((kept_ref, moved_ref)):
        for t in range(steps):
            rows_ref[t * blocks : (t + 1) * blocks, :] = ref[t] * norm_ref[...]
        for b in range(blocks):
            ready_ref[which, :, b * LANES : (b + 1) * LANES] = rows_ref[
                pl.ds(b, steps, stride=blocks), :
            ]
    for copy in copies:
        copy.wait()


def norm_kernel(info_ref, ready_ref, mine_ref, theirs_ref, out_ref):
    steps = ready_ref.shape[1]
    factor = lax.rsqrt((mine_ref[...] + theirs_ref[...]) * (1.0 / (H * P_SIZE)) + 1e-05)
    for which in range(ready_ref.shape[0]):
        full = info_ref[2 + 2 * which] > 0
        rows = factor[which * steps : (which + 1) * steps]
        for b in range(0, ready_ref.shape[2], LANES):
            values = jnp.where(full, ready_ref[which, :, b : b + LANES] * rows, 0.0)
            out_ref[info_ref[3 * which], :, b : b + LANES] = values.astype(jnp.bfloat16)


def partner_masks(owners):
    gray = [i ^ (i >> 1) for i in range(owners)]
    near, far = gray[1 : owners // 2], gray[owners // 2 :]
    order = [0]
    for i, k in enumerate(far):
        order += [k, *near[i : i + 1]]
    return tuple(order)


def on_device(
    counts,
    move_plan,
    ssm_state,
    conv_x_state,
    conv_bc_state,
    x_in,
    bc_in,
    z_in,
    dt_in,
    conv_w_x,
    conv_b_x,
    conv_w_bc,
    conv_b_bc,
    dt_bias,
    a_log,
    d_skip,
    norm_w,
):
    owners = lax.axis_size("req")
    owner = lax.axis_index("req").astype(jnp.int32)
    slots, heads, columns = ssm_state.shape
    places, steps, channels = x_in.shape
    taps = conv_x_state.shape[1]
    groups, pair = conv_bc_state.shape[2:]
    blocks = channels // LANES
    share = heads * columns // LANES // owners
    aux_rows = taps * blocks + AUX
    f32 = jnp.float32
    direct = owners <= 16 and owners & (owners - 1) == 0 and share % (QUAD * heads) == 0
    masks = partner_masks(owners) if direct else (0,)
    pieces = len(masks)
    smem = pl.BlockSpec(memory_space=pltpu.SMEM)
    vmem = pl.BlockSpec(memory_space=pltpu.VMEM)
    anywhere = pl.BlockSpec(memory_space=pl.ANY)

    def shaped(*shape, dtype=f32):
        return jax.ShapeDtypeStruct(shape, dtype)

    def call(kernel, name, in_specs, out_specs, out_shape, scratch=(), **more):
        return pl.pallas_call(
            kernel,
            in_specs=in_specs,
            out_specs=out_specs,
            out_shape=out_shape,
            scratch_shapes=scratch,
            compiler_params=pltpu.CompilerParams(vmem_limit_bytes=VMEM_LIMIT),
            name=name,
            **more,
        )

    def in_hbm(*values):
        return [pltpu.with_memory_space_constraint(v, pltpu.MemorySpace.HBM) for v in values]

    me = owner.reshape(1)
    conv_x_taps = jnp.transpose(conv_x_state, (1, 0, 2))
    piece = (share + AUX, LANES) if direct else (owners, share + AUX, LANES)
    sent = [shaped(*piece, dtype=jnp.int16)] * pieces
    payload = call(
        functools.partial(pack_kernel, masks), "pack", [smem] + [anywhere] * 5, [vmem] * pieces, sent,
        [
            pltpu.SMEM(counts.shape, jnp.int32),
            pltpu.SMEM(move_plan.shape, jnp.int32),
            pltpu.VMEM(ssm_state.shape, f32),
            pltpu.VMEM(conv_x_taps.shape, jnp.bfloat16),
            pltpu.VMEM(conv_bc_state.shape, jnp.bfloat16),
            pltpu.VMEM((max(aux_rows, pieces * AUX), LANES), f32),
            pltpu.SemaphoreType.DMA((4 + slots * heads // BLOCK,)),
        ],
    )(me, *in_hbm(counts, move_plan, ssm_state, conv_x_taps, conv_bc_state))

    def exchange(values):
        if not direct:
            return [lax.all_to_all(values[0], "req", split_axis=0, concat_axis=0, tiled=True)]
        out = list(values)
        for i, k in enumerate(masks):
            if k:
                out[i] = lax.ppermute(values[i], "req", [(o, o ^ k) for o in range(owners)])
        return out

    spread = exchange(payload)

    _, x_late = lax.optimization_barrier((payload[0], x_in))
    rows = (places, steps * blocks, LANES)
    info, x_dense, gate, dec, dt_dense, wide, skip, wx, perm, new_conv_x, new_conv_bc = call(
        prep_kernel, "prep", [smem] + [anywhere] * 2 + [vmem] * 8, [smem] + [vmem] * 10,
        [
            shaped(INFO + owners, dtype=jnp.int32), shaped(*rows), shaped(*rows), shaped(*rows),
            shaped(*rows), shaped(places, heads, LANES), shaped(blocks, LANES),
            shaped((taps + 1) * blocks, LANES),
            shaped(QUAD * P_SIZE, 2 * steps * P_SIZE, dtype=jnp.bfloat16),
            shaped(taps, places, channels, dtype=jnp.bfloat16),
            shaped(*conv_bc_state.shape, dtype=jnp.bfloat16),
        ],
        [
            pltpu.SMEM(counts.shape, jnp.int32),
            pltpu.SMEM(move_plan.shape, jnp.int32),
            pltpu.SemaphoreType.DMA((2,)),
        ],
    )(
        me, *in_hbm(counts, move_plan), x_late, z_in, bc_in, dt_in, dt_bias.reshape(1, -1),
        a_log.reshape(1, -1), d_skip.reshape(1, -1), conv_w_x,
    )

    picked = call(
        functools.partial(pick_kernel, masks), "pick", [smem] + [vmem] * pieces, [vmem] * pieces, sent,
        [pltpu.VMEM((owners, *piece), jnp.int16)] if direct else [],
    )(info, *spread)
    got = exchange(picked)

    _, info = lax.optimization_barrier((picked[0], info))
    common = [x_dense, bc_in, gate, dec, dt_dense, skip, wx]
    common += [conv_b_x.reshape(blocks, LANES), conv_w_bc, conv_b_bc, perm, wide]
    scratch = [pltpu.VMEM((steps * heads, LANES), f32)] * 2 + [pltpu.VMEM((LANES, LANES), f32)]
    held, kept_gated, kept_sums = call(
        kept_kernel, "kept", [smem] + [vmem] * (3 + len(common)), [anywhere, vmem, vmem],
        [shaped(places, heads, columns), shaped(steps, blocks, LANES), shaped(steps, LANES)],
        scratch
        + [
            pltpu.VMEM((taps * blocks, LANES), f32),
            pltpu.VMEM((heads, columns), f32),
            pltpu.SemaphoreType.DMA,
        ],
    )(info, ssm_state, conv_x_taps, conv_bc_state, *common)
    moved_gated, sums, spread_rows, b_steps, wide_scaled = call(
        functools.partial(moved_kernel, masks), "moved",
        [smem] + [vmem] * (pieces + 1 + len(common)), [vmem] * 5,
        [
            shaped(steps, blocks, LANES), shaped(2 * steps, LANES),
            shaped(steps * heads, 2 * LANES, dtype=jnp.bfloat16),
            shaped(steps, groups, pair), shaped(heads, LANES),
        ],
        scratch + [pltpu.VMEM((max(aux_rows, pieces * AUX), LANES), f32)],
    )(info, *got, kept_sums, *common)
    theirs = lax.ppermute(sums, "tp", [(0, 1), (1, 0)])
    new_ssm, ready = call(
        functools.partial(state_kernel, masks), "state",
        [smem] + [vmem] * pieces + [anywhere] + [vmem] * 6, [anywhere, vmem],
        [shaped(places, heads, columns), shaped(places, steps, channels)],
        [
            pltpu.VMEM((steps * blocks, LANES), f32),
            pltpu.VMEM((heads, columns), f32),
            pltpu.SemaphoreType.DMA((pieces,)),
        ],
        input_output_aliases={1 + pieces: 0},
    )(
        info, *got, held, kept_gated, moved_gated, norm_w.reshape(blocks, LANES), spread_rows,
        b_steps, wide_scaled,
    )
    y_out = call(
        norm_kernel, "norm", [smem] + [vmem] * 3, vmem,
        shaped(places, steps, channels, dtype=jnp.bfloat16),
    )(info, ready, sums, theirs)
    return (y_out, new_ssm, jnp.transpose(new_conv_x, (1, 0, 2)), new_conv_bc)


def solution(mesh):
    in_specs = (
        P("parts"),
        P("parts"),
        P(("parts", "req"), "tp", None),
        P(("parts", "req"), None, "tp"),
        P(("parts", "req"), None, "tp", None),
        P(("parts", "req"), None, "tp"),
        P(("parts", "req"), None, "tp", None),
        P(("parts", "req"), None, "tp"),
        P(("parts", "req"), None, "tp"),
        P(None, "tp"),
        P("tp"),
        P(None, "tp", None),
        P("tp", None),
        P("tp"),
        P("tp"),
        P("tp"),
        P("tp"),
    )
    out_specs = (
        P(("parts", "req"), None, "tp"),
        P(("parts", "req"), "tp", None),
        P(("parts", "req"), None, "tp"),
        P(("parts", "req"), None, "tp", None),
    )
    return jax.shard_map(
        on_device, mesh=mesh, in_specs=in_specs, out_specs=out_specs, check_vma=False
    )
```

```python
import functools

import jax
import jax.numpy as jnp
from jax import lax
from jax.experimental import pallas as pl
from jax.experimental.pallas import tpu as pltpu
from jax.sharding import PartitionSpec as P

H = 128
P_SIZE = 64
LANES = 128
AUX = 16
BLOCK = 16
QUAD = 4
COPIES = 8
INFO = 8
REACH = 6.0
LEVELS = 32767.0
VMEM_LIMIT = 48 * 1024 * 1024


def level_code(top):
    code = jnp.floor(-8.0 / jnp.log(2.0) * jnp.log(jnp.maximum(top, 1e-30) / REACH) - 0.01)
    return jnp.clip(code, 0.0, 800.0)


def level_scale(code):
    return REACH * jnp.exp(code * (-0.125 * jnp.log(2.0)))


def moving_slot(counts_ref, plan_ref, me, slots):
    slot = jnp.int32(0)
    for local in range(1, slots):
        live = local < counts_ref[me]
        away = plan_ref[me * slots + local] // slots != me
        slot = jnp.where(live & away, local, slot)
    return slot


def dense_rows(rows_ref, at, values):
    count, channels = values.shape
    blocks = channels // LANES
    for b in range(blocks):
        part = values[:, b * LANES : (b + 1) * LANES]
        if count == 1:
            rows_ref[at + b : at + b + 1, :] = part
        else:
            rows_ref[pl.ds(at + b, count, stride=blocks), :] = part


def copy_rows(src, dst, sems, at, count):
    run = dst.shape[0] // count
    copies = []
    for i in range(count):
        rows = pl.ds(i * run, run)
        copies.append(pltpu.make_async_copy(src.at[rows], dst.at[rows], sems.at[at + i]))
        copies[-1].start()
    return copies


def of_slot(values, slot):
    return jnp.where(slot == 0, values[0], values[1])


def pack_kernel(masks, me_ref, counts_hbm, plan_hbm, state_hbm, cx_hbm, cb_hbm, *refs):
    *out_refs, counts_ref, plan_ref, state_ref, cx_ref, cb_ref, rows_ref, sems = refs
    direct = len(out_refs) > 1
    slots, heads, columns = state_ref.shape
    owners = len(out_refs) if direct else out_refs[0].shape[0]
    share = out_refs[0].shape[-2] - AUX
    run = min(share, BLOCK)
    each = share // heads
    me = me_ref[0]
    small = [
        pltpu.make_async_copy(src, dst, sems.at[i])
        for i, (src, dst) in enumerate(
            ((counts_hbm, counts_ref), (plan_hbm, plan_ref), (cx_hbm, cx_ref), (cb_hbm, cb_ref))
        )
    ]
    for copy in small:
        copy.start()
    large = []
    for at in range(0, heads, BLOCK):
        for slot in range(slots):
            part = (slot, pl.ds(at, BLOCK))
            copy = pltpu.make_async_copy(
                state_hbm.at[part], state_ref.at[part], sems.at[len(small) + len(large)]
            )
            copy.start()
            large.append(copy)
    small[0].wait()
    small[1].wait()
    slot = moving_slot(counts_ref, plan_ref, me, slots)
    small[2].wait()
    small[3].wait()
    taps, _, channels = cx_ref.shape
    groups = cb_ref.shape[2]
    blocks = channels // LANES
    cx = cx_ref[...].astype(jnp.float32)
    cx = jnp.where(slot == 0, cx[:, 0], cx[:, 1])
    cb = of_slot(cb_ref[...].astype(jnp.float32), slot)
    code_x = level_code(jnp.max(jnp.abs(cx)).reshape(1, 1))
    code_b = level_code(jnp.max(jnp.abs(cb)).reshape(1, 1))
    dense_rows(rows_ref, 0, cx)
    last = taps * blocks
    rows_ref[last:, :] = jnp.zeros((rows_ref.shape[0] - last, LANES), jnp.float32)
    for k in range(taps):
        rows_ref[last + k * groups : last + (k + 1) * groups, :] = cb[k]
    lane = lax.broadcasted_iota(jnp.int32, (BLOCK, LANES), 1)
    row = lax.broadcasted_iota(jnp.int32, (BLOCK, LANES), 0)
    codes = jnp.where(lane[:1] == heads, code_x, 0.0)
    codes = jnp.where(lane[:1] == heads + 1, code_b, codes)
    for q in range(heads // BLOCK):
        for copy in large[q * slots : (q + 1) * slots]:
            copy.wait()
        at = q * BLOCK
        top = jnp.abs(state_ref[slot, at : at + BLOCK, :LANES])
        for j in range(1, columns // LANES):
            tile = state_ref[slot, at : at + BLOCK, j * LANES : (j + 1) * LANES]
            top = jnp.maximum(top, jnp.abs(tile))
        code = level_code(jnp.max(top, axis=1, keepdims=True))
        codes = codes + jnp.sum(jnp.where(row + at == lane, code, 0.0), axis=0, keepdims=True)
        factor = jnp.broadcast_to(LEVELS / level_scale(code), (BLOCK, LANES))
        for j in range(columns // LANES):
            place = (me ^ masks[j // each]) * each + j % each if direct else j
            lanes = pl.ds(pl.multiple_of(place * LANES, LANES), LANES)
            tile = state_ref[slot, at : at + BLOCK, lanes] * factor
            tile = jnp.round(tile).astype(jnp.int32).astype(jnp.int16)
            for part in range(0, BLOCK, run):
                flat = j * heads + at + part
                rows = pl.ds(flat % share, run)
                if direct:
                    out_refs[flat // share][rows, :] = tile[part : part + run]
                else:
                    out_refs[0][flat // share, rows, :] = tile[part : part + run]
    factor_x = LEVELS / level_scale(code_x)
    factor_b = LEVELS / level_scale(code_b)
    line = lax.broadcasted_iota(jnp.int32, (AUX, LANES), 0)
    rows_ref[:last, :] = rows_ref[:last, :] * factor_x
    values = rows_ref[last : last + AUX, :] * factor_b
    rows_ref[last : last + AUX, :] = jnp.where(line == taps * groups, codes, values)
    for m in range(owners):
        if direct:
            values = rows_ref[pl.ds(pl.multiple_of((me ^ masks[m]) * AUX, AUX), AUX), :]
        elif m * AUX < last + AUX:
            values = rows_ref[m * AUX : (m + 1) * AUX, :]
        else:
            values = jnp.zeros((AUX, LANES), jnp.float32)
        values = jnp.round(values).astype(jnp.int32).astype(jnp.int16)
        if direct:
            out_refs[m][share:, :] = values
        else:
            out_refs[0][m, share:, :] = values


def pick_kernel(masks, info_ref, *refs):
    if len(refs) == 2:
        in_ref, out_ref = refs
        for m in range(out_ref.shape[0]):
            out_ref[m] = in_ref[info_ref[INFO + m]]
        return
    owners = len(refs) // 2
    *in_refs, all_ref = refs[:owners] + refs[-1:]
    out_refs = refs[owners:-1]
    me = info_ref[5]
    for i, k in enumerate(masks):
        all_ref[k] = in_refs[i][...]
    for i, k in enumerate(masks):
        out_refs[i][...] = all_ref[info_ref[INFO + (me ^ k)] ^ me]


def silu(v):
    return v / (1.0 + jnp.exp(-v))


def split(v):
    high = v.astype(jnp.bfloat16)
    low = (v - high.astype(jnp.float32)).astype(jnp.bfloat16)
    return high, low


def small_steps(seq_x, seq_b, wx_ref, bx_ref, wb_ref, bb_ref, steps):
    taps = len(seq_x) - steps + 1
    blocks = bx_ref.shape[0]
    xs, bs, cs = [], [], []
    for t in range(steps):
        total = bx_ref[...]
        pairs = bb_ref[...]
        for k in range(taps):
            total = total + wx_ref[k * blocks : (k + 1) * blocks, :] * seq_x[t + k]
            pairs = pairs + wb_ref[k] * seq_b[t + k]
        xs.append(silu(total))
        pairs = silu(pairs)
        turned = jnp.concatenate([pairs[:, LANES // 2 :], pairs[:, : LANES // 2]], 1)
        lower = lax.broadcasted_iota(jnp.int32, pairs.shape, 1) < LANES // 2
        bs.append(jnp.where(lower, pairs, turned))
        cs.append(jnp.where(lower, turned, pairs))
    return xs, bs, cs


def by_group(rows, count):
    groups = rows.shape[0]
    run = count // groups
    return jnp.concatenate(
        [jnp.broadcast_to(rows[g : g + 1], (run, rows.shape[1])) for g in range(groups)], 0
    )


def spread_x(xs, dec, dts, spread_ref):
    blocks = xs[0].shape[0]
    heads = 2 * blocks
    lower = lax.broadcasted_iota(jnp.int32, (blocks, LANES), 1) < LANES // 2
    later = None
    for t in reversed(range(len(xs))):
        weighted = xs[t] * dts[t]
        if later is not None:
            weighted = weighted * later
        later = dec[t] if later is None else later * dec[t]
        spread_ref[pl.ds(t * heads, blocks, stride=2), :] = jnp.where(lower, weighted, 0.0)
        spread_ref[pl.ds(t * heads + 1, blocks, stride=2), :] = jnp.where(lower, 0.0, weighted)
    return jnp.concatenate(split(spread_ref[...]), 1)


def new_state(tile, first, wide, spread, bs, place_ref, write):
    steps = len(bs)
    heads = wide.shape[0]
    b_rows = [by_group(b, heads) for b in bs]
    for j in range(0, P_SIZE * P_SIZE // LANES, 2):
        at = pl.ds(pl.multiple_of(first(j) * LANES, LANES), 2 * LANES)
        grown = jnp.dot(
            spread,
            jnp.concatenate([place_ref[:, at]] * (spread.shape[1] // P_SIZE), 0),
            preferred_element_type=jnp.float32,
        )
        for half in range(2):
            new = wide * tile(j + half)
            for t in range(steps):
                piece = grown[t * heads : (t + 1) * heads, half * LANES : (half + 1) * LANES]
                new = new + piece * b_rows[t]
            write(j + half, new)


def against_c(tile, first, cs, perm_ref, rows_ref):
    steps = len(cs)
    groups = cs[0].shape[0]
    lower = lax.broadcasted_iota(jnp.int32, (steps, LANES), 1) < LANES // 2
    lefts = []
    for g in range(groups):
        rows = jnp.concatenate([c[g : g + 1] for c in cs], 0)
        rows = jnp.concatenate([jnp.where(lower, rows, 0.0), jnp.where(lower, 0.0, rows)], 0)
        lefts.append(jnp.concatenate([jnp.concatenate([v, v], 1) for v in split(rows)], 0))
    count = P_SIZE * P_SIZE // LANES
    line = 2 * steps
    run = LANES // QUAD
    for u in range(0, count, 2 * QUAD):
        parts = [jnp.concatenate(split(tile(j)), 1) for j in range(u, u + 2 * QUAD)]
        for g in range(groups):
            right = jnp.concatenate([p[g * run : (g + 1) * run] for p in parts], 0)
            out = lax.dot_general(
                lefts[g], right, (((1,), (1,)), ((), ())), preferred_element_type=jnp.float32
            )
            out = out[:line] + out[line:]
            for w in range(2):
                quad = first(u + w * QUAD) // QUAD
                at = pl.ds(pl.multiple_of(g * (count // QUAD) * line + quad * line, 8), line)
                rows_ref[at, :] = out[:, w * LANES : (w + 1) * LANES]
    turned = jnp.transpose(rows_ref[...])
    lower = lax.broadcasted_iota(jnp.int32, (run, LANES), 1) < LANES // 2
    straight = [turned[i * run : (i + 1) * run] for i in range(QUAD)]
    rolled = [
        jnp.concatenate([v[:, LANES // 2 :], v[:, : LANES // 2]], 1) for v in straight
    ]
    low_group = [jnp.where(lower, straight[i], rolled[i + 1]) for i in range(0, QUAD, 2)]
    high_group = [jnp.where(lower, rolled[i], straight[i + 1]) for i in range(0, QUAD, 2)]
    values = jnp.concatenate(
        [jnp.concatenate(low_group, 1), jnp.concatenate(high_group, 1)], 0
    )
    high = values.astype(jnp.bfloat16)
    rest = values - high.astype(jnp.float32)
    middle = rest.astype(jnp.bfloat16)
    low = (rest - middle.astype(jnp.float32)).astype(jnp.bfloat16)
    heads = values.shape[0]
    out = jnp.dot(
        jnp.concatenate([high, middle, low], 0), perm_ref[...], preferred_element_type=jnp.float32
    )
    return out[:heads] + out[heads : 2 * heads] + out[2 * heads :]


def gated_steps(mixed, scale, xs, bs, cs, dec, dts, skip, gate, mixed_ref):
    steps = len(xs)
    heads = mixed.shape[0]
    blocks = heads // 2
    lower = lax.broadcasted_iota(jnp.int32, (blocks, LANES), 1) < LANES // 2
    for t in range(steps):
        part = mixed[:, t * LANES : (t + 1) * LANES]
        mixed_ref[t * heads : (t + 1) * heads, :] = part if scale is None else part * scale
    gated, sums = [], []
    ahead = None
    weights = []
    for t in range(steps):
        weights = [w * dec[t] for w in weights] + [dts[t]]
        ahead = dec[t] if ahead is None else ahead * dec[t]
        even = mixed_ref[pl.ds(t * heads, blocks, stride=2), :]
        odd = mixed_ref[pl.ds(t * heads + 1, blocks, stride=2), :]
        out = ahead * jnp.where(lower, even, odd) + skip * xs[t]
        for s in range(t + 1):
            inner = 0.5 * jnp.sum(bs[s] * cs[t], axis=1, keepdims=True)
            inner = by_group(jnp.broadcast_to(inner, (inner.shape[0], LANES)), blocks)
            out = out + weights[s] * inner * xs[s]
        out = out * gate[t]
        gated.append(out)
        squares = jnp.sum(jnp.sum(out * out, axis=0, keepdims=True), axis=1, keepdims=True)
        sums.append(jnp.broadcast_to(squares, (1, LANES)))
    return gated, sums


def prep_kernel(
    me_ref, counts_hbm, plan_hbm, x_hbm, z_hbm, wx_hbm, state_hbm, bc_ref, dt_ref, bias_ref,
    rate_ref, skip_ref,
    info_ref, xd_ref, gate_ref, dec_ref, dtd_ref, wide_ref, skipd_ref, wxd_ref, perm_ref,
    place_ref, kept_ref, cx_ref, cb_ref,
    counts_ref, plan_ref, x_ref, z_ref, wx_ref, sems,
):
    slots, steps, channels = x_ref.shape
    heads = dt_ref.shape[2]
    blocks = channels // LANES
    taps = cx_ref.shape[0]
    me = me_ref[0]
    copies = [
        pltpu.make_async_copy(src, dst, sems.at[i])
        for i, (src, dst) in enumerate(
            (
                (counts_hbm, counts_ref), (plan_hbm, plan_ref), (x_hbm, x_ref), (z_hbm, z_ref),
                (wx_hbm, wx_ref),
            )
        )
    ]
    for copy in copies:
        copy.start()
    copies[0].wait()
    copies[1].wait()
    reqs = plan_ref.shape[0]
    owners = counts_ref.shape[0]
    for d in range(owners):
        info_ref[INFO + d] = 0

    def look(r, carry):
        kept_to, kept_from, has_kept, moved_to, has_moved = carry
        home, local = r // slots, r % slots
        goal = plan_ref[r]
        live = local < counts_ref[home]
        owner, place = goal // slots, goal % slots
        mine = live & (owner == me)
        own = mine & (home == me)
        into = mine & (home != me)

        @pl.when(live & (owner != home))
        def _():
            info_ref[INFO + owner] = home

        return (
            jnp.where(own, place, kept_to), jnp.where(own, local, kept_from),
            jnp.where(own, 1, has_kept), jnp.where(into, place, moved_to),
            jnp.where(into, 1, has_moved),
        )

    carry = (jnp.int32(0),) * 5
    if reqs <= 32:
        for r in range(reqs):
            carry = look(r, carry)
    else:
        carry = lax.fori_loop(0, reqs, look, carry)
    kept_to, kept_from, has_kept, moved_to, has_moved = carry
    moved_to = jnp.where(has_moved > 0, moved_to, jnp.where(has_kept > 0, 1 - kept_to, 0))
    kept_to = 1 - moved_to
    for i, v in enumerate((kept_to, kept_from, has_kept, moved_to, has_moved, me)):
        info_ref[i] = v
    copies += copy_rows(state_hbm.at[kept_from], kept_ref, sems, len(copies), COPIES)
    shape = perm_ref.shape
    line = lax.broadcasted_iota(jnp.int32, shape, 0)
    lane = lax.broadcasted_iota(jnp.int32, shape, 1)
    span = shape[0] // QUAD
    p = (line % span // (2 * steps) * QUAD + line // span) * 2 + line % (2 * steps) // steps
    hit = (lane // LANES == line % steps) & (lane % P_SIZE == p)
    perm_ref[...] = jnp.where(hit, 1.0, 0.0).astype(jnp.bfloat16)
    shape = place_ref.shape
    line = lax.broadcasted_iota(jnp.int32, shape, 0)
    lane = lax.broadcasted_iota(jnp.int32, shape, 1)
    place_ref[...] = jnp.where(lane // P_SIZE == line, 1.0, 0.0).astype(jnp.bfloat16)
    rate = jnp.exp(rate_ref[...])
    raw = [dt_ref[s] + bias_ref[...] for s in range(slots)]
    delta = [jnp.maximum(v, 0.0) + jnp.log1p(jnp.exp(-jnp.abs(v))) for v in raw]
    decay = [jnp.exp(-v * rate) for v in delta]
    at = lax.broadcasted_iota(jnp.int32, (blocks, heads), 0)
    of = lax.broadcasted_iota(jnp.int32, (blocks, heads), 1)
    lines = [v[t : t + 1] for v in delta + decay for t in range(steps)] + [skip_ref[...]]
    spread = jnp.concatenate([jnp.where(of // 2 == at, line, 0.0) for line in lines], 0)
    high = spread.astype(jnp.bfloat16)
    rest = spread - high.astype(jnp.float32)
    middle = rest.astype(jnp.bfloat16)
    low = (rest - middle.astype(jnp.float32)).astype(jnp.bfloat16)
    head = lax.broadcasted_iota(jnp.int32, (heads, LANES), 0)
    lane = lax.broadcasted_iota(jnp.int32, (heads, LANES), 1)
    chosen = jnp.where(head % 2 == lane // (LANES // 2), 1.0, 0.0).astype(jnp.bfloat16)
    out = jnp.dot(high, chosen, preferred_element_type=jnp.float32)
    out = out + jnp.dot(middle, chosen, preferred_element_type=jnp.float32)
    out = out + jnp.dot(low, chosen, preferred_element_type=jnp.float32)
    run = steps * blocks
    for s in range(slots):
        dtd_ref[s] = out[s * run : (s + 1) * run]
        dec_ref[s] = out[(slots + s) * run : (slots + s + 1) * run]
        total = decay[s][:1]
        for t in range(1, steps):
            total = total * decay[s][t : t + 1]
        total = jnp.concatenate([total, total], 1)
        wide = jnp.sum(jnp.where(head == lane, total, 0.0), axis=1, keepdims=True)
        wide_ref[s] = jnp.broadcast_to(wide, (heads, LANES))
    skipd_ref[...] = out[2 * slots * run :]
    for copy in copies[2:5]:
        copy.wait()
    x = [x_ref[s].astype(jnp.float32) for s in range(slots)]
    for s in range(slots):
        dense_rows(xd_ref.at[s], 0, x[s])
        dense_rows(gate_ref.at[s], 0, z_ref[s].astype(jnp.float32))
    dense_rows(wxd_ref, 0, wx_ref[...])
    gate_ref[...] = silu(gate_ref[...])
    full = [jnp.where(kept_to == s, has_kept, has_moved) > 0 for s in range(slots)]
    for k in range(taps):
        t = steps - taps + k
        rows = [jnp.where(full[s], x[s][t : t + 1], 0.0) for s in range(slots)]
        cx_ref[k] = jnp.concatenate(rows, 0).astype(jnp.bfloat16)
        for s in range(slots):
            pairs = bc_ref[s, t].astype(jnp.float32)
            cb_ref[s, k] = jnp.where(full[s], pairs, 0.0).astype(jnp.bfloat16)
    for copy in copies[5:]:
        copy.wait()


def slot_inputs(slot, steps, x_ref, bc_ref, gate_ref, dec_ref, dt_ref):
    blocks = x_ref.shape[1] // steps
    rows = [pl.ds(t * blocks, blocks) for t in range(steps)]
    return [[ref[slot, r, :] for r in rows] for ref in (x_ref, gate_ref, dec_ref, dt_ref)] + [
        [bc_ref[slot, t].astype(jnp.float32) for t in range(steps)]
    ]


def kept_kernel(
    info_ref, state_ref, cx_ref, cb_ref, x_ref, bc_ref, gate_ref, dec_ref, dt_ref, skip_ref,
    wx_ref, bx_ref, wb_ref, bb_ref, perm_ref, wide_ref, place_ref,
    out_hbm, gated_ref, sums_ref, spread_ref, mixed_ref, turn_ref, rows_ref, new_ref, sems,
):
    steps = bc_ref.shape[1]
    blocks = bx_ref.shape[0]
    taps = cx_ref.shape[0]
    slot, origin, full = info_ref[0], info_ref[1], info_ref[2] > 0
    cx = cx_ref[...].astype(jnp.float32)
    dense_rows(rows_ref, 0, jnp.where(origin == 0, cx[:, 0], cx[:, 1]))
    cb = of_slot(cb_ref[...].astype(jnp.float32), origin)
    new_x, gate, dec, dts, new_b = slot_inputs(
        slot, steps, x_ref, bc_ref, gate_ref, dec_ref, dt_ref
    )
    seq_x = [rows_ref[k * blocks : (k + 1) * blocks, :] for k in range(taps)] + new_x
    seq_b = [cb[k] for k in range(taps)] + new_b
    xs, bs, cs = small_steps(seq_x, seq_b, wx_ref, bx_ref, wb_ref, bb_ref, steps)

    def write(j, new):
        new_ref[:, j * LANES : (j + 1) * LANES] = jnp.where(full, new, 0.0)

    def tile(j):
        return state_ref[:, j * LANES : (j + 1) * LANES]

    mixed = against_c(tile, lambda j: j, cs, perm_ref, turn_ref)
    gated, sums = gated_steps(
        mixed, None, xs, bs, cs, dec, dts, skip_ref[...], gate, mixed_ref
    )
    spread = spread_x(xs, dec, dts, spread_ref)
    new_state(tile, lambda j: j, wide_ref[slot], spread, bs, place_ref, write)
    copies = copy_rows(new_ref, out_hbm.at[slot], sems, 0, COPIES)
    for t in range(steps):
        gated_ref[t] = gated[t]
    sums_ref[...] = jnp.concatenate(sums, 0)
    for copy in copies:
        copy.wait()


def piece_tiles(masks, me, got_refs, heads):
    direct = len(masks) > 1
    share = got_refs[0].shape[-2] - AUX
    run = min(share, heads)
    each = share // heads

    def load(m, rows):
        part = got_refs[m][rows, :] if direct else got_refs[0][m, rows, :]
        return part.astype(jnp.int32).astype(jnp.float32)

    def tile(j):
        if direct:
            return load(j // each, pl.ds(j % each * heads, heads))
        flats = range(j * heads, (j + 1) * heads, run)
        return jnp.concatenate([load(f // share, pl.ds(f % share, run)) for f in flats], 0)

    def first(j):
        return (me ^ masks[j // each]) * each + j % each if direct else j

    return load, tile, first


def moved_kernel(masks, info_ref, *refs):
    pieces = len(masks)
    got_refs = refs[:pieces]
    (
        kept_sums_ref, x_ref, bc_ref, gate_ref, dec_ref, dt_ref, skip_ref,
        wx_ref, bx_ref, wb_ref, bb_ref, perm_ref, wide_ref,
        gated_ref, sums_ref, spread_ref, b_ref, wide_out_ref, rows_ref, mixed_ref, turn_ref, aux_ref,
    ) = refs[pieces:]
    direct = pieces > 1
    steps, groups = bc_ref.shape[1:3]
    blocks = bx_ref.shape[0]
    taps = wx_ref.shape[0] // blocks - 1
    heads = wide_ref.shape[1]
    share = got_refs[0].shape[-2] - AUX
    slot, me = info_ref[3], info_ref[5]
    new_x, gate, dec, dts, new_b = slot_inputs(
        slot, steps, x_ref, bc_ref, gate_ref, dec_ref, dt_ref
    )
    load, tile, first = piece_tiles(masks, me, got_refs, heads)
    for m in range(pieces if direct else got_refs[0].shape[0]):
        if direct:
            at = pl.ds(pl.multiple_of((me ^ masks[m]) * AUX, AUX), AUX)
            aux_ref[at, :] = load(m, pl.ds(share, AUX))
        elif m * AUX < aux_ref.shape[0]:
            aux_ref[m * AUX : (m + 1) * AUX, :] = load(m, pl.ds(share, AUX))

    last = aux_ref[taps * blocks : taps * blocks + AUX, :]
    codes = last[taps * groups : taps * groups + 1]
    row = lax.broadcasted_iota(jnp.int32, (heads, LANES), 0)
    lane = lax.broadcasted_iota(jnp.int32, (heads, LANES), 1)
    code = jnp.sum(jnp.where(row == lane, codes, 0.0), axis=1, keepdims=True)
    scale = level_scale(code) * (1.0 / LEVELS)
    scale_x = level_scale(codes[:, heads : heads + 1]) * (1.0 / LEVELS)
    scale_b = level_scale(codes[:, heads + 1 : heads + 2]) * (1.0 / LEVELS)
    seq_x = [aux_ref[k * blocks : (k + 1) * blocks, :] * scale_x for k in range(taps)] + new_x
    seq_b = [last[k * groups : (k + 1) * groups] * scale_b for k in range(taps)] + new_b
    xs, bs, cs = small_steps(seq_x, seq_b, wx_ref, bx_ref, wb_ref, bb_ref, steps)
    mixed = against_c(tile, first, cs, perm_ref, turn_ref)
    gated, sums = gated_steps(
        mixed, scale, xs, bs, cs, dec, dts, skip_ref[...], gate, mixed_ref
    )
    for t in range(steps):
        gated_ref[t] = gated[t]
        b_ref[t] = bs[t]
    sums_ref[...] = jnp.concatenate([kept_sums_ref[...]] + sums, 0)
    spread_ref[...] = spread_x(xs, dec, dts, rows_ref)
    wide_out_ref[...] = wide_ref[slot] * scale


def state_kernel(masks, info_ref, *refs):
    pieces = len(masks)
    got_refs = refs[:pieces]
    (
        held_hbm, spread_ref, b_ref, wide_ref, place_ref, kept_ref, moved_ref, norm_ref,
        out_hbm, ready_ref, rows_ref, new_ref, sems,
    ) = refs[pieces:]
    del held_hbm
    direct = pieces > 1
    heads = wide_ref.shape[0]
    count = P_SIZE * P_SIZE // LANES
    each = (got_refs[0].shape[-2] - AUX) // heads if direct else count
    slot, full, me = info_ref[3], info_ref[4] > 0, info_ref[5]
    _, tile, first = piece_tiles(masks, me, got_refs, heads)
    copies = []

    def write(j, new):
        at = pl.ds(pl.multiple_of(first(j) * LANES, LANES), LANES)
        new_ref[:, at] = jnp.where(full, new, 0.0)
        if j % each == each - 1:
            span = pl.ds(pl.multiple_of(first(j - each + 1) * LANES, LANES), each * LANES)
            copy = pltpu.make_async_copy(
                new_ref.at[:, span], out_hbm.at[slot, :, span], sems.at[len(copies)]
            )
            copy.start()
            copies.append(copy)

    bs = [b_ref[t] for t in range(b_ref.shape[0])]
    new_state(tile, first, wide_ref[...], spread_ref[...], bs, place_ref, write)
    steps, blocks = kept_ref.shape[:2]
    for which, ref in enumerate((kept_ref, moved_ref)):
        for t in range(steps):
            rows_ref[t * blocks : (t + 1) * blocks, :] = ref[t] * norm_ref[...]
        for b in range(blocks):
            ready_ref[which, :, b * LANES : (b + 1) * LANES] = rows_ref[
                pl.ds(b, steps, stride=blocks), :
            ]
    for copy in copies:
        copy.wait()


def norm_kernel(info_ref, ready_ref, mine_ref, theirs_ref, out_ref):
    steps = ready_ref.shape[1]
    factor = lax.rsqrt((mine_ref[...] + theirs_ref[...]) * (1.0 / (H * P_SIZE)) + 1e-05)
    for which in range(ready_ref.shape[0]):
        full = info_ref[2 + 2 * which] > 0
        rows = factor[which * steps : (which + 1) * steps]
        for b in range(0, ready_ref.shape[2], LANES):
            values = jnp.where(full, ready_ref[which, :, b : b + LANES] * rows, 0.0)
            out_ref[info_ref[3 * which], :, b : b + LANES] = values.astype(jnp.bfloat16)


def partner_masks(owners):
    gray = [i ^ (i >> 1) for i in range(owners)]
    near, far = gray[1 : owners // 2], gray[owners // 2 :]
    order = [0]
    for i, k in enumerate(far):
        order += [k, *near[i : i + 1]]
    return tuple(order)


def on_device(
    counts,
    move_plan,
    ssm_state,
    conv_x_state,
    conv_bc_state,
    x_in,
    bc_in,
    z_in,
    dt_in,
    conv_w_x,
    conv_b_x,
    conv_w_bc,
    conv_b_bc,
    dt_bias,
    a_log,
    d_skip,
    norm_w,
):
    owners = lax.axis_size("req")
    owner = lax.axis_index("req").astype(jnp.int32)
    slots, heads, columns = ssm_state.shape
    places, steps, channels = x_in.shape
    taps = conv_x_state.shape[1]
    groups, pair = conv_bc_state.shape[2:]
    blocks = channels // LANES
    share = heads * columns // LANES // owners
    aux_rows = taps * blocks + AUX
    f32 = jnp.float32
    direct = owners <= 16 and owners & (owners - 1) == 0 and share % (QUAD * heads) == 0
    masks = partner_masks(owners) if direct else (0,)
    pieces = len(masks)
    smem = pl.BlockSpec(memory_space=pltpu.SMEM)
    vmem = pl.BlockSpec(memory_space=pltpu.VMEM)
    anywhere = pl.BlockSpec(memory_space=pl.ANY)

    def shaped(*shape, dtype=f32):
        return jax.ShapeDtypeStruct(shape, dtype)

    def call(kernel, name, in_specs, out_specs, out_shape, scratch=(), **more):
        return pl.pallas_call(
            kernel,
            in_specs=in_specs,
            out_specs=out_specs,
            out_shape=out_shape,
            scratch_shapes=scratch,
            compiler_params=pltpu.CompilerParams(vmem_limit_bytes=VMEM_LIMIT),
            name=name,
            **more,
        )

    def in_hbm(*values):
        return [pltpu.with_memory_space_constraint(v, pltpu.MemorySpace.HBM) for v in values]

    me = owner.reshape(1)
    conv_x_taps = jnp.transpose(conv_x_state, (1, 0, 2))
    piece = (share + AUX, LANES) if direct else (owners, share + AUX, LANES)
    sent = [shaped(*piece, dtype=jnp.int16)] * pieces
    payload = call(
        functools.partial(pack_kernel, masks), "pack", [smem] + [anywhere] * 5, [vmem] * pieces, sent,
        [
            pltpu.SMEM(counts.shape, jnp.int32),
            pltpu.SMEM(move_plan.shape, jnp.int32),
            pltpu.VMEM(ssm_state.shape, f32),
            pltpu.VMEM(conv_x_taps.shape, jnp.bfloat16),
            pltpu.VMEM(conv_bc_state.shape, jnp.bfloat16),
            pltpu.VMEM((max(aux_rows, pieces * AUX), LANES), f32),
            pltpu.SemaphoreType.DMA((4 + slots * heads // BLOCK,)),
        ],
    )(me, *in_hbm(counts, move_plan, ssm_state, conv_x_taps, conv_bc_state))

    def exchange(values):
        if not direct:
            return [lax.all_to_all(values[0], "req", split_axis=0, concat_axis=0, tiled=True)]
        out = list(values)
        for i, k in enumerate(masks):
            if k:
                out[i] = lax.ppermute(values[i], "req", [(o, o ^ k) for o in range(owners)])
        return out

    spread = exchange(payload)

    _, me_late = lax.optimization_barrier((payload[0], me))
    rows = (places, steps * blocks, LANES)
    info, x_dense, gate, dec, dt_dense, wide, skip, wx, perm, place, kept_state, *convs = call(
        prep_kernel, "prep", [smem] + [anywhere] * 6 + [vmem] * 5, [smem] + [vmem] * 12,
        [
            shaped(INFO + owners, dtype=jnp.int32), shaped(*rows), shaped(*rows), shaped(*rows),
            shaped(*rows), shaped(places, heads, LANES), shaped(blocks, LANES),
            shaped((taps + 1) * blocks, LANES),
            shaped(QUAD * P_SIZE, 2 * steps * P_SIZE, dtype=jnp.bfloat16),
            shaped(P_SIZE, columns, dtype=jnp.bfloat16), shaped(heads, columns),
            shaped(taps, places, channels, dtype=jnp.bfloat16),
            shaped(*conv_bc_state.shape, dtype=jnp.bfloat16),
        ],
        [
            pltpu.SMEM(counts.shape, jnp.int32),
            pltpu.SMEM(move_plan.shape, jnp.int32),
            pltpu.VMEM(x_in.shape, jnp.bfloat16),
            pltpu.VMEM(z_in.shape, jnp.bfloat16),
            pltpu.VMEM(conv_w_x.shape, f32),
            pltpu.SemaphoreType.DMA((5 + COPIES,)),
        ],
    )(
        me_late, *in_hbm(counts, move_plan, x_in, z_in, conv_w_x, ssm_state), bc_in, dt_in,
        dt_bias.reshape(1, -1), a_log.reshape(1, -1), d_skip.reshape(1, -1),
    )

    picked = call(
        functools.partial(pick_kernel, masks), "pick", [smem] + [vmem] * pieces, [vmem] * pieces, sent,
        [pltpu.VMEM((owners, *piece), jnp.int16)] if direct else [],
    )(info, *spread)
    got = exchange(picked)

    _, info = lax.optimization_barrier((picked[0], info))
    common = [x_dense, bc_in, gate, dec, dt_dense, skip, wx]
    common += [conv_b_x.reshape(blocks, LANES), conv_w_bc, conv_b_bc, perm, wide]
    scratch = [pltpu.VMEM((steps * heads, LANES), f32)] * 2 + [pltpu.VMEM((LANES, LANES), f32)]
    held, kept_gated, kept_sums = call(
        kept_kernel, "kept", [smem] + [vmem] * (4 + len(common)), [anywhere, vmem, vmem],
        [shaped(places, heads, columns), shaped(steps, blocks, LANES), shaped(steps, LANES)],
        scratch
        + [
            pltpu.VMEM((taps * blocks, LANES), f32),
            pltpu.VMEM((heads, columns), f32),
            pltpu.SemaphoreType.DMA((COPIES,)),
        ],
    )(info, kept_state, conv_x_taps, conv_bc_state, *common, place)
    moved_gated, sums, spread_rows, b_steps, wide_scaled = call(
        functools.partial(moved_kernel, masks), "moved",
        [smem] + [vmem] * (pieces + 1 + len(common)), [vmem] * 5,
        [
            shaped(steps, blocks, LANES), shaped(2 * steps, LANES),
            shaped(steps * heads, 2 * LANES, dtype=jnp.bfloat16),
            shaped(steps, groups, pair), shaped(heads, LANES),
        ],
        scratch + [pltpu.VMEM((max(aux_rows, pieces * AUX), LANES), f32)],
    )(info, *got, kept_sums, *common)
    theirs = lax.ppermute(sums, "tp", [(0, 1), (1, 0)])
    new_ssm, ready = call(
        functools.partial(state_kernel, masks), "state",
        [smem] + [vmem] * pieces + [anywhere] + [vmem] * 7, [anywhere, vmem],
        [shaped(places, heads, columns), shaped(places, steps, channels)],
        [
            pltpu.VMEM((steps * blocks, LANES), f32),
            pltpu.VMEM((heads, columns), f32),
            pltpu.SemaphoreType.DMA((pieces,)),
        ],
        input_output_aliases={1 + pieces: 0},
    )(
        info, *got, held, spread_rows, b_steps, wide_scaled, place, kept_gated, moved_gated,
        norm_w.reshape(blocks, LANES),
    )
    y_out = call(
        norm_kernel, "norm", [smem] + [vmem] * 3, vmem,
        shaped(places, steps, channels, dtype=jnp.bfloat16),
    )(info, ready, sums, theirs)
    return (y_out, new_ssm, jnp.transpose(convs[0], (1, 0, 2)), convs[1])


def solution(mesh):
    in_specs = (
        P("parts"),
        P("parts"),
        P(("parts", "req"), "tp", None),
        P(("parts", "req"), None, "tp"),
        P(("parts", "req"), None, "tp", None),
        P(("parts", "req"), None, "tp"),
        P(("parts", "req"), None, "tp", None),
        P(("parts", "req"), None, "tp"),
        P(("parts", "req"), None, "tp"),
        P(None, "tp"),
        P("tp"),
        P(None, "tp", None),
        P("tp", None),
        P("tp"),
        P("tp"),
        P("tp"),
        P("tp"),
    )
    out_specs = (
        P(("parts", "req"), None, "tp"),
        P(("parts", "req"), "tp", None),
        P(("parts", "req"), None, "tp"),
        P(("parts", "req"), None, "tp", None),
    )
    return jax.shard_map(
        on_device, mesh=mesh, in_specs=in_specs, out_specs=out_specs, check_vma=False
    )
```

```python
import functools

import jax
import jax.numpy as jnp
from jax import lax
from jax.experimental import pallas as pl
from jax.experimental.pallas import tpu as pltpu
from jax.sharding import PartitionSpec as P

H = 128
P_SIZE = 64
LANES = 128
AUX = 16
BLOCK = 16
QUAD = 4
COPIES = 8
INFO = 8
REACH = 6.0
LEVELS = 32767.0
VMEM_LIMIT = 48 * 1024 * 1024


def level_code(top):
    code = jnp.floor(-8.0 / jnp.log(2.0) * jnp.log(jnp.maximum(top, 1e-30) / REACH) - 0.01)
    return jnp.clip(code, 0.0, 800.0)


def level_scale(code):
    return REACH * jnp.exp(code * (-0.125 * jnp.log(2.0)))


def moving_slot(counts_ref, plan_ref, me, slots):
    slot = jnp.int32(0)
    for local in range(1, slots):
        live = local < counts_ref[me]
        away = plan_ref[me * slots + local] // slots != me
        slot = jnp.where(live & away, local, slot)
    return slot


def dense_rows(rows_ref, at, values):
    count, channels = values.shape
    blocks = channels // LANES
    for b in range(blocks):
        part = values[:, b * LANES : (b + 1) * LANES]
        if count == 1:
            rows_ref[at + b : at + b + 1, :] = part
        else:
            rows_ref[pl.ds(at + b, count, stride=blocks), :] = part


def copy_rows(src, dst, sems, at, count):
    run = dst.shape[0] // count
    copies = []
    for i in range(count):
        rows = pl.ds(i * run, run)
        copies.append(pltpu.make_async_copy(src.at[rows], dst.at[rows], sems.at[at + i]))
        copies[-1].start()
    return copies


def of_slot(values, slot):
    return jnp.where(slot == 0, values[0], values[1])


def pack_kernel(masks, me_ref, counts_hbm, plan_hbm, state_hbm, cx_hbm, cb_hbm, *refs):
    *out_refs, counts_ref, plan_ref, state_ref, cx_ref, cb_ref, rows_ref, sems = refs
    direct = len(out_refs) > 1
    slots, heads, columns = state_ref.shape
    owners = len(out_refs) if direct else out_refs[0].shape[0]
    share = out_refs[0].shape[-2] - AUX
    run = min(share, BLOCK)
    each = share // heads
    me = me_ref[0]
    small = [
        pltpu.make_async_copy(src, dst, sems.at[i])
        for i, (src, dst) in enumerate(
            ((counts_hbm, counts_ref), (plan_hbm, plan_ref), (cx_hbm, cx_ref), (cb_hbm, cb_ref))
        )
    ]
    for copy in small:
        copy.start()
    large = []
    for at in range(0, heads, BLOCK):
        for slot in range(slots):
            part = (slot, pl.ds(at, BLOCK))
            copy = pltpu.make_async_copy(
                state_hbm.at[part], state_ref.at[part], sems.at[len(small) + len(large)]
            )
            copy.start()
            large.append(copy)
    small[0].wait()
    small[1].wait()
    slot = moving_slot(counts_ref, plan_ref, me, slots)
    small[2].wait()
    small[3].wait()
    taps, _, channels = cx_ref.shape
    groups = cb_ref.shape[2]
    blocks = channels // LANES
    cx = cx_ref[...].astype(jnp.float32)
    cx = jnp.where(slot == 0, cx[:, 0], cx[:, 1])
    cb = of_slot(cb_ref[...].astype(jnp.float32), slot)
    code_x = level_code(jnp.max(jnp.abs(cx)).reshape(1, 1))
    code_b = level_code(jnp.max(jnp.abs(cb)).reshape(1, 1))
    dense_rows(rows_ref, 0, cx)
    last = taps * blocks
    rows_ref[last:, :] = jnp.zeros((rows_ref.shape[0] - last, LANES), jnp.float32)
    for k in range(taps):
        rows_ref[last + k * groups : last + (k + 1) * groups, :] = cb[k]
    lane = lax.broadcasted_iota(jnp.int32, (BLOCK, LANES), 1)
    row = lax.broadcasted_iota(jnp.int32, (BLOCK, LANES), 0)
    codes = jnp.where(lane[:1] == heads, code_x, 0.0)
    codes = jnp.where(lane[:1] == heads + 1, code_b, codes)
    for q in range(heads // BLOCK):
        for copy in large[q * slots : (q + 1) * slots]:
            copy.wait()
        at = q * BLOCK
        top = jnp.abs(state_ref[slot, at : at + BLOCK, :LANES])
        for j in range(1, columns // LANES):
            tile = state_ref[slot, at : at + BLOCK, j * LANES : (j + 1) * LANES]
            top = jnp.maximum(top, jnp.abs(tile))
        code = level_code(jnp.max(top, axis=1, keepdims=True))
        codes = codes + jnp.sum(jnp.where(row + at == lane, code, 0.0), axis=0, keepdims=True)
        factor = jnp.broadcast_to(LEVELS / level_scale(code), (BLOCK, LANES))
        for j in range(columns // LANES):
            place = (me ^ masks[j // each]) * each + j % each if direct else j
            lanes = pl.ds(pl.multiple_of(place * LANES, LANES), LANES)
            tile = state_ref[slot, at : at + BLOCK, lanes] * factor
            tile = jnp.round(tile).astype(jnp.int32).astype(jnp.int16)
            for part in range(0, BLOCK, run):
                flat = j * heads + at + part
                rows = pl.ds(flat % share, run)
                if direct:
                    out_refs[flat // share][rows, :] = tile[part : part + run]
                else:
                    out_refs[0][flat // share, rows, :] = tile[part : part + run]
    factor_x = LEVELS / level_scale(code_x)
    factor_b = LEVELS / level_scale(code_b)
    line = lax.broadcasted_iota(jnp.int32, (AUX, LANES), 0)
    rows_ref[:last, :] = rows_ref[:last, :] * factor_x
    values = rows_ref[last : last + AUX, :] * factor_b
    rows_ref[last : last + AUX, :] = jnp.where(line == taps * groups, codes, values)
    for m in range(owners):
        if direct:
            values = rows_ref[pl.ds(pl.multiple_of((me ^ masks[m]) * AUX, AUX), AUX), :]
        elif m * AUX < last + AUX:
            values = rows_ref[m * AUX : (m + 1) * AUX, :]
        else:
            values = jnp.zeros((AUX, LANES), jnp.float32)
        values = jnp.round(values).astype(jnp.int32).astype(jnp.int16)
        if direct:
            out_refs[m][share:, :] = values
        else:
            out_refs[0][m, share:, :] = values


def pick_kernel(masks, info_ref, *refs):
    if len(refs) == 2:
        in_ref, out_ref = refs
        for m in range(out_ref.shape[0]):
            out_ref[m] = in_ref[info_ref[INFO + m]]
        return
    owners = len(refs) // 2
    *in_refs, all_ref = refs[:owners] + refs[-1:]
    out_refs = refs[owners:-1]
    me = info_ref[5]
    for i, k in enumerate(masks):
        all_ref[k] = in_refs[i][...]
    for i, k in enumerate(masks):
        out_refs[i][...] = all_ref[info_ref[INFO + (me ^ k)] ^ me]


def silu(v):
    return v / (1.0 + jnp.exp(-v))


def split(v):
    high = v.astype(jnp.bfloat16)
    low = (v - high.astype(jnp.float32)).astype(jnp.bfloat16)
    return high, low


def small_steps(seq_x, seq_b, wx_ref, bx_ref, wb_ref, bb_ref, steps):
    taps = len(seq_x) - steps + 1
    blocks = bx_ref.shape[0]
    xs, bs, cs = [], [], []
    for t in range(steps):
        total = bx_ref[...]
        pairs = bb_ref[...]
        for k in range(taps):
            total = total + wx_ref[k * blocks : (k + 1) * blocks, :] * seq_x[t + k]
            pairs = pairs + wb_ref[k] * seq_b[t + k]
        xs.append(silu(total))
        pairs = silu(pairs)
        turned = jnp.concatenate([pairs[:, LANES // 2 :], pairs[:, : LANES // 2]], 1)
        lower = lax.broadcasted_iota(jnp.int32, pairs.shape, 1) < LANES // 2
        bs.append(jnp.where(lower, pairs, turned))
        cs.append(jnp.where(lower, turned, pairs))
    return xs, bs, cs


def by_group(rows, count):
    groups = rows.shape[0]
    run = count // groups
    return jnp.concatenate(
        [jnp.broadcast_to(rows[g : g + 1], (run, rows.shape[1])) for g in range(groups)], 0
    )


def spread_x(xs, dec, dts, spread_ref):
    blocks = xs[0].shape[0]
    heads = 2 * blocks
    lower = lax.broadcasted_iota(jnp.int32, (blocks, LANES), 1) < LANES // 2
    later = None
    for t in reversed(range(len(xs))):
        weighted = xs[t] * dts[t]
        if later is not None:
            weighted = weighted * later
        later = dec[t] if later is None else later * dec[t]
        spread_ref[pl.ds(t * heads, blocks, stride=2), :] = jnp.where(lower, weighted, 0.0)
        spread_ref[pl.ds(t * heads + 1, blocks, stride=2), :] = jnp.where(lower, 0.0, weighted)
    return jnp.concatenate(split(spread_ref[...]), 1)


def new_state(tile, first, wide, spread, bs, place_ref, write):
    steps = len(bs)
    heads = wide.shape[0]
    b_rows = [by_group(b, heads) for b in bs]
    for j in range(0, P_SIZE * P_SIZE // LANES, 2):
        at = pl.ds(pl.multiple_of(first(j) * LANES, LANES), 2 * LANES)
        grown = jnp.dot(
            spread,
            jnp.concatenate([place_ref[:, at]] * (spread.shape[1] // P_SIZE), 0),
            preferred_element_type=jnp.float32,
        )
        for half in range(2):
            new = wide * tile(j + half)
            for t in range(steps):
                piece = grown[t * heads : (t + 1) * heads, half * LANES : (half + 1) * LANES]
                new = new + piece * b_rows[t]
            write(j + half, new)


def against_c(tile, first, cs, perm_ref, rows_ref):
    steps = len(cs)
    groups = cs[0].shape[0]
    lower = lax.broadcasted_iota(jnp.int32, (steps, LANES), 1) < LANES // 2
    lefts = []
    for g in range(groups):
        rows = jnp.concatenate([c[g : g + 1] for c in cs], 0)
        rows = jnp.concatenate([jnp.where(lower, rows, 0.0), jnp.where(lower, 0.0, rows)], 0)
        lefts.append(jnp.concatenate([jnp.concatenate([v, v], 1) for v in split(rows)], 0))
    count = P_SIZE * P_SIZE // LANES
    line = 2 * steps
    run = LANES // QUAD
    for u in range(0, count, 2 * QUAD):
        parts = [jnp.concatenate(split(tile(j)), 1) for j in range(u, u + 2 * QUAD)]
        for g in range(groups):
            right = jnp.concatenate([p[g * run : (g + 1) * run] for p in parts], 0)
            out = lax.dot_general(
                lefts[g], right, (((1,), (1,)), ((), ())), preferred_element_type=jnp.float32
            )
            out = out[:line] + out[line:]
            for w in range(2):
                quad = first(u + w * QUAD) // QUAD
                at = pl.ds(pl.multiple_of(g * (count // QUAD) * line + quad * line, 8), line)
                rows_ref[at, :] = out[:, w * LANES : (w + 1) * LANES]
    turned = jnp.transpose(rows_ref[...])
    lower = lax.broadcasted_iota(jnp.int32, (run, LANES), 1) < LANES // 2
    straight = [turned[i * run : (i + 1) * run] for i in range(QUAD)]
    rolled = [
        jnp.concatenate([v[:, LANES // 2 :], v[:, : LANES // 2]], 1) for v in straight
    ]
    low_group = [jnp.where(lower, straight[i], rolled[i + 1]) for i in range(0, QUAD, 2)]
    high_group = [jnp.where(lower, rolled[i], straight[i + 1]) for i in range(0, QUAD, 2)]
    values = jnp.concatenate(
        [jnp.concatenate(low_group, 1), jnp.concatenate(high_group, 1)], 0
    )
    high = values.astype(jnp.bfloat16)
    rest = values - high.astype(jnp.float32)
    middle = rest.astype(jnp.bfloat16)
    low = (rest - middle.astype(jnp.float32)).astype(jnp.bfloat16)
    heads = values.shape[0]
    out = jnp.dot(
        jnp.concatenate([high, middle, low], 0), perm_ref[...], preferred_element_type=jnp.float32
    )
    return out[:heads] + out[heads : 2 * heads] + out[2 * heads :]


def gated_steps(mixed, scale, xs, bs, cs, dec, dts, skip, gate, mixed_ref):
    steps = len(xs)
    heads = mixed.shape[0]
    blocks = heads // 2
    lower = lax.broadcasted_iota(jnp.int32, (blocks, LANES), 1) < LANES // 2
    for t in range(steps):
        part = mixed[:, t * LANES : (t + 1) * LANES]
        mixed_ref[t * heads : (t + 1) * heads, :] = part if scale is None else part * scale
    gated, sums = [], []
    ahead = None
    weights = []
    for t in range(steps):
        weights = [w * dec[t] for w in weights] + [dts[t]]
        ahead = dec[t] if ahead is None else ahead * dec[t]
        even = mixed_ref[pl.ds(t * heads, blocks, stride=2), :]
        odd = mixed_ref[pl.ds(t * heads + 1, blocks, stride=2), :]
        out = ahead * jnp.where(lower, even, odd) + skip * xs[t]
        for s in range(t + 1):
            inner = 0.5 * jnp.sum(bs[s] * cs[t], axis=1, keepdims=True)
            inner = by_group(jnp.broadcast_to(inner, (inner.shape[0], LANES)), blocks)
            out = out + weights[s] * inner * xs[s]
        out = out * gate[t]
        gated.append(out)
        squares = jnp.sum(jnp.sum(out * out, axis=0, keepdims=True), axis=1, keepdims=True)
        sums.append(jnp.broadcast_to(squares, (1, LANES)))
    return gated, sums


def prep_kernel(
    me_ref, counts_hbm, plan_hbm, x_hbm, z_hbm, wx_hbm, state_hbm, bc_ref, dt_ref, bias_ref,
    rate_ref, skip_ref,
    info_ref, xd_ref, gate_ref, dec_ref, dtd_ref, wide_ref, skipd_ref, wxd_ref, perm_ref,
    place_ref, kept_ref, cx_ref, cb_ref,
    counts_ref, plan_ref, x_ref, z_ref, wx_ref, sems,
):
    slots, steps, channels = x_ref.shape
    heads = dt_ref.shape[2]
    blocks = channels // LANES
    taps = cx_ref.shape[0]
    me = me_ref[0]
    copies = [
        pltpu.make_async_copy(src, dst, sems.at[i])
        for i, (src, dst) in enumerate(
            (
                (counts_hbm, counts_ref), (plan_hbm, plan_ref), (x_hbm, x_ref), (z_hbm, z_ref),
                (wx_hbm, wx_ref),
            )
        )
    ]
    for copy in copies:
        copy.start()
    copies[0].wait()
    copies[1].wait()
    reqs = plan_ref.shape[0]
    owners = counts_ref.shape[0]
    for d in range(owners):
        info_ref[INFO + d] = 0

    def look(r, carry):
        kept_to, kept_from, has_kept, moved_to, has_moved = carry
        home, local = r // slots, r % slots
        goal = plan_ref[r]
        live = local < counts_ref[home]
        owner, place = goal // slots, goal % slots
        mine = live & (owner == me)
        own = mine & (home == me)
        into = mine & (home != me)

        @pl.when(live & (owner != home))
        def _():
            info_ref[INFO + owner] = home

        return (
            jnp.where(own, place, kept_to), jnp.where(own, local, kept_from),
            jnp.where(own, 1, has_kept), jnp.where(into, place, moved_to),
            jnp.where(into, 1, has_moved),
        )

    carry = (jnp.int32(0),) * 5
    if reqs <= 32:
        for r in range(reqs):
            carry = look(r, carry)
    else:
        carry = lax.fori_loop(0, reqs, look, carry)
    kept_to, kept_from, has_kept, moved_to, has_moved = carry
    moved_to = jnp.where(has_moved > 0, moved_to, jnp.where(has_kept > 0, 1 - kept_to, 0))
    kept_to = 1 - moved_to
    for i, v in enumerate((kept_to, kept_from, has_kept, moved_to, has_moved, me)):
        info_ref[i] = v
    copies += copy_rows(state_hbm.at[kept_from], kept_ref, sems, len(copies), COPIES)
    shape = perm_ref.shape
    line = lax.broadcasted_iota(jnp.int32, shape, 0)
    lane = lax.broadcasted_iota(jnp.int32, shape, 1)
    span = shape[0] // QUAD
    p = (line % span // (2 * steps) * QUAD + line // span) * 2 + line % (2 * steps) // steps
    hit = (lane // LANES == line % steps) & (lane % P_SIZE == p)
    perm_ref[...] = jnp.where(hit, 1.0, 0.0).astype(jnp.bfloat16)
    shape = place_ref.shape
    line = lax.broadcasted_iota(jnp.int32, shape, 0)
    lane = lax.broadcasted_iota(jnp.int32, shape, 1)
    place_ref[...] = jnp.where(lane // P_SIZE == line, 1.0, 0.0).astype(jnp.bfloat16)
    rate = jnp.exp(rate_ref[...])
    raw = [dt_ref[s] + bias_ref[...] for s in range(slots)]
    delta = [jnp.maximum(v, 0.0) + jnp.log1p(jnp.exp(-jnp.abs(v))) for v in raw]
    decay = [jnp.exp(-v * rate) for v in delta]
    at = lax.broadcasted_iota(jnp.int32, (blocks, heads), 0)
    of = lax.broadcasted_iota(jnp.int32, (blocks, heads), 1)
    lines = [v[t : t + 1] for v in delta + decay for t in range(steps)] + [skip_ref[...]]
    spread = jnp.concatenate([jnp.where(of // 2 == at, line, 0.0) for line in lines], 0)
    high = spread.astype(jnp.bfloat16)
    rest = spread - high.astype(jnp.float32)
    middle = rest.astype(jnp.bfloat16)
    low = (rest - middle.astype(jnp.float32)).astype(jnp.bfloat16)
    head = lax.broadcasted_iota(jnp.int32, (heads, LANES), 0)
    lane = lax.broadcasted_iota(jnp.int32, (heads, LANES), 1)
    chosen = jnp.where(head % 2 == lane // (LANES // 2), 1.0, 0.0).astype(jnp.bfloat16)
    out = jnp.dot(high, chosen, preferred_element_type=jnp.float32)
    out = out + jnp.dot(middle, chosen, preferred_element_type=jnp.float32)
    out = out + jnp.dot(low, chosen, preferred_element_type=jnp.float32)
    run = steps * blocks
    for s in range(slots):
        dtd_ref[s] = out[s * run : (s + 1) * run]
        dec_ref[s] = out[(slots + s) * run : (slots + s + 1) * run]
        total = decay[s][:1]
        for t in range(1, steps):
            total = total * decay[s][t : t + 1]
        total = jnp.concatenate([total, total], 1)
        wide = jnp.sum(jnp.where(head == lane, total, 0.0), axis=1, keepdims=True)
        wide_ref[s] = jnp.broadcast_to(wide, (heads, LANES))
    skipd_ref[...] = out[2 * slots * run :]
    for copy in copies[2:5]:
        copy.wait()
    x = [x_ref[s].astype(jnp.float32) for s in range(slots)]
    for s in range(slots):
        dense_rows(xd_ref.at[s], 0, x[s])
        dense_rows(gate_ref.at[s], 0, z_ref[s].astype(jnp.float32))
    dense_rows(wxd_ref, 0, wx_ref[...])
    gate_ref[...] = silu(gate_ref[...])
    full = [jnp.where(kept_to == s, has_kept, has_moved) > 0 for s in range(slots)]
    for k in range(taps):
        t = steps - taps + k
        rows = [jnp.where(full[s], x[s][t : t + 1], 0.0) for s in range(slots)]
        cx_ref[k] = jnp.concatenate(rows, 0).astype(jnp.bfloat16)
        for s in range(slots):
            pairs = bc_ref[s, t].astype(jnp.float32)
            cb_ref[s, k] = jnp.where(full[s], pairs, 0.0).astype(jnp.bfloat16)
    for copy in copies[5:]:
        copy.wait()


def slot_inputs(slot, steps, x_ref, bc_ref, gate_ref, dec_ref, dt_ref):
    blocks = x_ref.shape[1] // steps
    rows = [pl.ds(t * blocks, blocks) for t in range(steps)]
    return [[ref[slot, r, :] for r in rows] for ref in (x_ref, gate_ref, dec_ref, dt_ref)] + [
        [bc_ref[slot, t].astype(jnp.float32) for t in range(steps)]
    ]


def kept_kernel(
    info_ref, state_ref, cx_ref, cb_ref, x_ref, bc_ref, gate_ref, dec_ref, dt_ref, skip_ref,
    wx_ref, bx_ref, wb_ref, bb_ref, perm_ref, wide_ref, place_ref,
    out_hbm, gated_ref, sums_ref, spread_ref, mixed_ref, turn_ref, rows_ref, new_ref, sems,
):
    steps = bc_ref.shape[1]
    blocks = bx_ref.shape[0]
    taps = cx_ref.shape[0]
    slot, origin, full = info_ref[0], info_ref[1], info_ref[2] > 0
    cx = cx_ref[...].astype(jnp.float32)
    dense_rows(rows_ref, 0, jnp.where(origin == 0, cx[:, 0], cx[:, 1]))
    cb = of_slot(cb_ref[...].astype(jnp.float32), origin)
    new_x, gate, dec, dts, new_b = slot_inputs(
        slot, steps, x_ref, bc_ref, gate_ref, dec_ref, dt_ref
    )
    seq_x = [rows_ref[k * blocks : (k + 1) * blocks, :] for k in range(taps)] + new_x
    seq_b = [cb[k] for k in range(taps)] + new_b
    xs, bs, cs = small_steps(seq_x, seq_b, wx_ref, bx_ref, wb_ref, bb_ref, steps)

    def write(j, new):
        new_ref[:, j * LANES : (j + 1) * LANES] = jnp.where(full, new, 0.0)

    def tile(j):
        return state_ref[:, j * LANES : (j + 1) * LANES]

    mixed = against_c(tile, lambda j: j, cs, perm_ref, turn_ref)
    gated, sums = gated_steps(
        mixed, None, xs, bs, cs, dec, dts, skip_ref[...], gate, mixed_ref
    )
    spread = spread_x(xs, dec, dts, spread_ref)
    new_state(tile, lambda j: j, wide_ref[slot], spread, bs, place_ref, write)
    copies = copy_rows(new_ref, out_hbm.at[slot], sems, 0, COPIES)
    for t in range(steps):
        gated_ref[t] = gated[t]
    sums_ref[...] = jnp.concatenate(sums, 0)
    for copy in copies:
        copy.wait()


def piece_tiles(masks, me, got_refs, heads):
    direct = len(masks) > 1
    share = got_refs[0].shape[-2] - AUX
    run = min(share, heads)
    each = share // heads

    def load(m, rows):
        part = got_refs[m][rows, :] if direct else got_refs[0][m, rows, :]
        return part.astype(jnp.int32).astype(jnp.float32)

    def tile(j):
        if direct:
            return load(j // each, pl.ds(j % each * heads, heads))
        flats = range(j * heads, (j + 1) * heads, run)
        return jnp.concatenate([load(f // share, pl.ds(f % share, run)) for f in flats], 0)

    def first(j):
        return (me ^ masks[j // each]) * each + j % each if direct else j

    return load, tile, first


def moved_kernel(masks, info_ref, *refs):
    pieces = len(masks)
    got_refs = refs[:pieces]
    (
        kept_sums_ref, x_ref, bc_ref, gate_ref, dec_ref, dt_ref, skip_ref,
        wx_ref, bx_ref, wb_ref, bb_ref, perm_ref, wide_ref,
        gated_ref, sums_ref, spread_ref, b_ref, wide_out_ref, rows_ref, mixed_ref, turn_ref, aux_ref,
    ) = refs[pieces:]
    direct = pieces > 1
    steps, groups = bc_ref.shape[1:3]
    blocks = bx_ref.shape[0]
    taps = wx_ref.shape[0] // blocks - 1
    heads = wide_ref.shape[1]
    share = got_refs[0].shape[-2] - AUX
    slot, me = info_ref[3], info_ref[5]
    new_x, gate, dec, dts, new_b = slot_inputs(
        slot, steps, x_ref, bc_ref, gate_ref, dec_ref, dt_ref
    )
    load, tile, first = piece_tiles(masks, me, got_refs, heads)
    for m in range(pieces if direct else got_refs[0].shape[0]):
        if direct:
            at = pl.ds(pl.multiple_of((me ^ masks[m]) * AUX, AUX), AUX)
            aux_ref[at, :] = load(m, pl.ds(share, AUX))
        elif m * AUX < aux_ref.shape[0]:
            aux_ref[m * AUX : (m + 1) * AUX, :] = load(m, pl.ds(share, AUX))

    last = aux_ref[taps * blocks : taps * blocks + AUX, :]
    codes = last[taps * groups : taps * groups + 1]
    row = lax.broadcasted_iota(jnp.int32, (heads, LANES), 0)
    lane = lax.broadcasted_iota(jnp.int32, (heads, LANES), 1)
    code = jnp.sum(jnp.where(row == lane, codes, 0.0), axis=1, keepdims=True)
    scale = level_scale(code) * (1.0 / LEVELS)
    scale_x = level_scale(codes[:, heads : heads + 1]) * (1.0 / LEVELS)
    scale_b = level_scale(codes[:, heads + 1 : heads + 2]) * (1.0 / LEVELS)
    seq_x = [aux_ref[k * blocks : (k + 1) * blocks, :] * scale_x for k in range(taps)] + new_x
    seq_b = [last[k * groups : (k + 1) * groups] * scale_b for k in range(taps)] + new_b
    xs, bs, cs = small_steps(seq_x, seq_b, wx_ref, bx_ref, wb_ref, bb_ref, steps)
    mixed = against_c(tile, first, cs, perm_ref, turn_ref)
    gated, sums = gated_steps(
        mixed, scale, xs, bs, cs, dec, dts, skip_ref[...], gate, mixed_ref
    )
    for t in range(steps):
        gated_ref[t] = gated[t]
        b_ref[t] = bs[t]
    sums_ref[...] = jnp.concatenate([kept_sums_ref[...]] + sums, 0)
    spread_ref[...] = spread_x(xs, dec, dts, rows_ref)
    wide_out_ref[...] = wide_ref[slot] * scale


def state_kernel(masks, info_ref, *refs):
    pieces = len(masks)
    got_refs = refs[:pieces]
    (
        spread_ref, b_ref, wide_ref, place_ref, kept_ref, moved_ref, norm_ref,
        new_ref, ready_ref, rows_ref,
    ) = refs[pieces:]
    full, me = info_ref[4] > 0, info_ref[5]
    _, tile, first = piece_tiles(masks, me, got_refs, wide_ref.shape[0])

    def write(j, new):
        at = pl.ds(pl.multiple_of(first(j) * LANES, LANES), LANES)
        new_ref[:, at] = jnp.where(full, new, 0.0)

    bs = [b_ref[t] for t in range(b_ref.shape[0])]
    new_state(tile, first, wide_ref[...], spread_ref[...], bs, place_ref, write)
    steps, blocks = kept_ref.shape[:2]
    for which, ref in enumerate((kept_ref, moved_ref)):
        for t in range(steps):
            rows_ref[t * blocks : (t + 1) * blocks, :] = ref[t] * norm_ref[...]
        for b in range(blocks):
            ready_ref[which, :, b * LANES : (b + 1) * LANES] = rows_ref[
                pl.ds(b, steps, stride=blocks), :
            ]


def norm_kernel(
    info_ref, held_hbm, new_ref, ready_ref, mine_ref, theirs_ref, out_hbm, y_hbm, y_ref, sems
):
    del held_hbm
    copies = copy_rows(new_ref, out_hbm.at[info_ref[3]], sems, 0, COPIES)
    steps = ready_ref.shape[1]
    factor = lax.rsqrt((mine_ref[...] + theirs_ref[...]) * (1.0 / (H * P_SIZE)) + 1e-05)
    for which in range(ready_ref.shape[0]):
        full = info_ref[2 + 2 * which] > 0
        rows = factor[which * steps : (which + 1) * steps]
        for b in range(0, ready_ref.shape[2], LANES):
            values = jnp.where(full, ready_ref[which, :, b : b + LANES] * rows, 0.0)
            y_ref[info_ref[3 * which], :, b : b + LANES] = values.astype(jnp.bfloat16)
    copies.append(pltpu.make_async_copy(y_ref, y_hbm, sems.at[COPIES]))
    copies[-1].start()
    for copy in copies:
        copy.wait()


def partner_masks(owners):
    gray = [i ^ (i >> 1) for i in range(owners)]
    near, far = gray[1 : owners // 2], gray[owners // 2 :]
    order = [0]
    for i, k in enumerate(far):
        order += [k, *near[i : i + 1]]
    return tuple(order)


def on_device(
    counts,
    move_plan,
    ssm_state,
    conv_x_state,
    conv_bc_state,
    x_in,
    bc_in,
    z_in,
    dt_in,
    conv_w_x,
    conv_b_x,
    conv_w_bc,
    conv_b_bc,
    dt_bias,
    a_log,
    d_skip,
    norm_w,
):
    owners = lax.axis_size("req")
    owner = lax.axis_index("req").astype(jnp.int32)
    slots, heads, columns = ssm_state.shape
    places, steps, channels = x_in.shape
    taps = conv_x_state.shape[1]
    groups, pair = conv_bc_state.shape[2:]
    blocks = channels // LANES
    share = heads * columns // LANES // owners
    aux_rows = taps * blocks + AUX
    f32 = jnp.float32
    direct = owners <= 16 and owners & (owners - 1) == 0 and share % (QUAD * heads) == 0
    masks = partner_masks(owners) if direct else (0,)
    pieces = len(masks)
    smem = pl.BlockSpec(memory_space=pltpu.SMEM)
    vmem = pl.BlockSpec(memory_space=pltpu.VMEM)
    anywhere = pl.BlockSpec(memory_space=pl.ANY)

    def shaped(*shape, dtype=f32):
        return jax.ShapeDtypeStruct(shape, dtype)

    def call(kernel, name, in_specs, out_specs, out_shape, scratch=(), **more):
        return pl.pallas_call(
            kernel,
            in_specs=in_specs,
            out_specs=out_specs,
            out_shape=out_shape,
            scratch_shapes=scratch,
            compiler_params=pltpu.CompilerParams(vmem_limit_bytes=VMEM_LIMIT),
            name=name,
            **more,
        )

    def in_hbm(*values):
        return [pltpu.with_memory_space_constraint(v, pltpu.MemorySpace.HBM) for v in values]

    me = owner.reshape(1)
    conv_x_taps = jnp.transpose(conv_x_state, (1, 0, 2))
    piece = (share + AUX, LANES) if direct else (owners, share + AUX, LANES)
    sent = [shaped(*piece, dtype=jnp.int16)] * pieces
    payload = call(
        functools.partial(pack_kernel, masks), "pack", [smem] + [anywhere] * 5, [vmem] * pieces, sent,
        [
            pltpu.SMEM(counts.shape, jnp.int32),
            pltpu.SMEM(move_plan.shape, jnp.int32),
            pltpu.VMEM(ssm_state.shape, f32),
            pltpu.VMEM(conv_x_taps.shape, jnp.bfloat16),
            pltpu.VMEM(conv_bc_state.shape, jnp.bfloat16),
            pltpu.VMEM((max(aux_rows, pieces * AUX), LANES), f32),
            pltpu.SemaphoreType.DMA((4 + slots * heads // BLOCK,)),
        ],
    )(me, *in_hbm(counts, move_plan, ssm_state, conv_x_taps, conv_bc_state))

    def exchange(values):
        if not direct:
            return [lax.all_to_all(values[0], "req", split_axis=0, concat_axis=0, tiled=True)]
        out = list(values)
        for i, k in enumerate(masks):
            if k:
                out[i] = lax.ppermute(values[i], "req", [(o, o ^ k) for o in range(owners)])
        return out

    spread = exchange(payload)

    (
        _, me_late, cx_late, cb_late, bc_late, dt_late, bias_late, rate_late, skip_late,
        bx_late, wb_late, bb_late, norm_late,
    ) = lax.optimization_barrier(
        (
            payload[0], me, conv_x_taps, conv_bc_state, bc_in, dt_in, dt_bias, a_log, d_skip,
            conv_b_x, conv_w_bc, conv_b_bc, norm_w,
        )
    )
    rows = (places, steps * blocks, LANES)
    info, x_dense, gate, dec, dt_dense, wide, skip, wx, perm, place, kept_state, *convs = call(
        prep_kernel, "prep", [smem] + [anywhere] * 6 + [vmem] * 5, [smem] + [vmem] * 12,
        [
            shaped(INFO + owners, dtype=jnp.int32), shaped(*rows), shaped(*rows), shaped(*rows),
            shaped(*rows), shaped(places, heads, LANES), shaped(blocks, LANES),
            shaped((taps + 1) * blocks, LANES),
            shaped(QUAD * P_SIZE, 2 * steps * P_SIZE, dtype=jnp.bfloat16),
            shaped(P_SIZE, columns, dtype=jnp.bfloat16), shaped(heads, columns),
            shaped(taps, places, channels, dtype=jnp.bfloat16),
            shaped(*conv_bc_state.shape, dtype=jnp.bfloat16),
        ],
        [
            pltpu.SMEM(counts.shape, jnp.int32),
            pltpu.SMEM(move_plan.shape, jnp.int32),
            pltpu.VMEM(x_in.shape, jnp.bfloat16),
            pltpu.VMEM(z_in.shape, jnp.bfloat16),
            pltpu.VMEM(conv_w_x.shape, f32),
            pltpu.SemaphoreType.DMA((5 + COPIES,)),
        ],
    )(
        me_late, *in_hbm(counts, move_plan, x_in, z_in, conv_w_x, ssm_state), bc_late,
        dt_late, bias_late.reshape(1, -1), rate_late.reshape(1, -1), skip_late.reshape(1, -1),
    )

    picked = call(
        functools.partial(pick_kernel, masks), "pick", [smem] + [vmem] * pieces, [vmem] * pieces, sent,
        [pltpu.VMEM((owners, *piece), jnp.int16)] if direct else [],
    )(info, *spread)
    got = exchange(picked)

    _, info = lax.optimization_barrier((picked[0], info))
    common = [x_dense, bc_late, gate, dec, dt_dense, skip, wx]
    common += [bx_late.reshape(blocks, LANES), wb_late, bb_late, perm, wide]
    scratch = [pltpu.VMEM((steps * heads, LANES), f32)] * 2 + [pltpu.VMEM((LANES, LANES), f32)]
    held, kept_gated, kept_sums = call(
        kept_kernel, "kept", [smem] + [vmem] * (4 + len(common)), [anywhere, vmem, vmem],
        [shaped(places, heads, columns), shaped(steps, blocks, LANES), shaped(steps, LANES)],
        scratch
        + [
            pltpu.VMEM((taps * blocks, LANES), f32),
            pltpu.VMEM((heads, columns), f32),
            pltpu.SemaphoreType.DMA((COPIES,)),
        ],
    )(info, kept_state, cx_late, cb_late, *common, place)
    moved_gated, sums, spread_rows, b_steps, wide_scaled = call(
        functools.partial(moved_kernel, masks), "moved",
        [smem] + [vmem] * (pieces + 1 + len(common)), [vmem] * 5,
        [
            shaped(steps, blocks, LANES), shaped(2 * steps, LANES),
            shaped(steps * heads, 2 * LANES, dtype=jnp.bfloat16),
            shaped(steps, groups, pair), shaped(heads, LANES),
        ],
        scratch + [pltpu.VMEM((max(aux_rows, pieces * AUX), LANES), f32)],
    )(info, *got, kept_sums, *common)
    theirs = lax.ppermute(sums, "tp", [(0, 1), (1, 0)])
    new, ready = call(
        functools.partial(state_kernel, masks), "state",
        [smem] + [vmem] * (pieces + 7), [vmem] * 2,
        [shaped(heads, columns), shaped(places, steps, channels)],
        [pltpu.VMEM((steps * blocks, LANES), f32)],
    )(
        info, *got, spread_rows, b_steps, wide_scaled, place, kept_gated, moved_gated,
        norm_late.reshape(blocks, LANES),
    )
    new_ssm, y_out = call(
        norm_kernel, "norm", [smem, anywhere] + [vmem] * 4, [anywhere, anywhere],
        [
            shaped(places, heads, columns),
            shaped(places, steps, channels, dtype=jnp.bfloat16),
        ],
        [
            pltpu.VMEM((places, steps, channels), jnp.bfloat16),
            pltpu.SemaphoreType.DMA((COPIES + 1,)),
        ],
        input_output_aliases={1: 0},
    )(info, held, new, ready, sums, theirs)
    return (y_out, new_ssm, jnp.transpose(convs[0], (1, 0, 2)), convs[1])


def solution(mesh):
    in_specs = (
        P("parts"),
        P("parts"),
        P(("parts", "req"), "tp", None),
        P(("parts", "req"), None, "tp"),
        P(("parts", "req"), None, "tp", None),
        P(("parts", "req"), None, "tp"),
        P(("parts", "req"), None, "tp", None),
        P(("parts", "req"), None, "tp"),
        P(("parts", "req"), None, "tp"),
        P(None, "tp"),
        P("tp"),
        P(None, "tp", None),
        P("tp", None),
        P("tp"),
        P("tp"),
        P("tp"),
        P("tp"),
    )
    out_specs = (
        P(("parts", "req"), None, "tp"),
        P(("parts", "req"), "tp", None),
        P(("parts", "req"), None, "tp"),
        P(("parts", "req"), None, "tp", None),
    )
    return jax.shard_map(
        on_device, mesh=mesh, in_specs=in_specs, out_specs=out_specs, check_vma=False
    )
```

```python
import functools

import jax
import jax.numpy as jnp
from jax import lax
from jax.experimental import pallas as pl
from jax.experimental.pallas import tpu as pltpu
from jax.sharding import PartitionSpec as P

H = 128
P_SIZE = 64
LANES = 128
AUX = 16
BLOCK = 16
QUAD = 4
COPIES = 8
INFO = 8
REACH = 6.0
LEVELS = 32767.0
VMEM_LIMIT = 48 * 1024 * 1024


def level_code(top):
    code = jnp.floor(-8.0 / jnp.log(2.0) * jnp.log(jnp.maximum(top, 1e-30) / REACH) - 0.01)
    return jnp.clip(code, 0.0, 800.0)


def level_scale(code):
    return REACH * jnp.exp(code * (-0.125 * jnp.log(2.0)))


def moving_slot(counts_ref, plan_ref, me, slots):
    slot = jnp.int32(0)
    for local in range(1, slots):
        live = local < counts_ref[me]
        away = plan_ref[me * slots + local] // slots != me
        slot = jnp.where(live & away, local, slot)
    return slot


def dense_rows(rows_ref, at, values):
    count, channels = values.shape
    blocks = channels // LANES
    for b in range(blocks):
        part = values[:, b * LANES : (b + 1) * LANES]
        if count == 1:
            rows_ref[at + b : at + b + 1, :] = part
        else:
            rows_ref[pl.ds(at + b, count, stride=blocks), :] = part


def copy_rows(src, dst, sems, at, count):
    run = dst.shape[0] // count
    copies = []
    for i in range(count):
        rows = pl.ds(i * run, run)
        copies.append(pltpu.make_async_copy(src.at[rows], dst.at[rows], sems.at[at + i]))
        copies[-1].start()
    return copies


def of_slot(values, slot):
    return jnp.where(slot == 0, values[0], values[1])


def pack_kernel(masks, me_ref, counts_hbm, plan_hbm, state_hbm, cx_ref, cb_ref, *refs):
    *out_refs, counts_ref, plan_ref, state_ref, rows_ref, sems = refs
    direct = len(out_refs) > 1
    slots, heads, columns = state_ref.shape
    owners = len(out_refs) if direct else out_refs[0].shape[0]
    share = out_refs[0].shape[-2] - AUX
    run = min(share, BLOCK)
    each = share // heads
    me = me_ref[0]
    small = [
        pltpu.make_async_copy(src, dst, sems.at[i])
        for i, (src, dst) in enumerate(
            ((counts_hbm, counts_ref), (plan_hbm, plan_ref))
        )
    ]
    for copy in small:
        copy.start()
    large = []
    for at in range(0, heads, BLOCK):
        for slot in range(slots):
            part = (slot, pl.ds(at, BLOCK))
            copy = pltpu.make_async_copy(
                state_hbm.at[part], state_ref.at[part], sems.at[len(small) + len(large)]
            )
            copy.start()
            large.append(copy)
    small[0].wait()
    small[1].wait()
    slot = moving_slot(counts_ref, plan_ref, me, slots)
    taps, _, channels = cx_ref.shape
    groups = cb_ref.shape[2]
    blocks = channels // LANES
    cx = cx_ref[...].astype(jnp.float32)
    cx = jnp.where(slot == 0, cx[:, 0], cx[:, 1])
    cb = of_slot(cb_ref[...].astype(jnp.float32), slot)
    code_x = level_code(jnp.max(jnp.abs(cx)).reshape(1, 1))
    code_b = level_code(jnp.max(jnp.abs(cb)).reshape(1, 1))
    dense_rows(rows_ref, 0, cx)
    last = taps * blocks
    rows_ref[last:, :] = jnp.zeros((rows_ref.shape[0] - last, LANES), jnp.float32)
    for k in range(taps):
        rows_ref[last + k * groups : last + (k + 1) * groups, :] = cb[k]
    lane = lax.broadcasted_iota(jnp.int32, (BLOCK, LANES), 1)
    row = lax.broadcasted_iota(jnp.int32, (BLOCK, LANES), 0)
    codes = jnp.where(lane[:1] == heads, code_x, 0.0)
    codes = jnp.where(lane[:1] == heads + 1, code_b, codes)
    for q in range(heads // BLOCK):
        for copy in large[q * slots : (q + 1) * slots]:
            copy.wait()
        at = q * BLOCK
        top = jnp.abs(state_ref[slot, at : at + BLOCK, :LANES])
        for j in range(1, columns // LANES):
            tile = state_ref[slot, at : at + BLOCK, j * LANES : (j + 1) * LANES]
            top = jnp.maximum(top, jnp.abs(tile))
        code = level_code(jnp.max(top, axis=1, keepdims=True))
        codes = codes + jnp.sum(jnp.where(row + at == lane, code, 0.0), axis=0, keepdims=True)
        factor = jnp.broadcast_to(LEVELS / level_scale(code), (BLOCK, LANES))
        for j in range(columns // LANES):
            place = (me ^ masks[j // each]) * each + j % each if direct else j
            lanes = pl.ds(pl.multiple_of(place * LANES, LANES), LANES)
            tile = state_ref[slot, at : at + BLOCK, lanes] * factor
            tile = jnp.round(tile).astype(jnp.int32).astype(jnp.int16)
            for part in range(0, BLOCK, run):
                flat = j * heads + at + part
                rows = pl.ds(flat % share, run)
                if direct:
                    out_refs[flat // share][rows, :] = tile[part : part + run]
                else:
                    out_refs[0][flat // share, rows, :] = tile[part : part + run]
    factor_x = LEVELS / level_scale(code_x)
    factor_b = LEVELS / level_scale(code_b)
    line = lax.broadcasted_iota(jnp.int32, (AUX, LANES), 0)
    rows_ref[:last, :] = rows_ref[:last, :] * factor_x
    values = rows_ref[last : last + AUX, :] * factor_b
    rows_ref[last : last + AUX, :] = jnp.where(line == taps * groups, codes, values)
    for m in range(owners):
        if direct:
            values = rows_ref[pl.ds(pl.multiple_of((me ^ masks[m]) * AUX, AUX), AUX), :]
        elif m * AUX < last + AUX:
            values = rows_ref[m * AUX : (m + 1) * AUX, :]
        else:
            values = jnp.zeros((AUX, LANES), jnp.float32)
        values = jnp.round(values).astype(jnp.int32).astype(jnp.int16)
        if direct:
            out_refs[m][share:, :] = values
        else:
            out_refs[0][m, share:, :] = values


def pick_kernel(masks, info_ref, *refs):
    if len(refs) == 2:
        in_ref, out_ref = refs
        for m in range(out_ref.shape[0]):
            out_ref[m] = in_ref[info_ref[INFO + m]]
        return
    owners = len(refs) // 2
    *in_refs, all_ref = refs[:owners] + refs[-1:]
    out_refs = refs[owners:-1]
    me = info_ref[5]
    for i, k in enumerate(masks):
        all_ref[k] = in_refs[i][...]
    for i, k in enumerate(masks):
        out_refs[i][...] = all_ref[info_ref[INFO + (me ^ k)] ^ me]


def silu(v):
    return v / (1.0 + jnp.exp(-v))


def split(v):
    high = v.astype(jnp.bfloat16)
    low = (v - high.astype(jnp.float32)).astype(jnp.bfloat16)
    return high, low


def small_steps(seq_x, seq_b, wx_ref, bx_ref, wb_ref, bb_ref, steps):
    taps = len(seq_x) - steps + 1
    blocks = bx_ref.shape[0]
    xs, bs, cs = [], [], []
    for t in range(steps):
        total = bx_ref[...]
        pairs = bb_ref[...]
        for k in range(taps):
            total = total + wx_ref[k * blocks : (k + 1) * blocks, :] * seq_x[t + k]
            pairs = pairs + wb_ref[k] * seq_b[t + k]
        xs.append(silu(total))
        pairs = silu(pairs)
        turned = jnp.concatenate([pairs[:, LANES // 2 :], pairs[:, : LANES // 2]], 1)
        lower = lax.broadcasted_iota(jnp.int32, pairs.shape, 1) < LANES // 2
        bs.append(jnp.where(lower, pairs, turned))
        cs.append(jnp.where(lower, turned, pairs))
    return xs, bs, cs


def by_group(rows, count):
    groups = rows.shape[0]
    run = count // groups
    return jnp.concatenate(
        [jnp.broadcast_to(rows[g : g + 1], (run, rows.shape[1])) for g in range(groups)], 0
    )


def spread_x(xs, dec, dts, spread_ref):
    blocks = xs[0].shape[0]
    heads = 2 * blocks
    lower = lax.broadcasted_iota(jnp.int32, (blocks, LANES), 1) < LANES // 2
    later = None
    for t in reversed(range(len(xs))):
        weighted = xs[t] * dts[t]
        if later is not None:
            weighted = weighted * later
        later = dec[t] if later is None else later * dec[t]
        spread_ref[pl.ds(t * heads, blocks, stride=2), :] = jnp.where(lower, weighted, 0.0)
        spread_ref[pl.ds(t * heads + 1, blocks, stride=2), :] = jnp.where(lower, 0.0, weighted)
    return jnp.concatenate(split(spread_ref[...]), 1)


def new_state(tile, first, wide, spread, bs, place_ref, write):
    steps = len(bs)
    heads = wide.shape[0]
    b_rows = [by_group(b, heads) for b in bs]
    for j in range(0, P_SIZE * P_SIZE // LANES, 2):
        at = pl.ds(pl.multiple_of(first(j) * LANES, LANES), 2 * LANES)
        grown = jnp.dot(
            spread,
            jnp.concatenate([place_ref[:, at]] * (spread.shape[1] // P_SIZE), 0),
            preferred_element_type=jnp.float32,
        )
        for half in range(2):
            new = wide * tile(j + half)
            for t in range(steps):
                piece = grown[t * heads : (t + 1) * heads, half * LANES : (half + 1) * LANES]
                new = new + piece * b_rows[t]
            write(j + half, new)


def against_c(tile, first, cs, perm_ref, rows_ref):
    steps = len(cs)
    groups = cs[0].shape[0]
    lower = lax.broadcasted_iota(jnp.int32, (steps, LANES), 1) < LANES // 2
    lefts = []
    for g in range(groups):
        rows = jnp.concatenate([c[g : g + 1] for c in cs], 0)
        rows = jnp.concatenate([jnp.where(lower, rows, 0.0), jnp.where(lower, 0.0, rows)], 0)
        lefts.append(jnp.concatenate([jnp.concatenate([v, v], 1) for v in split(rows)], 0))
    count = P_SIZE * P_SIZE // LANES
    line = 2 * steps
    run = LANES // QUAD
    for u in range(0, count, 2 * QUAD):
        parts = [jnp.concatenate(split(tile(j)), 1) for j in range(u, u + 2 * QUAD)]
        for g in range(groups):
            right = jnp.concatenate([p[g * run : (g + 1) * run] for p in parts], 0)
            out = lax.dot_general(
                lefts[g], right, (((1,), (1,)), ((), ())), preferred_element_type=jnp.float32
            )
            out = out[:line] + out[line:]
            for w in range(2):
                quad = first(u + w * QUAD) // QUAD
                at = pl.ds(pl.multiple_of(g * (count // QUAD) * line + quad * line, 8), line)
                rows_ref[at, :] = out[:, w * LANES : (w + 1) * LANES]
    turned = jnp.transpose(rows_ref[...])
    lower = lax.broadcasted_iota(jnp.int32, (run, LANES), 1) < LANES // 2
    straight = [turned[i * run : (i + 1) * run] for i in range(QUAD)]
    rolled = [
        jnp.concatenate([v[:, LANES // 2 :], v[:, : LANES // 2]], 1) for v in straight
    ]
    low_group = [jnp.where(lower, straight[i], rolled[i + 1]) for i in range(0, QUAD, 2)]
    high_group = [jnp.where(lower, rolled[i], straight[i + 1]) for i in range(0, QUAD, 2)]
    values = jnp.concatenate(
        [jnp.concatenate(low_group, 1), jnp.concatenate(high_group, 1)], 0
    )
    high = values.astype(jnp.bfloat16)
    rest = values - high.astype(jnp.float32)
    middle = rest.astype(jnp.bfloat16)
    low = (rest - middle.astype(jnp.float32)).astype(jnp.bfloat16)
    heads = values.shape[0]
    out = jnp.dot(
        jnp.concatenate([high, middle, low], 0), perm_ref[...], preferred_element_type=jnp.float32
    )
    return out[:heads] + out[heads : 2 * heads] + out[2 * heads :]


def gated_steps(mixed, scale, xs, bs, cs, dec, dts, skip, gate, mixed_ref):
    steps = len(xs)
    heads = mixed.shape[0]
    blocks = heads // 2
    lower = lax.broadcasted_iota(jnp.int32, (blocks, LANES), 1) < LANES // 2
    for t in range(steps):
        part = mixed[:, t * LANES : (t + 1) * LANES]
        mixed_ref[t * heads : (t + 1) * heads, :] = part if scale is None else part * scale
    gated, sums = [], []
    ahead = None
    weights = []
    for t in range(steps):
        weights = [w * dec[t] for w in weights] + [dts[t]]
        ahead = dec[t] if ahead is None else ahead * dec[t]
        even = mixed_ref[pl.ds(t * heads, blocks, stride=2), :]
        odd = mixed_ref[pl.ds(t * heads + 1, blocks, stride=2), :]
        out = ahead * jnp.where(lower, even, odd) + skip * xs[t]
        for s in range(t + 1):
            inner = 0.5 * jnp.sum(bs[s] * cs[t], axis=1, keepdims=True)
            inner = by_group(jnp.broadcast_to(inner, (inner.shape[0], LANES)), blocks)
            out = out + weights[s] * inner * xs[s]
        out = out * gate[t]
        gated.append(out)
        squares = jnp.sum(jnp.sum(out * out, axis=0, keepdims=True), axis=1, keepdims=True)
        sums.append(jnp.broadcast_to(squares, (1, LANES)))
    return gated, sums


def prep_kernel(
    me_ref, counts_hbm, plan_hbm, wx_hbm, state_hbm, x_ref, z_ref, bc_ref, dt_ref, bias_ref,
    rate_ref, skip_ref,
    info_ref, xd_ref, gate_ref, dec_ref, dtd_ref, wide_ref, skipd_ref, wxd_ref, perm_ref,
    place_ref, kept_ref, cx_ref, cb_ref,
    counts_ref, plan_ref, wx_ref, sems,
):
    slots, steps, channels = x_ref.shape
    heads = dt_ref.shape[2]
    blocks = channels // LANES
    taps = cx_ref.shape[0]
    me = me_ref[0]
    copies = [
        pltpu.make_async_copy(src, dst, sems.at[i])
        for i, (src, dst) in enumerate(
            (
                (counts_hbm, counts_ref), (plan_hbm, plan_ref), (wx_hbm, wx_ref),
            )
        )
    ]
    for copy in copies:
        copy.start()
    copies[0].wait()
    copies[1].wait()
    reqs = plan_ref.shape[0]
    owners = counts_ref.shape[0]
    for d in range(owners):
        info_ref[INFO + d] = 0

    def look(r, carry):
        kept_to, kept_from, has_kept, moved_to, has_moved = carry
        home, local = r // slots, r % slots
        goal = plan_ref[r]
        live = local < counts_ref[home]
        owner, place = goal // slots, goal % slots
        mine = live & (owner == me)
        own = mine & (home == me)
        into = mine & (home != me)

        @pl.when(live & (owner != home))
        def _():
            info_ref[INFO + owner] = home

        return (
            jnp.where(own, place, kept_to), jnp.where(own, local, kept_from),
            jnp.where(own, 1, has_kept), jnp.where(into, place, moved_to),
            jnp.where(into, 1, has_moved),
        )

    carry = (jnp.int32(0),) * 5
    if reqs <= 32:
        for r in range(reqs):
            carry = look(r, carry)
    else:
        carry = lax.fori_loop(0, reqs, look, carry)
    kept_to, kept_from, has_kept, moved_to, has_moved = carry
    moved_to = jnp.where(has_moved > 0, moved_to, jnp.where(has_kept > 0, 1 - kept_to, 0))
    kept_to = 1 - moved_to
    for i, v in enumerate((kept_to, kept_from, has_kept, moved_to, has_moved, me)):
        info_ref[i] = v
    copies += copy_rows(state_hbm.at[kept_from], kept_ref, sems, len(copies), COPIES)
    shape = perm_ref.shape
    line = lax.broadcasted_iota(jnp.int32, shape, 0)
    lane = lax.broadcasted_iota(jnp.int32, shape, 1)
    span = shape[0] // QUAD
    p = (line % span // (2 * steps) * QUAD + line // span) * 2 + line % (2 * steps) // steps
    hit = (lane // LANES == line % steps) & (lane % P_SIZE == p)
    perm_ref[...] = jnp.where(hit, 1.0, 0.0).astype(jnp.bfloat16)
    shape = place_ref.shape
    line = lax.broadcasted_iota(jnp.int32, shape, 0)
    lane = lax.broadcasted_iota(jnp.int32, shape, 1)
    place_ref[...] = jnp.where(lane // P_SIZE == line, 1.0, 0.0).astype(jnp.bfloat16)
    rate = jnp.exp(rate_ref[...])
    raw = [dt_ref[s] + bias_ref[...] for s in range(slots)]
    delta = [jnp.maximum(v, 0.0) + jnp.log1p(jnp.exp(-jnp.abs(v))) for v in raw]
    decay = [jnp.exp(-v * rate) for v in delta]
    at = lax.broadcasted_iota(jnp.int32, (blocks, heads), 0)
    of = lax.broadcasted_iota(jnp.int32, (blocks, heads), 1)
    lines = [v[t : t + 1] for v in delta + decay for t in range(steps)] + [skip_ref[...]]
    spread = jnp.concatenate([jnp.where(of // 2 == at, line, 0.0) for line in lines], 0)
    high = spread.astype(jnp.bfloat16)
    rest = spread - high.astype(jnp.float32)
    middle = rest.astype(jnp.bfloat16)
    low = (rest - middle.astype(jnp.float32)).astype(jnp.bfloat16)
    head = lax.broadcasted_iota(jnp.int32, (heads, LANES), 0)
    lane = lax.broadcasted_iota(jnp.int32, (heads, LANES), 1)
    chosen = jnp.where(head % 2 == lane // (LANES // 2), 1.0, 0.0).astype(jnp.bfloat16)
    out = jnp.dot(high, chosen, preferred_element_type=jnp.float32)
    out = out + jnp.dot(middle, chosen, preferred_element_type=jnp.float32)
    out = out + jnp.dot(low, chosen, preferred_element_type=jnp.float32)
    run = steps * blocks
    for s in range(slots):
        dtd_ref[s] = out[s * run : (s + 1) * run]
        dec_ref[s] = out[(slots + s) * run : (slots + s + 1) * run]
        total = decay[s][:1]
        for t in range(1, steps):
            total = total * decay[s][t : t + 1]
        total = jnp.concatenate([total, total], 1)
        wide = jnp.sum(jnp.where(head == lane, total, 0.0), axis=1, keepdims=True)
        wide_ref[s] = jnp.broadcast_to(wide, (heads, LANES))
    skipd_ref[...] = out[2 * slots * run :]
    for copy in copies[2:3]:
        copy.wait()
    x = [x_ref[s].astype(jnp.float32) for s in range(slots)]
    for s in range(slots):
        dense_rows(xd_ref.at[s], 0, x[s])
        dense_rows(gate_ref.at[s], 0, z_ref[s].astype(jnp.float32))
    dense_rows(wxd_ref, 0, wx_ref[...])
    gate_ref[...] = silu(gate_ref[...])
    full = [jnp.where(kept_to == s, has_kept, has_moved) > 0 for s in range(slots)]
    for k in range(taps):
        t = steps - taps + k
        rows = [jnp.where(full[s], x[s][t : t + 1], 0.0) for s in range(slots)]
        cx_ref[k] = jnp.concatenate(rows, 0).astype(jnp.bfloat16)
        for s in range(slots):
            pairs = bc_ref[s, t].astype(jnp.float32)
            cb_ref[s, k] = jnp.where(full[s], pairs, 0.0).astype(jnp.bfloat16)
    for copy in copies[3:]:
        copy.wait()


def slot_inputs(slot, steps, x_ref, bc_ref, gate_ref, dec_ref, dt_ref):
    blocks = x_ref.shape[1] // steps
    rows = [pl.ds(t * blocks, blocks) for t in range(steps)]
    return [[ref[slot, r, :] for r in rows] for ref in (x_ref, gate_ref, dec_ref, dt_ref)] + [
        [bc_ref[slot, t].astype(jnp.float32) for t in range(steps)]
    ]


def kept_kernel(
    info_ref, state_ref, cx_ref, cb_ref, x_ref, bc_ref, gate_ref, dec_ref, dt_ref, skip_ref,
    wx_ref, bx_ref, wb_ref, bb_ref, perm_ref, wide_ref, place_ref,
    out_hbm, gated_ref, sums_ref, spread_ref, mixed_ref, turn_ref, rows_ref, new_ref, sems,
):
    steps = bc_ref.shape[1]
    blocks = bx_ref.shape[0]
    taps = cx_ref.shape[0]
    slot, origin, full = info_ref[0], info_ref[1], info_ref[2] > 0
    cx = cx_ref[...].astype(jnp.float32)
    dense_rows(rows_ref, 0, jnp.where(origin == 0, cx[:, 0], cx[:, 1]))
    cb = of_slot(cb_ref[...].astype(jnp.float32), origin)
    new_x, gate, dec, dts, new_b = slot_inputs(
        slot, steps, x_ref, bc_ref, gate_ref, dec_ref, dt_ref
    )
    seq_x = [rows_ref[k * blocks : (k + 1) * blocks, :] for k in range(taps)] + new_x
    seq_b = [cb[k] for k in range(taps)] + new_b
    xs, bs, cs = small_steps(seq_x, seq_b, wx_ref, bx_ref, wb_ref, bb_ref, steps)

    def write(j, new):
        new_ref[:, j * LANES : (j + 1) * LANES] = jnp.where(full, new, 0.0)

    def tile(j):
        return state_ref[:, j * LANES : (j + 1) * LANES]

    mixed = against_c(tile, lambda j: j, cs, perm_ref, turn_ref)
    gated, sums = gated_steps(
        mixed, None, xs, bs, cs, dec, dts, skip_ref[...], gate, mixed_ref
    )
    spread = spread_x(xs, dec, dts, spread_ref)
    new_state(tile, lambda j: j, wide_ref[slot], spread, bs, place_ref, write)
    copies = copy_rows(new_ref, out_hbm.at[slot], sems, 0, COPIES)
    for t in range(steps):
        gated_ref[t] = gated[t]
    sums_ref[...] = jnp.concatenate(sums, 0)
    for copy in copies:
        copy.wait()


def piece_tiles(masks, me, got_refs, heads):
    direct = len(masks) > 1
    share = got_refs[0].shape[-2] - AUX
    run = min(share, heads)
    each = share // heads

    def load(m, rows):
        part = got_refs[m][rows, :] if direct else got_refs[0][m, rows, :]
        return part.astype(jnp.int32).astype(jnp.float32)

    def tile(j):
        if direct:
            return load(j // each, pl.ds(j % each * heads, heads))
        flats = range(j * heads, (j + 1) * heads, run)
        return jnp.concatenate([load(f // share, pl.ds(f % share, run)) for f in flats], 0)

    def first(j):
        return (me ^ masks[j // each]) * each + j % each if direct else j

    return load, tile, first


def moved_kernel(masks, info_ref, *refs):
    pieces = len(masks)
    got_refs = refs[:pieces]
    (
        kept_sums_ref, x_ref, bc_ref, gate_ref, dec_ref, dt_ref, skip_ref,
        wx_ref, bx_ref, wb_ref, bb_ref, perm_ref, wide_ref,
        gated_ref, sums_ref, spread_ref, b_ref, wide_out_ref, rows_ref, mixed_ref, turn_ref, aux_ref,
    ) = refs[pieces:]
    direct = pieces > 1
    steps, groups = bc_ref.shape[1:3]
    blocks = bx_ref.shape[0]
    taps = wx_ref.shape[0] // blocks - 1
    heads = wide_ref.shape[1]
    share = got_refs[0].shape[-2] - AUX
    slot, me = info_ref[3], info_ref[5]
    new_x, gate, dec, dts, new_b = slot_inputs(
        slot, steps, x_ref, bc_ref, gate_ref, dec_ref, dt_ref
    )
    load, tile, first = piece_tiles(masks, me, got_refs, heads)
    for m in range(pieces if direct else got_refs[0].shape[0]):
        if direct:
            at = pl.ds(pl.multiple_of((me ^ masks[m]) * AUX, AUX), AUX)
            aux_ref[at, :] = load(m, pl.ds(share, AUX))
        elif m * AUX < aux_ref.shape[0]:
            aux_ref[m * AUX : (m + 1) * AUX, :] = load(m, pl.ds(share, AUX))

    last = aux_ref[taps * blocks : taps * blocks + AUX, :]
    codes = last[taps * groups : taps * groups + 1]
    row = lax.broadcasted_iota(jnp.int32, (heads, LANES), 0)
    lane = lax.broadcasted_iota(jnp.int32, (heads, LANES), 1)
    code = jnp.sum(jnp.where(row == lane, codes, 0.0), axis=1, keepdims=True)
    scale = level_scale(code) * (1.0 / LEVELS)
    scale_x = level_scale(codes[:, heads : heads + 1]) * (1.0 / LEVELS)
    scale_b = level_scale(codes[:, heads + 1 : heads + 2]) * (1.0 / LEVELS)
    seq_x = [aux_ref[k * blocks : (k + 1) * blocks, :] * scale_x for k in range(taps)] + new_x
    seq_b = [last[k * groups : (k + 1) * groups] * scale_b for k in range(taps)] + new_b
    xs, bs, cs = small_steps(seq_x, seq_b, wx_ref, bx_ref, wb_ref, bb_ref, steps)
    mixed = against_c(tile, first, cs, perm_ref, turn_ref)
    gated, sums = gated_steps(
        mixed, scale, xs, bs, cs, dec, dts, skip_ref[...], gate, mixed_ref
    )
    for t in range(steps):
        gated_ref[t] = gated[t]
        b_ref[t] = bs[t]
    sums_ref[...] = jnp.concatenate([kept_sums_ref[...]] + sums, 0)
    spread_ref[...] = spread_x(xs, dec, dts, rows_ref)
    wide_out_ref[...] = wide_ref[slot] * scale


def state_kernel(masks, info_ref, *refs):
    pieces = len(masks)
    got_refs = refs[:pieces]
    (
        spread_ref, b_ref, wide_ref, place_ref, kept_ref, moved_ref, norm_ref,
        new_ref, ready_ref, rows_ref,
    ) = refs[pieces:]
    full, me = info_ref[4] > 0, info_ref[5]
    _, tile, first = piece_tiles(masks, me, got_refs, wide_ref.shape[0])

    def write(j, new):
        at = pl.ds(pl.multiple_of(first(j) * LANES, LANES), LANES)
        new_ref[:, at] = jnp.where(full, new, 0.0)

    bs = [b_ref[t] for t in range(b_ref.shape[0])]
    new_state(tile, first, wide_ref[...], spread_ref[...], bs, place_ref, write)
    steps, blocks = kept_ref.shape[:2]
    for which, ref in enumerate((kept_ref, moved_ref)):
        for t in range(steps):
            rows_ref[t * blocks : (t + 1) * blocks, :] = ref[t] * norm_ref[...]
        for b in range(blocks):
            ready_ref[which, :, b * LANES : (b + 1) * LANES] = rows_ref[
                pl.ds(b, steps, stride=blocks), :
            ]


def norm_kernel(
    info_ref, held_hbm, new_ref, ready_ref, mine_ref, theirs_ref, out_hbm, y_ref, sems
):
    del held_hbm
    copies = copy_rows(new_ref, out_hbm.at[info_ref[3]], sems, 0, COPIES)
    steps = ready_ref.shape[1]
    factor = lax.rsqrt((mine_ref[...] + theirs_ref[...]) * (1.0 / (H * P_SIZE)) + 1e-05)
    for which in range(ready_ref.shape[0]):
        full = info_ref[2 + 2 * which] > 0
        rows = factor[which * steps : (which + 1) * steps]
        for b in range(0, ready_ref.shape[2], LANES):
            values = jnp.where(full, ready_ref[which, :, b : b + LANES] * rows, 0.0)
            y_ref[info_ref[3 * which], :, b : b + LANES] = values.astype(jnp.bfloat16)
    for copy in copies:
        copy.wait()


def partner_masks(owners):
    gray = [i ^ (i >> 1) for i in range(owners)]
    near, far = gray[1 : owners // 2], gray[owners // 2 :]
    order = [0]
    for i, k in enumerate(far):
        order += [k, *near[i : i + 1]]
    return tuple(order)


def on_device(
    counts,
    move_plan,
    ssm_state,
    conv_x_state,
    conv_bc_state,
    x_in,
    bc_in,
    z_in,
    dt_in,
    conv_w_x,
    conv_b_x,
    conv_w_bc,
    conv_b_bc,
    dt_bias,
    a_log,
    d_skip,
    norm_w,
):
    owners = lax.axis_size("req")
    owner = lax.axis_index("req").astype(jnp.int32)
    slots, heads, columns = ssm_state.shape
    places, steps, channels = x_in.shape
    taps = conv_x_state.shape[1]
    groups, pair = conv_bc_state.shape[2:]
    blocks = channels // LANES
    share = heads * columns // LANES // owners
    aux_rows = taps * blocks + AUX
    f32 = jnp.float32
    direct = owners <= 16 and owners & (owners - 1) == 0 and share % (QUAD * heads) == 0
    masks = partner_masks(owners) if direct else (0,)
    pieces = len(masks)
    smem = pl.BlockSpec(memory_space=pltpu.SMEM)
    vmem = pl.BlockSpec(memory_space=pltpu.VMEM)
    anywhere = pl.BlockSpec(memory_space=pl.ANY)

    def shaped(*shape, dtype=f32):
        return jax.ShapeDtypeStruct(shape, dtype)

    def call(kernel, name, in_specs, out_specs, out_shape, scratch=(), **more):
        return pl.pallas_call(
            kernel,
            in_specs=in_specs,
            out_specs=out_specs,
            out_shape=out_shape,
            scratch_shapes=scratch,
            compiler_params=pltpu.CompilerParams(vmem_limit_bytes=VMEM_LIMIT),
            name=name,
            **more,
        )

    def in_hbm(*values):
        return [pltpu.with_memory_space_constraint(v, pltpu.MemorySpace.HBM) for v in values]

    me = owner.reshape(1)
    conv_x_taps = jnp.transpose(conv_x_state, (1, 0, 2))
    piece = (share + AUX, LANES) if direct else (owners, share + AUX, LANES)
    sent = [shaped(*piece, dtype=jnp.int16)] * pieces
    payload = call(
        functools.partial(pack_kernel, masks), "pack", [smem] + [anywhere] * 3 + [vmem] * 2, [vmem] * pieces, sent,
        [
            pltpu.SMEM(counts.shape, jnp.int32),
            pltpu.SMEM(move_plan.shape, jnp.int32),
            pltpu.VMEM(ssm_state.shape, f32),
            pltpu.VMEM((max(aux_rows, pieces * AUX), LANES), f32),
            pltpu.SemaphoreType.DMA((2 + slots * heads // BLOCK,)),
        ],
    )(me, *in_hbm(counts, move_plan, ssm_state), conv_x_taps, conv_bc_state)

    def exchange(values):
        if not direct:
            return [lax.all_to_all(values[0], "req", split_axis=0, concat_axis=0, tiled=True)]
        out = list(values)
        for i, k in enumerate(masks):
            if k:
                out[i] = lax.ppermute(values[i], "req", [(o, o ^ k) for o in range(owners)])
        return out

    spread = exchange(payload)

    (
        _, me_late, cx_late, cb_late, bc_late, dt_late, bias_late, rate_late, skip_late,
        bx_late, wb_late, bb_late, norm_late, x_late, z_late,
    ) = lax.optimization_barrier(
        (
            payload[0], me, conv_x_taps, conv_bc_state, bc_in, dt_in, dt_bias, a_log, d_skip,
            conv_b_x, conv_w_bc, conv_b_bc, norm_w, x_in, z_in,
        )
    )
    rows = (places, steps * blocks, LANES)
    info, x_dense, gate, dec, dt_dense, wide, skip, wx, perm, place, kept_state, *convs = call(
        prep_kernel, "prep", [smem] + [anywhere] * 4 + [vmem] * 7, [smem] + [vmem] * 12,
        [
            shaped(INFO + owners, dtype=jnp.int32), shaped(*rows), shaped(*rows), shaped(*rows),
            shaped(*rows), shaped(places, heads, LANES), shaped(blocks, LANES),
            shaped((taps + 1) * blocks, LANES),
            shaped(QUAD * P_SIZE, 2 * steps * P_SIZE, dtype=jnp.bfloat16),
            shaped(P_SIZE, columns, dtype=jnp.bfloat16), shaped(heads, columns),
            shaped(taps, places, channels, dtype=jnp.bfloat16),
            shaped(*conv_bc_state.shape, dtype=jnp.bfloat16),
        ],
        [
            pltpu.SMEM(counts.shape, jnp.int32),
            pltpu.SMEM(move_plan.shape, jnp.int32),
            pltpu.VMEM(conv_w_x.shape, f32),
            pltpu.SemaphoreType.DMA((3 + COPIES,)),
        ],
    )(
        me_late, *in_hbm(counts, move_plan, conv_w_x, ssm_state), x_late, z_late, bc_late,
        dt_late, bias_late.reshape(1, -1), rate_late.reshape(1, -1), skip_late.reshape(1, -1),
    )

    picked = call(
        functools.partial(pick_kernel, masks), "pick", [smem] + [vmem] * pieces, [vmem] * pieces, sent,
        [pltpu.VMEM((owners, *piece), jnp.int16)] if direct else [],
    )(info, *spread)
    got = exchange(picked)

    _, info = lax.optimization_barrier((picked[0], info))
    common = [x_dense, bc_late, gate, dec, dt_dense, skip, wx]
    common += [bx_late.reshape(blocks, LANES), wb_late, bb_late, perm, wide]
    scratch = [pltpu.VMEM((steps * heads, LANES), f32)] * 2 + [pltpu.VMEM((LANES, LANES), f32)]
    held, kept_gated, kept_sums = call(
        kept_kernel, "kept", [smem] + [vmem] * (4 + len(common)), [anywhere, vmem, vmem],
        [shaped(places, heads, columns), shaped(steps, blocks, LANES), shaped(steps, LANES)],
        scratch
        + [
            pltpu.VMEM((taps * blocks, LANES), f32),
            pltpu.VMEM((heads, columns), f32),
            pltpu.SemaphoreType.DMA((COPIES,)),
        ],
    )(info, kept_state, cx_late, cb_late, *common, place)
    moved_gated, sums, spread_rows, b_steps, wide_scaled = call(
        functools.partial(moved_kernel, masks), "moved",
        [smem] + [vmem] * (pieces + 1 + len(common)), [vmem] * 5,
        [
            shaped(steps, blocks, LANES), shaped(2 * steps, LANES),
            shaped(steps * heads, 2 * LANES, dtype=jnp.bfloat16),
            shaped(steps, groups, pair), shaped(heads, LANES),
        ],
        scratch + [pltpu.VMEM((max(aux_rows, pieces * AUX), LANES), f32)],
    )(info, *got, kept_sums, *common)
    theirs = lax.ppermute(sums, "tp", [(0, 1), (1, 0)])
    new, ready = call(
        functools.partial(state_kernel, masks), "state",
        [smem] + [vmem] * (pieces + 7), [vmem] * 2,
        [shaped(heads, columns), shaped(places, steps, channels)],
        [pltpu.VMEM((steps * blocks, LANES), f32)],
    )(
        info, *got, spread_rows, b_steps, wide_scaled, place, kept_gated, moved_gated,
        norm_late.reshape(blocks, LANES),
    )
    new_ssm, y_out = call(
        norm_kernel, "norm", [smem, anywhere] + [vmem] * 4, [anywhere, vmem],
        [
            shaped(places, heads, columns),
            shaped(places, steps, channels, dtype=jnp.bfloat16),
        ],
        [pltpu.SemaphoreType.DMA((COPIES,))],
        input_output_aliases={1: 0},
    )(info, held, new, ready, sums, theirs)
    return (y_out, new_ssm, jnp.transpose(convs[0], (1, 0, 2)), convs[1])


def solution(mesh):
    in_specs = (
        P("parts"),
        P("parts"),
        P(("parts", "req"), "tp", None),
        P(("parts", "req"), None, "tp"),
        P(("parts", "req"), None, "tp", None),
        P(("parts", "req"), None, "tp"),
        P(("parts", "req"), None, "tp", None),
        P(("parts", "req"), None, "tp"),
        P(("parts", "req"), None, "tp"),
        P(None, "tp"),
        P("tp"),
        P(None, "tp", None),
        P("tp", None),
        P("tp"),
        P("tp"),
        P("tp"),
        P("tp"),
    )
    out_specs = (
        P(("parts", "req"), None, "tp"),
        P(("parts", "req"), "tp", None),
        P(("parts", "req"), None, "tp"),
        P(("parts", "req"), None, "tp", None),
    )
    return jax.shard_map(
        on_device, mesh=mesh, in_specs=in_specs, out_specs=out_specs, check_vma=False
    )
```

```python
import functools

import jax
import jax.numpy as jnp
from jax import lax
from jax.experimental import pallas as pl
from jax.experimental.pallas import tpu as pltpu
from jax.sharding import PartitionSpec as P

H = 128
P_SIZE = 64
LANES = 128
AUX = 16
BLOCK = 32
QUAD = 4
COPIES = 8
INFO = 8
REACH = 6.0
LEVELS = 32767.0
VMEM_LIMIT = 48 * 1024 * 1024


def level_code(top):
    code = jnp.floor(-8.0 / jnp.log(2.0) * jnp.log(jnp.maximum(top, 1e-30) / REACH) - 0.01)
    return jnp.clip(code, 0.0, 800.0)


def level_scale(code):
    return REACH * jnp.exp(code * (-0.125 * jnp.log(2.0)))


def moving_slot(counts_ref, plan_ref, me, slots):
    slot = jnp.int32(0)
    for local in range(1, slots):
        live = local < counts_ref[me]
        away = plan_ref[me * slots + local] // slots != me
        slot = jnp.where(live & away, local, slot)
    return slot


def dense_rows(rows_ref, at, values):
    count, channels = values.shape
    blocks = channels // LANES
    for b in range(blocks):
        part = values[:, b * LANES : (b + 1) * LANES]
        if count == 1:
            rows_ref[at + b : at + b + 1, :] = part
        else:
            rows_ref[pl.ds(at + b, count, stride=blocks), :] = part


def copy_rows(src, dst, sems, at, count):
    run = dst.shape[0] // count
    copies = []
    for i in range(count):
        rows = pl.ds(i * run, run)
        copies.append(pltpu.make_async_copy(src.at[rows], dst.at[rows], sems.at[at + i]))
        copies[-1].start()
    return copies


def of_slot(values, slot):
    return jnp.where(slot == 0, values[0], values[1])


def pack_kernel(masks, me_ref, counts_hbm, plan_hbm, state_hbm, cx_hbm, cb_hbm, *refs):
    *out_refs, counts_ref, plan_ref, state_ref, cx_ref, cb_ref, rows_ref, sems = refs
    direct = len(out_refs) > 1
    slots, heads, columns = state_ref.shape
    owners = len(out_refs) if direct else out_refs[0].shape[0]
    share = out_refs[0].shape[-2] - AUX
    run = min(share, BLOCK)
    each = share // heads
    me = me_ref[0]
    small = [
        pltpu.make_async_copy(src, dst, sems.at[i])
        for i, (src, dst) in enumerate(
            ((counts_hbm, counts_ref), (plan_hbm, plan_ref), (cx_hbm, cx_ref), (cb_hbm, cb_ref))
        )
    ]
    for copy in small:
        copy.start()
    large = []
    for at in range(0, heads, BLOCK):
        for slot in range(slots):
            part = (slot, pl.ds(at, BLOCK))
            copy = pltpu.make_async_copy(
                state_hbm.at[part], state_ref.at[part], sems.at[len(small) + len(large)]
            )
            copy.start()
            large.append(copy)
    small[0].wait()
    small[1].wait()
    slot = moving_slot(counts_ref, plan_ref, me, slots)
    small[2].wait()
    small[3].wait()
    taps, _, channels = cx_ref.shape
    groups = cb_ref.shape[2]
    blocks = channels // LANES
    cx = cx_ref[...].astype(jnp.float32)
    cx = jnp.where(slot == 0, cx[:, 0], cx[:, 1])
    cb = of_slot(cb_ref[...].astype(jnp.float32), slot)
    code_x = level_code(jnp.max(jnp.abs(cx)).reshape(1, 1))
    code_b = level_code(jnp.max(jnp.abs(cb)).reshape(1, 1))
    dense_rows(rows_ref, 0, cx)
    last = taps * blocks
    rows_ref[last:, :] = jnp.zeros((rows_ref.shape[0] - last, LANES), jnp.float32)
    for k in range(taps):
        rows_ref[last + k * groups : last + (k + 1) * groups, :] = cb[k]
    lane = lax.broadcasted_iota(jnp.int32, (BLOCK, LANES), 1)
    row = lax.broadcasted_iota(jnp.int32, (BLOCK, LANES), 0)
    codes = jnp.where(lane[:1] == heads, code_x, 0.0)
    codes = jnp.where(lane[:1] == heads + 1, code_b, codes)
    for q in range(heads // BLOCK):
        for copy in large[q * slots : (q + 1) * slots]:
            copy.wait()
        at = q * BLOCK
        top = jnp.abs(state_ref[slot, at : at + BLOCK, :LANES])
        for j in range(1, columns // LANES):
            tile = state_ref[slot, at : at + BLOCK, j * LANES : (j + 1) * LANES]
            top = jnp.maximum(top, jnp.abs(tile))
        code = level_code(jnp.max(top, axis=1, keepdims=True))
        codes = codes + jnp.sum(jnp.where(row + at == lane, code, 0.0), axis=0, keepdims=True)
        factor = jnp.broadcast_to(LEVELS / level_scale(code), (BLOCK, LANES))
        for j in range(columns // LANES):
            place = (me ^ masks[j // each]) * each + j % each if direct else j
            lanes = pl.ds(pl.multiple_of(place * LANES, LANES), LANES)
            tile = state_ref[slot, at : at + BLOCK, lanes] * factor
            tile = jnp.round(tile).astype(jnp.int32).astype(jnp.int16)
            for part in range(0, BLOCK, run):
                flat = j * heads + at + part
                rows = pl.ds(flat % share, run)
                if direct:
                    out_refs[flat // share][rows, :] = tile[part : part + run]
                else:
                    out_refs[0][flat // share, rows, :] = tile[part : part + run]
    factor_x = LEVELS / level_scale(code_x)
    factor_b = LEVELS / level_scale(code_b)
    line = lax.broadcasted_iota(jnp.int32, (AUX, LANES), 0)
    rows_ref[:last, :] = rows_ref[:last, :] * factor_x
    values = rows_ref[last : last + AUX, :] * factor_b
    rows_ref[last : last + AUX, :] = jnp.where(line == taps * groups, codes, values)
    for m in range(owners):
        if direct:
            values = rows_ref[pl.ds(pl.multiple_of((me ^ masks[m]) * AUX, AUX), AUX), :]
        elif m * AUX < last + AUX:
            values = rows_ref[m * AUX : (m + 1) * AUX, :]
        else:
            values = jnp.zeros((AUX, LANES), jnp.float32)
        values = jnp.round(values).astype(jnp.int32).astype(jnp.int16)
        if direct:
            out_refs[m][share:, :] = values
        else:
            out_refs[0][m, share:, :] = values


def pick_kernel(masks, info_ref, *refs):
    if len(refs) == 2:
        in_ref, out_ref = refs
        for m in range(out_ref.shape[0]):
            out_ref[m] = in_ref[info_ref[INFO + m]]
        return
    owners = len(refs) // 2
    *in_refs, all_ref = refs[:owners] + refs[-1:]
    out_refs = refs[owners:-1]
    me = info_ref[5]
    for i, k in enumerate(masks):
        all_ref[k] = in_refs[i][...]
    for i, k in enumerate(masks):
        out_refs[i][...] = all_ref[info_ref[INFO + (me ^ k)] ^ me]


def silu(v):
    return v / (1.0 + jnp.exp(-v))


def split(v):
    high = v.astype(jnp.bfloat16)
    low = (v - high.astype(jnp.float32)).astype(jnp.bfloat16)
    return high, low


def small_steps(seq_x, seq_b, wx_ref, bx_ref, wb_ref, bb_ref, steps):
    taps = len(seq_x) - steps + 1
    blocks = bx_ref.shape[0]
    xs, bs, cs = [], [], []
    for t in range(steps):
        total = bx_ref[...]
        pairs = bb_ref[...]
        for k in range(taps):
            total = total + wx_ref[k * blocks : (k + 1) * blocks, :] * seq_x[t + k]
            pairs = pairs + wb_ref[k] * seq_b[t + k]
        xs.append(silu(total))
        pairs = silu(pairs)
        turned = jnp.concatenate([pairs[:, LANES // 2 :], pairs[:, : LANES // 2]], 1)
        lower = lax.broadcasted_iota(jnp.int32, pairs.shape, 1) < LANES // 2
        bs.append(jnp.where(lower, pairs, turned))
        cs.append(jnp.where(lower, turned, pairs))
    return xs, bs, cs


def by_group(rows, count):
    groups = rows.shape[0]
    run = count // groups
    return jnp.concatenate(
        [jnp.broadcast_to(rows[g : g + 1], (run, rows.shape[1])) for g in range(groups)], 0
    )


def spread_x(xs, dec, dts, spread_ref):
    blocks = xs[0].shape[0]
    heads = 2 * blocks
    lower = lax.broadcasted_iota(jnp.int32, (blocks, LANES), 1) < LANES // 2
    later = None
    for t in reversed(range(len(xs))):
        weighted = xs[t] * dts[t]
        if later is not None:
            weighted = weighted * later
        later = dec[t] if later is None else later * dec[t]
        spread_ref[pl.ds(t * heads, blocks, stride=2), :] = jnp.where(lower, weighted, 0.0)
        spread_ref[pl.ds(t * heads + 1, blocks, stride=2), :] = jnp.where(lower, 0.0, weighted)
    return jnp.concatenate(split(spread_ref[...]), 1)


def new_state(tile, first, wide, spread, bs, place_ref, write):
    steps = len(bs)
    heads = wide.shape[0]
    b_rows = [by_group(b, heads) for b in bs]
    for j in range(0, P_SIZE * P_SIZE // LANES, 2):
        at = pl.ds(pl.multiple_of(first(j) * LANES, LANES), 2 * LANES)
        grown = jnp.dot(
            spread,
            jnp.concatenate([place_ref[:, at]] * (spread.shape[1] // P_SIZE), 0),
            preferred_element_type=jnp.float32,
        )
        for half in range(2):
            new = wide * tile(j + half)
            for t in range(steps):
                piece = grown[t * heads : (t + 1) * heads, half * LANES : (half + 1) * LANES]
                new = new + piece * b_rows[t]
            write(j + half, new)


def against_c(tile, first, cs, perm_ref, rows_ref):
    steps = len(cs)
    groups = cs[0].shape[0]
    lower = lax.broadcasted_iota(jnp.int32, (steps, LANES), 1) < LANES // 2
    lefts = []
    for g in range(groups):
        rows = jnp.concatenate([c[g : g + 1] for c in cs], 0)
        rows = jnp.concatenate([jnp.where(lower, rows, 0.0), jnp.where(lower, 0.0, rows)], 0)
        lefts.append(jnp.concatenate([jnp.concatenate([v, v], 1) for v in split(rows)], 0))
    count = P_SIZE * P_SIZE // LANES
    line = 2 * steps
    run = LANES // QUAD
    for u in range(0, count, 2 * QUAD):
        parts = [jnp.concatenate(split(tile(j)), 1) for j in range(u, u + 2 * QUAD)]
        for g in range(groups):
            right = jnp.concatenate([p[g * run : (g + 1) * run] for p in parts], 0)
            out = lax.dot_general(
                lefts[g], right, (((1,), (1,)), ((), ())), preferred_element_type=jnp.float32
            )
            out = out[:line] + out[line:]
            for w in range(2):
                quad = first(u + w * QUAD) // QUAD
                at = pl.ds(pl.multiple_of(g * (count // QUAD) * line + quad * line, 8), line)
                rows_ref[at, :] = out[:, w * LANES : (w + 1) * LANES]
    turned = jnp.transpose(rows_ref[...])
    lower = lax.broadcasted_iota(jnp.int32, (run, LANES), 1) < LANES // 2
    straight = [turned[i * run : (i + 1) * run] for i in range(QUAD)]
    rolled = [
        jnp.concatenate([v[:, LANES // 2 :], v[:, : LANES // 2]], 1) for v in straight
    ]
    low_group = [jnp.where(lower, straight[i], rolled[i + 1]) for i in range(0, QUAD, 2)]
    high_group = [jnp.where(lower, rolled[i], straight[i + 1]) for i in range(0, QUAD, 2)]
    values = jnp.concatenate(
        [jnp.concatenate(low_group, 1), jnp.concatenate(high_group, 1)], 0
    )
    heads = values.shape[0]
    out = jnp.dot(
        jnp.concatenate(split(values), 0), perm_ref[...], preferred_element_type=jnp.float32
    )
    return out[:heads] + out[heads:]


def gated_steps(mixed, scale, xs, bs, cs, dec, dts, skip, gate, mixed_ref):
    steps = len(xs)
    heads = mixed.shape[0]
    blocks = heads // 2
    lower = lax.broadcasted_iota(jnp.int32, (blocks, LANES), 1) < LANES // 2
    for t in range(steps):
        part = mixed[:, t * LANES : (t + 1) * LANES]
        mixed_ref[t * heads : (t + 1) * heads, :] = part if scale is None else part * scale
    gated, sums = [], []
    ahead = None
    weights = []
    for t in range(steps):
        weights = [w * dec[t] for w in weights] + [dts[t]]
        ahead = dec[t] if ahead is None else ahead * dec[t]
        even = mixed_ref[pl.ds(t * heads, blocks, stride=2), :]
        odd = mixed_ref[pl.ds(t * heads + 1, blocks, stride=2), :]
        out = ahead * jnp.where(lower, even, odd) + skip * xs[t]
        for s in range(t + 1):
            inner = 0.5 * jnp.sum(bs[s] * cs[t], axis=1, keepdims=True)
            inner = by_group(jnp.broadcast_to(inner, (inner.shape[0], LANES)), blocks)
            out = out + weights[s] * inner * xs[s]
        out = out * gate[t]
        gated.append(out)
        squares = jnp.sum(jnp.sum(out * out, axis=0, keepdims=True), axis=1, keepdims=True)
        sums.append(jnp.broadcast_to(squares, (1, LANES)))
    return gated, sums


def prep_kernel(
    me_ref, counts_hbm, plan_hbm, x_hbm, z_hbm, wx_hbm, state_hbm, bc_ref, dt_ref, bias_ref,
    rate_ref, skip_ref,
    info_ref, xd_ref, gate_ref, dec_ref, dtd_ref, wide_ref, skipd_ref, wxd_ref, perm_ref,
    place_ref, kept_ref, cx_ref, cb_ref,
    counts_ref, plan_ref, x_ref, z_ref, wx_ref, sems,
):
    slots, steps, channels = x_ref.shape
    heads = dt_ref.shape[2]
    blocks = channels // LANES
    taps = cx_ref.shape[0]
    me = me_ref[0]
    copies = [
        pltpu.make_async_copy(src, dst, sems.at[i])
        for i, (src, dst) in enumerate(
            (
                (counts_hbm, counts_ref), (plan_hbm, plan_ref), (x_hbm, x_ref), (z_hbm, z_ref),
                (wx_hbm, wx_ref),
            )
        )
    ]
    for copy in copies:
        copy.start()
    copies[0].wait()
    copies[1].wait()
    reqs = plan_ref.shape[0]
    owners = counts_ref.shape[0]
    for d in range(owners):
        info_ref[INFO + d] = 0

    def look(r, carry):
        kept_to, kept_from, has_kept, moved_to, has_moved = carry
        home, local = r // slots, r % slots
        goal = plan_ref[r]
        live = local < counts_ref[home]
        owner, place = goal // slots, goal % slots
        mine = live & (owner == me)
        own = mine & (home == me)
        into = mine & (home != me)

        @pl.when(live & (owner != home))
        def _():
            info_ref[INFO + owner] = home

        return (
            jnp.where(own, place, kept_to), jnp.where(own, local, kept_from),
            jnp.where(own, 1, has_kept), jnp.where(into, place, moved_to),
            jnp.where(into, 1, has_moved),
        )

    carry = (jnp.int32(0),) * 5
    if reqs <= 32:
        for r in range(reqs):
            carry = look(r, carry)
    else:
        carry = lax.fori_loop(0, reqs, look, carry)
    kept_to, kept_from, has_kept, moved_to, has_moved = carry
    moved_to = jnp.where(has_moved > 0, moved_to, jnp.where(has_kept > 0, 1 - kept_to, 0))
    kept_to = 1 - moved_to
    for i, v in enumerate((kept_to, kept_from, has_kept, moved_to, has_moved, me)):
        info_ref[i] = v
    copies += copy_rows(state_hbm.at[kept_from], kept_ref, sems, len(copies), COPIES)
    shape = perm_ref.shape
    line = lax.broadcasted_iota(jnp.int32, shape, 0)
    lane = lax.broadcasted_iota(jnp.int32, shape, 1)
    span = shape[0] // QUAD
    p = (line % span // (2 * steps) * QUAD + line // span) * 2 + line % (2 * steps) // steps
    hit = (lane // LANES == line % steps) & (lane % P_SIZE == p)
    perm_ref[...] = jnp.where(hit, 1.0, 0.0).astype(jnp.bfloat16)
    shape = place_ref.shape
    line = lax.broadcasted_iota(jnp.int32, shape, 0)
    lane = lax.broadcasted_iota(jnp.int32, shape, 1)
    place_ref[...] = jnp.where(lane // P_SIZE == line, 1.0, 0.0).astype(jnp.bfloat16)
    rate = jnp.exp(rate_ref[...])
    raw = [dt_ref[s] + bias_ref[...] for s in range(slots)]
    delta = [jnp.maximum(v, 0.0) + jnp.log1p(jnp.exp(-jnp.abs(v))) for v in raw]
    decay = [jnp.exp(-v * rate) for v in delta]
    at = lax.broadcasted_iota(jnp.int32, (blocks, heads), 0)
    of = lax.broadcasted_iota(jnp.int32, (blocks, heads), 1)
    lines = [v[t : t + 1] for v in delta + decay for t in range(steps)] + [skip_ref[...]]
    spread = jnp.concatenate([jnp.where(of // 2 == at, line, 0.0) for line in lines], 0)
    high = spread.astype(jnp.bfloat16)
    rest = spread - high.astype(jnp.float32)
    middle = rest.astype(jnp.bfloat16)
    low = (rest - middle.astype(jnp.float32)).astype(jnp.bfloat16)
    head = lax.broadcasted_iota(jnp.int32, (heads, LANES), 0)
    lane = lax.broadcasted_iota(jnp.int32, (heads, LANES), 1)
    chosen = jnp.where(head % 2 == lane // (LANES // 2), 1.0, 0.0).astype(jnp.bfloat16)
    out = jnp.dot(high, chosen, preferred_element_type=jnp.float32)
    out = out + jnp.dot(middle, chosen, preferred_element_type=jnp.float32)
    out = out + jnp.dot(low, chosen, preferred_element_type=jnp.float32)
    run = steps * blocks
    for s in range(slots):
        dtd_ref[s] = out[s * run : (s + 1) * run]
        dec_ref[s] = out[(slots + s) * run : (slots + s + 1) * run]
        total = decay[s][:1]
        for t in range(1, steps):
            total = total * decay[s][t : t + 1]
        total = jnp.concatenate([total, total], 1)
        wide = jnp.sum(jnp.where(head == lane, total, 0.0), axis=1, keepdims=True)
        wide_ref[s] = jnp.broadcast_to(wide, (heads, LANES))
    skipd_ref[...] = out[2 * slots * run :]
    for copy in copies[2:5]:
        copy.wait()
    x = [x_ref[s].astype(jnp.float32) for s in range(slots)]
    for s in range(slots):
        dense_rows(xd_ref.at[s], 0, x[s])
        dense_rows(gate_ref.at[s], 0, z_ref[s].astype(jnp.float32))
    dense_rows(wxd_ref, 0, wx_ref[...])
    gate_ref[...] = silu(gate_ref[...])
    full = [jnp.where(kept_to == s, has_kept, has_moved) > 0 for s in range(slots)]
    for k in range(taps):
        t = steps - taps + k
        rows = [jnp.where(full[s], x[s][t : t + 1], 0.0) for s in range(slots)]
        cx_ref[k] = jnp.concatenate(rows, 0).astype(jnp.bfloat16)
        for s in range(slots):
            pairs = bc_ref[s, t].astype(jnp.float32)
            cb_ref[s, k] = jnp.where(full[s], pairs, 0.0).astype(jnp.bfloat16)
    for copy in copies[5:]:
        copy.wait()


def slot_inputs(slot, steps, x_ref, bc_ref, gate_ref, dec_ref, dt_ref):
    blocks = x_ref.shape[1] // steps
    rows = [pl.ds(t * blocks, blocks) for t in range(steps)]
    return [[ref[slot, r, :] for r in rows] for ref in (x_ref, gate_ref, dec_ref, dt_ref)] + [
        [bc_ref[slot, t].astype(jnp.float32) for t in range(steps)]
    ]


def make_ready(gated, norm_ref, rows_ref, ready_ref):
    blocks = norm_ref.shape[0]
    steps = len(gated)
    for t in range(steps):
        rows_ref[t * blocks : (t + 1) * blocks, :] = gated[t] * norm_ref[...]
    for b in range(blocks):
        ready_ref[:, b * LANES : (b + 1) * LANES] = rows_ref[pl.ds(b, steps, stride=blocks), :]


def kept_kernel(
    info_ref, state_ref, cx_ref, cb_ref, x_ref, bc_ref, gate_ref, dec_ref, dt_ref, skip_ref,
    wx_ref, bx_ref, wb_ref, bb_ref, perm_ref, wide_ref, place_ref, norm_ref,
    out_hbm, ready_ref, sums_ref, spread_ref, mixed_ref, turn_ref, rows_ref, new_ref, sems,
):
    steps = bc_ref.shape[1]
    blocks = bx_ref.shape[0]
    taps = cx_ref.shape[0]
    slot, origin, full = info_ref[0], info_ref[1], info_ref[2] > 0
    cx = cx_ref[...].astype(jnp.float32)
    dense_rows(rows_ref, 0, jnp.where(origin == 0, cx[:, 0], cx[:, 1]))
    cb = of_slot(cb_ref[...].astype(jnp.float32), origin)
    new_x, gate, dec, dts, new_b = slot_inputs(
        slot, steps, x_ref, bc_ref, gate_ref, dec_ref, dt_ref
    )
    seq_x = [rows_ref[k * blocks : (k + 1) * blocks, :] for k in range(taps)] + new_x
    seq_b = [cb[k] for k in range(taps)] + new_b
    xs, bs, cs = small_steps(seq_x, seq_b, wx_ref, bx_ref, wb_ref, bb_ref, steps)

    def write(j, new):
        new_ref[:, j * LANES : (j + 1) * LANES] = jnp.where(full, new, 0.0)

    def tile(j):
        return state_ref[:, j * LANES : (j + 1) * LANES]

    mixed = against_c(tile, lambda j: j, cs, perm_ref, turn_ref)
    gated, sums = gated_steps(
        mixed, None, xs, bs, cs, dec, dts, skip_ref[...], gate, mixed_ref
    )
    spread = spread_x(xs, dec, dts, spread_ref)
    new_state(tile, lambda j: j, wide_ref[slot], spread, bs, place_ref, write)
    copies = copy_rows(new_ref, out_hbm.at[slot], sems, 0, COPIES)
    make_ready(gated, norm_ref, mixed_ref, ready_ref)
    sums_ref[...] = jnp.concatenate(sums, 0)
    for copy in copies:
        copy.wait()


def piece_tiles(masks, me, got_refs, heads):
    direct = len(masks) > 1
    share = got_refs[0].shape[-2] - AUX
    run = min(share, heads)
    each = share // heads

    def load(m, rows):
        part = got_refs[m][rows, :] if direct else got_refs[0][m, rows, :]
        return part.astype(jnp.int32).astype(jnp.float32)

    def tile(j):
        if direct:
            return load(j // each, pl.ds(j % each * heads, heads))
        flats = range(j * heads, (j + 1) * heads, run)
        return jnp.concatenate([load(f // share, pl.ds(f % share, run)) for f in flats], 0)

    def first(j):
        return (me ^ masks[j // each]) * each + j % each if direct else j

    return load, tile, first


def moved_kernel(masks, info_ref, *refs):
    pieces = len(masks)
    got_refs = refs[:pieces]
    (
        kept_sums_ref, x_ref, bc_ref, gate_ref, dec_ref, dt_ref, skip_ref,
        wx_ref, bx_ref, wb_ref, bb_ref, perm_ref, wide_ref,
        gated_ref, sums_ref, spread_ref, b_ref, wide_out_ref, rows_ref, mixed_ref, turn_ref, aux_ref,
    ) = refs[pieces:]
    direct = pieces > 1
    steps, groups = bc_ref.shape[1:3]
    blocks = bx_ref.shape[0]
    taps = wx_ref.shape[0] // blocks - 1
    heads = wide_ref.shape[1]
    share = got_refs[0].shape[-2] - AUX
    slot, me = info_ref[3], info_ref[5]
    new_x, gate, dec, dts, new_b = slot_inputs(
        slot, steps, x_ref, bc_ref, gate_ref, dec_ref, dt_ref
    )
    load, tile, first = piece_tiles(masks, me, got_refs, heads)
    for m in range(pieces if direct else got_refs[0].shape[0]):
        if direct:
            at = pl.ds(pl.multiple_of((me ^ masks[m]) * AUX, AUX), AUX)
            aux_ref[at, :] = load(m, pl.ds(share, AUX))
        elif m * AUX < aux_ref.shape[0]:
            aux_ref[m * AUX : (m + 1) * AUX, :] = load(m, pl.ds(share, AUX))

    last = aux_ref[taps * blocks : taps * blocks + AUX, :]
    codes = last[taps * groups : taps * groups + 1]
    row = lax.broadcasted_iota(jnp.int32, (heads, LANES), 0)
    lane = lax.broadcasted_iota(jnp.int32, (heads, LANES), 1)
    code = jnp.sum(jnp.where(row == lane, codes, 0.0), axis=1, keepdims=True)
    scale = level_scale(code) * (1.0 / LEVELS)
    scale_x = level_scale(codes[:, heads : heads + 1]) * (1.0 / LEVELS)
    scale_b = level_scale(codes[:, heads + 1 : heads + 2]) * (1.0 / LEVELS)
    seq_x = [aux_ref[k * blocks : (k + 1) * blocks, :] * scale_x for k in range(taps)] + new_x
    seq_b = [last[k * groups : (k + 1) * groups] * scale_b for k in range(taps)] + new_b
    xs, bs, cs = small_steps(seq_x, seq_b, wx_ref, bx_ref, wb_ref, bb_ref, steps)
    mixed = against_c(tile, first, cs, perm_ref, turn_ref)
    gated, sums = gated_steps(
        mixed, scale, xs, bs, cs, dec, dts, skip_ref[...], gate, mixed_ref
    )
    for t in range(steps):
        gated_ref[t] = gated[t]
        b_ref[t] = bs[t]
    sums_ref[...] = jnp.concatenate([kept_sums_ref[...]] + sums, 0)
    spread_ref[...] = spread_x(xs, dec, dts, rows_ref)
    wide_out_ref[...] = wide_ref[slot] * scale


def state_kernel(masks, info_ref, *refs):
    pieces = len(masks)
    got_refs = refs[:pieces]
    (
        spread_ref, b_ref, wide_ref, place_ref, moved_ref, norm_ref,
        new_ref, ready_ref, rows_ref,
    ) = refs[pieces:]
    full, me = info_ref[4] > 0, info_ref[5]
    _, tile, first = piece_tiles(masks, me, got_refs, wide_ref.shape[0])

    def write(j, new):
        at = pl.ds(pl.multiple_of(first(j) * LANES, LANES), LANES)
        new_ref[:, at] = jnp.where(full, new, 0.0)

    bs = [b_ref[t] for t in range(b_ref.shape[0])]
    new_state(tile, first, wide_ref[...], spread_ref[...], bs, place_ref, write)
    gated = [moved_ref[t] for t in range(moved_ref.shape[0])]
    make_ready(gated, norm_ref, rows_ref, ready_ref)


def norm_kernel(
    info_ref, held_hbm, new_ref, kept_ref, moved_ref, mine_ref, theirs_ref, out_hbm, y_hbm, y_ref, sems
):
    del held_hbm
    copies = copy_rows(new_ref, out_hbm.at[info_ref[3]], sems, 0, COPIES)
    steps, channels = kept_ref.shape
    factor = lax.rsqrt((mine_ref[...] + theirs_ref[...]) * (1.0 / (H * P_SIZE)) + 1e-05)
    for which, ready_ref in enumerate((kept_ref, moved_ref)):
        full = info_ref[2 + 2 * which] > 0
        rows = factor[which * steps : (which + 1) * steps]
        for b in range(0, channels, LANES):
            values = jnp.where(full, ready_ref[:, b : b + LANES] * rows, 0.0)
            y_ref[info_ref[3 * which], :, b : b + LANES] = values.astype(jnp.bfloat16)
    copies.append(pltpu.make_async_copy(y_ref, y_hbm, sems.at[COPIES]))
    copies[-1].start()
    for copy in copies:
        copy.wait()


def partner_masks(owners):
    gray = [i ^ (i >> 1) for i in range(owners)]
    near, far = gray[1 : owners // 2], gray[owners // 2 :]
    order = [0]
    for i, k in enumerate(far):
        order += [k, *near[i : i + 1]]
    return tuple(order)


def on_device(
    counts,
    move_plan,
    ssm_state,
    conv_x_state,
    conv_bc_state,
    x_in,
    bc_in,
    z_in,
    dt_in,
    conv_w_x,
    conv_b_x,
    conv_w_bc,
    conv_b_bc,
    dt_bias,
    a_log,
    d_skip,
    norm_w,
):
    owners = lax.axis_size("req")
    owner = lax.axis_index("req").astype(jnp.int32)
    slots, heads, columns = ssm_state.shape
    places, steps, channels = x_in.shape
    taps = conv_x_state.shape[1]
    groups, pair = conv_bc_state.shape[2:]
    blocks = channels // LANES
    share = heads * columns // LANES // owners
    aux_rows = taps * blocks + AUX
    f32 = jnp.float32
    direct = owners <= 16 and owners & (owners - 1) == 0 and share % (QUAD * heads) == 0
    masks = partner_masks(owners) if direct else (0,)
    pieces = len(masks)
    smem = pl.BlockSpec(memory_space=pltpu.SMEM)
    vmem = pl.BlockSpec(memory_space=pltpu.VMEM)
    anywhere = pl.BlockSpec(memory_space=pl.ANY)

    def shaped(*shape, dtype=f32):
        return jax.ShapeDtypeStruct(shape, dtype)

    def call(kernel, name, in_specs, out_specs, out_shape, scratch=(), **more):
        return pl.pallas_call(
            kernel,
            in_specs=in_specs,
            out_specs=out_specs,
            out_shape=out_shape,
            scratch_shapes=scratch,
            compiler_params=pltpu.CompilerParams(vmem_limit_bytes=VMEM_LIMIT),
            name=name,
            **more,
        )

    def in_hbm(*values):
        return [pltpu.with_memory_space_constraint(v, pltpu.MemorySpace.HBM) for v in values]

    me = owner.reshape(1)
    conv_x_taps = jnp.transpose(conv_x_state, (1, 0, 2))
    piece = (share + AUX, LANES) if direct else (owners, share + AUX, LANES)
    sent = [shaped(*piece, dtype=jnp.int16)] * pieces
    payload = call(
        functools.partial(pack_kernel, masks), "pack", [smem] + [anywhere] * 5, [vmem] * pieces, sent,
        [
            pltpu.SMEM(counts.shape, jnp.int32),
            pltpu.SMEM(move_plan.shape, jnp.int32),
            pltpu.VMEM(ssm_state.shape, f32),
            pltpu.VMEM(conv_x_taps.shape, jnp.bfloat16),
            pltpu.VMEM(conv_bc_state.shape, jnp.bfloat16),
            pltpu.VMEM((max(aux_rows, pieces * AUX), LANES), f32),
            pltpu.SemaphoreType.DMA((4 + slots * heads // BLOCK,)),
        ],
    )(me, *in_hbm(counts, move_plan, ssm_state, conv_x_taps, conv_bc_state))

    def exchange(values):
        if not direct:
            return [lax.all_to_all(values[0], "req", split_axis=0, concat_axis=0, tiled=True)]
        out = list(values)
        for i, k in enumerate(masks):
            if k:
                out[i] = lax.ppermute(values[i], "req", [(o, o ^ k) for o in range(owners)])
        return out

    spread = exchange(payload)

    (
        _, me_late, cx_late, cb_late, bc_late, dt_late, bias_late, rate_late, skip_late,
        bx_late, wb_late, bb_late, norm_late,
    ) = lax.optimization_barrier(
        (
            payload[0], me, conv_x_taps, conv_bc_state, bc_in, dt_in, dt_bias, a_log, d_skip,
            conv_b_x, conv_w_bc, conv_b_bc, norm_w,
        )
    )
    rows = (places, steps * blocks, LANES)
    info, x_dense, gate, dec, dt_dense, wide, skip, wx, perm, place, kept_state, *convs = call(
        prep_kernel, "prep", [smem] + [anywhere] * 6 + [vmem] * 5, [smem] + [vmem] * 12,
        [
            shaped(INFO + owners, dtype=jnp.int32), shaped(*rows), shaped(*rows), shaped(*rows),
            shaped(*rows), shaped(places, heads, LANES), shaped(blocks, LANES),
            shaped((taps + 1) * blocks, LANES),
            shaped(QUAD * P_SIZE, 2 * steps * P_SIZE, dtype=jnp.bfloat16),
            shaped(P_SIZE, columns, dtype=jnp.bfloat16), shaped(heads, columns),
            shaped(taps, places, channels, dtype=jnp.bfloat16),
            shaped(*conv_bc_state.shape, dtype=jnp.bfloat16),
        ],
        [
            pltpu.SMEM(counts.shape, jnp.int32),
            pltpu.SMEM(move_plan.shape, jnp.int32),
            pltpu.VMEM(x_in.shape, jnp.bfloat16),
            pltpu.VMEM(z_in.shape, jnp.bfloat16),
            pltpu.VMEM(conv_w_x.shape, f32),
            pltpu.SemaphoreType.DMA((5 + COPIES,)),
        ],
    )(
        me_late, *in_hbm(counts, move_plan, x_in, z_in, conv_w_x, ssm_state), bc_late,
        dt_late, bias_late.reshape(1, -1), rate_late.reshape(1, -1), skip_late.reshape(1, -1),
    )

    picked = call(
        functools.partial(pick_kernel, masks), "pick", [smem] + [vmem] * pieces, [vmem] * pieces, sent,
        [pltpu.VMEM((owners, *piece), jnp.int16)] if direct else [],
    )(info, *spread)
    got = exchange(picked)

    _, info = lax.optimization_barrier((picked[0], info))
    common = [x_dense, bc_late, gate, dec, dt_dense, skip, wx]
    common += [bx_late.reshape(blocks, LANES), wb_late, bb_late, perm, wide]
    scratch = [pltpu.VMEM((steps * heads, LANES), f32)] * 2 + [pltpu.VMEM((LANES, LANES), f32)]
    norm_rows = norm_late.reshape(blocks, LANES)
    held, kept_ready, kept_sums = call(
        kept_kernel, "kept", [smem] + [vmem] * (5 + len(common)), [anywhere, vmem, vmem],
        [shaped(places, heads, columns), shaped(steps, channels), shaped(steps, LANES)],
        scratch
        + [
            pltpu.VMEM((taps * blocks, LANES), f32),
            pltpu.VMEM((heads, columns), f32),
            pltpu.SemaphoreType.DMA((COPIES,)),
        ],
    )(info, kept_state, cx_late, cb_late, *common, place, norm_rows)
    moved_gated, sums, spread_rows, b_steps, wide_scaled = call(
        functools.partial(moved_kernel, masks), "moved",
        [smem] + [vmem] * (pieces + 1 + len(common)), [vmem] * 5,
        [
            shaped(steps, blocks, LANES), shaped(2 * steps, LANES),
            shaped(steps * heads, 2 * LANES, dtype=jnp.bfloat16),
            shaped(steps, groups, pair), shaped(heads, LANES),
        ],
        scratch + [pltpu.VMEM((max(aux_rows, pieces * AUX), LANES), f32)],
    )(info, *got, kept_sums, *common)
    theirs = lax.ppermute(sums, "tp", [(0, 1), (1, 0)])
    new, moved_ready = call(
        functools.partial(state_kernel, masks), "state",
        [smem] + [vmem] * (pieces + 6), [vmem] * 2,
        [shaped(heads, columns), shaped(steps, channels)],
        [pltpu.VMEM((steps * blocks, LANES), f32)],
    )(
        info, *got, spread_rows, b_steps, wide_scaled, place, moved_gated, norm_rows
    )
    new_ssm, y_out = call(
        norm_kernel, "norm", [smem, anywhere] + [vmem] * 5, [anywhere, anywhere],
        [
            shaped(places, heads, columns),
            shaped(places, steps, channels, dtype=jnp.bfloat16),
        ],
        [
            pltpu.VMEM((places, steps, channels), jnp.bfloat16),
            pltpu.SemaphoreType.DMA((COPIES + 1,)),
        ],
        input_output_aliases={1: 0},
    )(info, held, new, kept_ready, moved_ready, sums, theirs)
    return (y_out, new_ssm, jnp.transpose(convs[0], (1, 0, 2)), convs[1])


def solution(mesh):
    in_specs = (
        P("parts"),
        P("parts"),
        P(("parts", "req"), "tp", None),
        P(("parts", "req"), None, "tp"),
        P(("parts", "req"), None, "tp", None),
        P(("parts", "req"), None, "tp"),
        P(("parts", "req"), None, "tp", None),
        P(("parts", "req"), None, "tp"),
        P(("parts", "req"), None, "tp"),
        P(None, "tp"),
        P("tp"),
        P(None, "tp", None),
        P("tp", None),
        P("tp"),
        P("tp"),
        P("tp"),
        P("tp"),
    )
    out_specs = (
        P(("parts", "req"), None, "tp"),
        P(("parts", "req"), "tp", None),
        P(("parts", "req"), None, "tp"),
        P(("parts", "req"), None, "tp", None),
    )
    return jax.shard_map(
        on_device, mesh=mesh, in_specs=in_specs, out_specs=out_specs, check_vma=False
    )
```
